32 devices in a mesh: section: 4 (over x, core), tp: 8 (over z, y).
Axes of the slice: x: 2, y: 2, z: 4, core: 2. Of those that a mesh axis runs over, the one named last changes fastest.
Arguments:
- gate_codes: bfloat16 [4, 96, 1280], P('section', None, 'tp'), may hold values from -128 to 127, as said below
- gate_exponents: int32 [4, 96, 40], P('section', None, 'tp'), may hold values from -8 to -6
- up_codes: bfloat16 [4, 96, 1280], P('section', None, 'tp'), may hold values from -128 to 127, as said below
- up_exponents: int32 [4, 96, 40], P('section', None, 'tp'), may hold values from -8 to -6
- down_codes: bfloat16 [4, 1280, 4096], P('section', 'tp'), may hold values from -128 to 127, as said below
- down_exponents: int32 [4, 40, 4096], P('section', 'tp'), may hold values from -14 to -12
- grad_held: bfloat16 [4, 96, 4096], P('section', 'tp'), may hold values from -6 to 6
Outputs:
- down_grad: bfloat16 [4, 1280, 4096], P('section', 'tp')
- gate_grad: bfloat16 [4, 96, 1280], P('section', None, 'tp')
- up_grad: bfloat16 [4, 96, 1280], P('section', None, 'tp')
The draws below stay inside these ranges and needn't reach their ends.
Inputs may be any that keep to these rules, and one draw needn't show every extreme that they name: `gate_codes`: every entry is a whole number, independent of the others. `up_codes`: every entry is a whole number, independent of the others. `down_codes`: every entry is a whole number, independent of the others.
All inputs are finite; a program needn't handle non-finite values.
Results may differ from the reference program's by a relative error of at most 0.005.
Values may be sent and summed in bfloat16 or wider, within the bound.
No kernel may reach another device: no remote copies, remote signals or barrier semaphores. Data moves between devices by JAX's collectives and lax.ppermute only.
A program may use at most 64 MiB of HBM per device.

```python
import jax
import jax.numpy as jnp
from jax import lax

D = 4096
FF = 1280
TOKENS = 96
SECTIONS = 4


def draw_gate_codes(key, part):
    whole = jax.random.randint(jax.random.fold_in(key, 11), (SECTIONS, TOKENS, FF), -128, 128)
    return whole.astype(jnp.float32).astype(jnp.bfloat16)


def draw_up_codes(key, part):
    whole = jax.random.randint(jax.random.fold_in(key, 23), (SECTIONS, TOKENS, FF), -128, 128)
    return whole.astype(jnp.float32).astype(jnp.bfloat16)


def draw_down_codes(key, part):
    whole = jax.random.randint(jax.random.fold_in(key, 37), (SECTIONS, FF, D), -128, 128)
    return whole.astype(jnp.float32).astype(jnp.bfloat16)


def with_ends(array, own_key, low, top_value):
    dims = array.shape
    spot = [jax.random.randint(jax.random.fold_in(own_key, axis), (), 0, dims[axis]) for axis in range(len(dims))]
    array = array.at[tuple(spot)].set(low)
    longest = dims.index(max(dims))
    spot[longest] = (spot[longest] + 1) % dims[longest]
    return array.at[tuple(spot)].set(top_value)


def level_of(key, extent, pieces, least, high):
    def one(position, blocks):
        steps = jax.random.uniform(jax.random.fold_in(jax.random.fold_in(key, 6), position), (blocks,), jnp.float32, least / len(pieces), high / len(pieces))
        return jnp.repeat(jnp.exp(steps), extent[position] // blocks).reshape((-1,) + (1,) * (len(extent) - position - 1))

    gain = one(*pieces[0])
    for cut in pieces[1:]:
        gain = gain * one(*cut)
    return gain


def bell_draw(stream_key, extent, width, reach, split=(), dtype=jnp.bfloat16):
    entries = jax.random.normal(stream_key, extent, jnp.float32) * width
    if len(split) > 0:
        entries = level_of(stream_key, extent, split, -0.22, 0.18) * entries
    return jnp.clip(entries, min=-reach, max=reach).astype(dtype)


def setup_inputs(seed: int = 0) -> dict:
    arg_keys = jax.random.split(jax.random.key(seed), 8)
    return {
        "gate_codes": draw_gate_codes(jax.random.fold_in(arg_keys[7], 71), 0),
        "gate_exponents": with_ends(jax.random.randint(arg_keys[1], (SECTIONS, TOKENS, FF // 32), -8, -5), jax.random.fold_in(arg_keys[1], 1), -8, (-5) - 1).astype(jnp.int32),
        "up_codes": draw_up_codes(jax.random.fold_in(arg_keys[7], 71), 0),
        "up_exponents": with_ends(jax.random.randint(arg_keys[3], (SECTIONS, TOKENS, FF // 32), -8, -5), jax.random.fold_in(arg_keys[3], 1), -8, (-5) - 1).astype(jnp.int32),
        "down_codes": draw_down_codes(jax.random.fold_in(arg_keys[7], 71), 0),
        "down_exponents": with_ends(jax.random.randint(arg_keys[5], (SECTIONS, FF // 32, D), -14, -11), jax.random.fold_in(arg_keys[5], 1), -14, (-11) - 1).astype(jnp.int32),
        "grad_held": bell_draw(arg_keys[6], (SECTIONS, TOKENS, D), 1.0, 6.0, ((0, 4), (1, 8))),
    }


def dequantize(codes, exponents, target_axis):
    scales = jnp.exp2(jnp.repeat(exponents, 32, axis=target_axis).astype(jnp.float32))
    return (codes.astype(jnp.float32) * scales).astype(jnp.bfloat16)


def one_section(operands):
    gate_packed, gate_scale, up_packed, up_scale, down_packed, down_scale, arriving = operands
    gate_value = dequantize(gate_packed, gate_scale, 1)
    up_value = dequantize(up_packed, up_scale, 1)
    weight_rows = dequantize(down_packed, down_scale, 0)
    gate_wide = gate_value.astype(jnp.float32)
    up_wide = up_value.astype(jnp.float32)
    sigmoid_gate = jax.nn.sigmoid(gate_wide)
    silu_gate = gate_wide * sigmoid_gate
    hidden = (silu_gate * up_wide).astype(jnp.bfloat16)
    weight_sum = lax.dot_general(hidden, arriving, (((0,), (0,)), ((), ())), preferred_element_type=jnp.float32)
    hidden_slope = lax.dot_general(arriving, weight_rows, (((1,), (1,)), ((), ())), preferred_element_type=jnp.float32)
    gate_grad = (hidden_slope * up_wide * sigmoid_gate * (1.0 + gate_wide * (1.0 - sigmoid_gate))).astype(jnp.bfloat16)
    up_grad = (hidden_slope * silu_gate).astype(jnp.bfloat16)
    return weight_sum.astype(jnp.bfloat16), gate_grad, up_grad


def reference(gate_codes, gate_exponents, up_codes, up_exponents, down_codes, down_exponents, grad_held):
    incoming = jnp.roll(grad_held, -1, axis=0)
    results = lax.map(one_section, (gate_codes, gate_exponents, up_codes, up_exponents, down_codes, down_exponents, incoming))
    return (results[0], results[1], results[2])
```

```python
import jax
import jax.numpy as jnp
from jax import lax
from jax.sharding import PartitionSpec as P

TILE = 16


def dequantize(codes, exponents, target_axis):
    per = codes.shape[target_axis] // exponents.shape[target_axis]
    scales = jnp.exp2(jnp.repeat(exponents, per, axis=target_axis).astype(jnp.float32))
    return (codes.astype(jnp.float32) * scales).astype(jnp.bfloat16)


def send(array, flip, hop):
    sections, count = lax.axis_size("section"), lax.axis_size("tp")
    if hop == 0:
        return lax.ppermute(array, "tp", [(t, t ^ flip) for t in range(count)])
    pairs = [
        (s * count + t, ((s - hop) % sections) * count + (t ^ flip))
        for s in range(sections)
        for t in range(count)
    ]
    return lax.ppermute(array, ("section", "tp"), pairs)


def packed(rows):
    count, width = rows.shape
    free = TILE - count
    keep = width * count // TILE
    parts = count // free
    tail = rows[:, keep:].reshape(parts, free, width - keep)
    low = tail.transpose(1, 0, 2).reshape(free, keep)
    return jnp.concatenate([rows[:, :keep], low], axis=0)


def unpacked(slots, count, width):
    free = TILE - count
    keep = width * count // TILE
    parts = count // free
    number = slots.shape[0]
    low = slots[:, count:, :].reshape(number, free, parts, width - keep)
    tail = low.transpose(0, 2, 1, 3).reshape(number, count, width - keep)
    return jnp.concatenate([slots[:, :count, :], tail], axis=2)


def gathered(rows):
    count, width = rows.shape
    n = lax.axis_size("tp")
    p = packed(rows)
    got = {}
    for flip in sorted([f for f in range(n) if f % 2 == 0 and f > 0], reverse=True):
        got[flip] = send(p, flip, 1)
    got[0] = send(p, 0, 1)
    got[1] = send(p, 1, 1)
    for flip in range(2, n, 2):
        got[flip + 1] = send(got[flip], 1, 0)
    return unpacked(jnp.stack([got[j] for j in range(n)]), count, width)


def body(gate_codes, gate_exponents, up_codes, up_exponents, down_codes, down_exponents, grad_held):
    n = lax.axis_size("tp")
    rows, width = grad_held.shape[1:]
    gate_value = dequantize(gate_codes[0], gate_exponents[0], 1)
    up_value = dequantize(up_codes[0], up_exponents[0], 1)
    weight_rows = dequantize(down_codes[0], down_exponents[0], 0)
    if n & (n - 1) == 0 and n <= TILE:
        order = jnp.bitwise_xor(lax.axis_index("tp"), jnp.arange(n))
        every_row = gathered(grad_held[0]).reshape(n * rows, width)
    else:
        order = jnp.arange(n)
        count = lax.axis_size("section")
        received = lax.ppermute(grad_held[0], "section", [(i, (i - 1) % count) for i in range(count)])
        every_row = lax.all_gather(received, "tp", axis=0, tiled=True)

    def reordered(array):
        return array.reshape(n, rows, -1)[order].reshape(array.shape)

    gate_wide = reordered(gate_value).astype(jnp.float32)
    up_wide = reordered(up_value).astype(jnp.float32)
    sigmoid_gate = jax.nn.sigmoid(gate_wide)
    silu_gate = gate_wide * sigmoid_gate
    hidden = (silu_gate * up_wide).astype(jnp.bfloat16)
    down_grad = lax.dot_general(
        hidden, every_row, (((0,), (0,)), ((), ())), preferred_element_type=jnp.float32
    )
    slope = lax.dot_general(
        every_row, weight_rows, (((1,), (1,)), ((), ())), preferred_element_type=jnp.float32
    )
    gate_grad = (slope * up_wide * sigmoid_gate * (1.0 + gate_wide * (1.0 - sigmoid_gate))).astype(jnp.bfloat16)
    up_grad = (slope * silu_gate).astype(jnp.bfloat16)
    return (down_grad.astype(jnp.bfloat16)[None], reordered(gate_grad)[None], reordered(up_grad)[None])


def solution(mesh):
    placed = (
        P("section", None, "tp"),
        P("section", None, "tp"),
        P("section", None, "tp"),
        P("section", None, "tp"),
        P("section", "tp", None),
        P("section", "tp", None),
        P("section", "tp", None),
    )
    return jax.shard_map(
        body,
        mesh=mesh,
        in_specs=placed,
        out_specs=(P("section", "tp", None), P("section", None, "tp"), P("section", None, "tp")),
        check_vma=False,
    )
```

```python
import functools

import jax
import jax.numpy as jnp
from jax import lax
from jax.experimental import pallas as pl
from jax.experimental.pallas import tpu as pltpu
from jax.sharding import PartitionSpec as P

TILE = 16
WHOLE = pl.BlockSpec(memory_space=pltpu.VMEM)
LEFT = pl.BlockSpec(memory_space=pltpu.HBM)
PARAMS = pltpu.CompilerParams(vmem_limit_bytes=24 * 1024 * 1024)


def send(array, flip, hop):
    sections, count = lax.axis_size("section"), lax.axis_size("tp")
    if hop == 0:
        return lax.ppermute(array, "tp", [(t, t ^ flip) for t in range(count)])
    pairs = [
        (s * count + t, ((s - hop) % sections) * count + (t ^ flip))
        for s in range(sections)
        for t in range(count)
    ]
    return lax.ppermute(array, ("section", "tp"), pairs)


def fetched(refs, held_refs, sems):
    copies = [pltpu.make_async_copy(ref, held, sems.at[i]) for i, (ref, held) in enumerate(zip(refs, held_refs))]
    for copy in copies:
        copy.start()
    return copies


def pack_kernel(held_ref, packed_ref, rows_ref, sems):
    for copy in fetched([held_ref], [rows_ref], sems):
        copy.wait()
    count, width = rows_ref.shape
    free = TILE - count
    keep = width * count // TILE
    rows = rows_ref[...]
    parts = [rows[at : at + free, keep:] for at in range(0, count, free)]
    packed_ref[...] = jnp.concatenate([rows[:, :keep], jnp.concatenate(parts, axis=1)], axis=0)


def pack(rows):
    count, width = rows.shape
    return pl.pallas_call(
        pack_kernel,
        out_shape=pltpu.VMEM((TILE, width * count // TILE), jnp.bfloat16),
        in_specs=[LEFT],
        out_specs=WHOLE,
        scratch_shapes=[pltpu.VMEM(rows.shape, rows.dtype), pltpu.SemaphoreType.DMA((1,))],
        compiler_params=PARAMS,
    )(pltpu.with_memory_space_constraint(rows, pltpu.HBM))


def spread(tokens, slots, count, position):
    shape = (tokens, slots * TILE)
    lane = lax.broadcasted_iota(jnp.int32, shape, 1)
    row = lane & (TILE - 1)
    token = ((lane >> (TILE.bit_length() - 1)) ^ position) * count + row
    hit = (lax.broadcasted_iota(jnp.int32, shape, 0) == token) & (row < count)
    return jnp.where(hit, 1.0, 0.0).astype(jnp.bfloat16)


def decoded(codes_ref, exponents_ref):
    blocks = exponents_ref.shape[0]
    per = codes_ref.shape[0] // blocks
    parts = []
    for b in range(blocks):
        scale = jnp.exp2(exponents_ref[b].astype(jnp.float32))
        codes = codes_ref[pl.ds(b * per, per), :].astype(jnp.float32)
        parts.append((codes * scale).astype(jnp.bfloat16))
    return jnp.concatenate(parts, axis=0)


def prepare_kernel(
    slots, count, *refs
):
    weight_ref, hidden_ref, gate_factor_ref, up_factor_ref = refs[6:10]
    gate_ref, gate_exp_ref, up_ref, up_exp_ref, down_ref, down_exp_ref = refs[10:16]
    copies = fetched(refs[:6], refs[10:16], refs[16])
    for copy in copies[:4]:
        copy.wait()
    where = spread(gate_ref.shape[1], slots, count, lax.axis_index("tp"))
    gate = jnp.dot(decoded(gate_ref, gate_exp_ref), where, preferred_element_type=jnp.float32)
    up = jnp.dot(decoded(up_ref, up_exp_ref), where, preferred_element_type=jnp.float32)
    sigmoid = jax.nn.sigmoid(gate)
    silu = gate * sigmoid
    hidden_ref[...] = (silu * up).astype(jnp.bfloat16)
    gate_factor_ref[...] = up * sigmoid * (1.0 + gate * (1.0 - sigmoid))
    up_factor_ref[...] = silu
    for copy in copies[4:]:
        copy.wait()
    blocks = down_exp_ref.shape[0]
    per = down_ref.shape[0] // blocks
    for b in range(blocks):
        scale = jnp.exp2(down_exp_ref[b].astype(jnp.float32))
        codes = down_ref[pl.ds(b * per, per), :].astype(jnp.float32)
        weight_ref[pl.ds(b * per, per), :] = (codes * scale).astype(jnp.bfloat16)


def prepare(slots, count, *operands):
    units, width = operands[4].shape
    lanes = slots * TILE
    return pl.pallas_call(
        functools.partial(prepare_kernel, slots, count),
        out_shape=(
            pltpu.VMEM((units, width), jnp.bfloat16),
            pltpu.VMEM((units, lanes), jnp.bfloat16),
            pltpu.VMEM((units, lanes), jnp.float32),
            pltpu.VMEM((units, lanes), jnp.float32),
        ),
        in_specs=[LEFT] * 6,
        out_specs=[WHOLE] * 4,
        scratch_shapes=[pltpu.VMEM(operand.shape, operand.dtype) for operand in operands]
        + [pltpu.SemaphoreType.DMA((len(operands),))],
        compiler_params=PARAMS,
        cost_estimate=pl.CostEstimate(flops=4 * units * width, bytes_accessed=4 * units * width, transcendentals=0),
    )(*[pltpu.with_memory_space_constraint(operand, pltpu.HBM) for operand in operands])


def products_kernel(slots, count, chunk, *refs):
    slot_refs = refs[:slots]
    weight_ref, hidden_ref, gate_factor_ref, up_factor_ref = refs[slots : slots + 4]
    down_ref, gate_grad_ref, up_grad_ref, tile_ref, sems = refs[slots + 4 :]
    units, width = weight_ref.shape
    keep = slot_refs[0].shape[1]
    free = TILE - count
    rest = width - keep
    hidden = hidden_ref[...]
    slope = jnp.zeros((units, slots * TILE), jnp.float32)
    copies = []
    for at in range(0, width, chunk):
        parts = []
        for ref in slot_refs:
            if at < keep:
                parts.append(ref[:, at : at + chunk])
            else:
                low = ref[...][count:TILE, :]
                for j in range(count // free):
                    from_ = j * rest + at - keep
                    parts.append(low[:, from_ : from_ + chunk])
                parts.append(jnp.zeros((free, chunk), jnp.bfloat16))
        incoming = jnp.concatenate(parts, axis=0)
        down = jnp.dot(hidden, incoming, preferred_element_type=jnp.float32)
        tile_ref[:, at : at + chunk] = down.astype(jnp.bfloat16)
        copy = pltpu.make_async_copy(
            tile_ref.at[:, pl.ds(at, chunk)], down_ref.at[:, pl.ds(at, chunk)], sems.at[at // chunk]
        )
        copy.start()
        copies.append(copy)
        slope += lax.dot_general(
            weight_ref[:, at : at + chunk], incoming, (((1,), (1,)), ((), ())), preferred_element_type=jnp.float32
        )
    where = spread(gate_grad_ref.shape[1], slots, count, lax.axis_index("tp"))
    for factor_ref, grad_ref in ((gate_factor_ref, gate_grad_ref), (up_factor_ref, up_grad_ref)):
        grad = (slope * factor_ref[...]).astype(jnp.bfloat16)
        placed = lax.dot_general(grad, where, (((1,), (1,)), ((), ())), preferred_element_type=jnp.float32)
        grad_ref[...] = placed.astype(jnp.bfloat16)
    for copy in copies:
        copy.wait()


def products(got, count, weight, hidden, gate_factor, up_factor):
    slots = len(got)
    units, width = weight.shape
    tokens = slots * count
    chunk = width // 8
    return pl.pallas_call(
        functools.partial(products_kernel, slots, count, chunk),
        out_shape=(
            jax.ShapeDtypeStruct((units, width), jnp.bfloat16),
            jax.ShapeDtypeStruct((units, tokens), jnp.bfloat16),
            jax.ShapeDtypeStruct((units, tokens), jnp.bfloat16),
        ),
        in_specs=[WHOLE] * (slots + 4),
        out_specs=[LEFT, WHOLE, WHOLE],
        scratch_shapes=[
            pltpu.VMEM((units, width), jnp.bfloat16),
            pltpu.SemaphoreType.DMA((width // chunk,)),
        ],
        compiler_params=PARAMS,
        cost_estimate=pl.CostEstimate(
            flops=4 * units * width * slots * TILE, bytes_accessed=4 * units * width, transcendentals=0
        ),
    )(*got, weight, hidden, gate_factor, up_factor)


def fanned(gate_codes, gate_exponents, up_codes, up_exponents, down_codes, down_exponents, grad_held):
    n = lax.axis_size("tp")
    count = grad_held.shape[1]
    p = pack(grad_held[0])
    got = {}
    for flip in range(n - 2, -1, -2):
        got[flip] = send(p, flip, 1)
    got[1] = send(p, 1, 1)
    ready = prepare(
        n,
        count,
        gate_codes[0].T,
        gate_exponents.transpose(2, 0, 1),
        up_codes[0].T,
        up_exponents.transpose(2, 0, 1),
        down_codes[0],
        down_exponents.transpose(1, 0, 2),
    )
    for flip in range(n - 2, 0, -2):
        got[flip], _ = lax.optimization_barrier((got[flip], ready[1]))
        got[flip + 1] = send(got[flip], 1, 0)
    down_grad, gate_grad, up_grad = products([got[j] for j in range(n)], count, *ready)
    return down_grad[None], gate_grad.T[None], up_grad.T[None]


def dequantize(codes, exponents, target_axis):
    per = codes.shape[target_axis] // exponents.shape[target_axis]
    scales = jnp.exp2(jnp.repeat(exponents, per, axis=target_axis).astype(jnp.float32))
    return (codes.astype(jnp.float32) * scales).astype(jnp.bfloat16)


def ringed(gate_codes, gate_exponents, up_codes, up_exponents, down_codes, down_exponents, grad_held):
    gate = dequantize(gate_codes[0], gate_exponents[0], 1).astype(jnp.float32)
    up = dequantize(up_codes[0], up_exponents[0], 1).astype(jnp.float32)
    weight = dequantize(down_codes[0], down_exponents[0], 0)
    count = lax.axis_size("section")
    received = lax.ppermute(grad_held[0], "section", [(i, (i - 1) % count) for i in range(count)])
    incoming = lax.all_gather(received, "tp", axis=0, tiled=True)
    sigmoid = jax.nn.sigmoid(gate)
    silu = gate * sigmoid
    hidden = (silu * up).astype(jnp.bfloat16)
    down_grad = lax.dot_general(hidden, incoming, (((0,), (0,)), ((), ())), preferred_element_type=jnp.float32)
    slope = lax.dot_general(incoming, weight, (((1,), (1,)), ((), ())), preferred_element_type=jnp.float32)
    gate_grad = (slope * up * sigmoid * (1.0 + gate * (1.0 - sigmoid))).astype(jnp.bfloat16)
    up_grad = (slope * silu).astype(jnp.bfloat16)
    return down_grad.astype(jnp.bfloat16)[None], gate_grad[None], up_grad[None]


def body(*operands):
    n = lax.axis_size("tp")
    count, width = operands[-1].shape[1:]
    free = TILE - count
    small = n & (n - 1) == 0 and 2 <= n <= TILE
    fits = 0 < free < TILE and count % free == 0 and width * free % (TILE * 8 * 128) == 0
    return fanned(*operands) if small and fits else ringed(*operands)


def solution(mesh):
    wide, tall = P("section", None, "tp"), P("section", "tp", None)
    return jax.shard_map(
        body,
        mesh=mesh,
        in_specs=(wide, wide, wide, wide, tall, tall, tall),
        out_specs=(tall, wide, wide),
        check_vma=False,
    )
```

```python
import functools

import jax
import jax.numpy as jnp
from jax import lax
from jax.experimental import pallas as pl
from jax.experimental.pallas import tpu as pltpu
from jax.sharding import PartitionSpec as P

TILE = 16
WHOLE = pl.BlockSpec(memory_space=pltpu.VMEM)
LEFT = pl.BlockSpec(memory_space=pltpu.HBM)
COST = pl.CostEstimate(flops=0, bytes_accessed=16 * 1024 * 1024, transcendentals=0)
PARAMS = pltpu.CompilerParams(vmem_limit_bytes=24 * 1024 * 1024)


def send(array, flip, hop):
    sections, count = lax.axis_size("section"), lax.axis_size("tp")
    if hop == 0:
        return lax.ppermute(array, "tp", [(t, t ^ flip) for t in range(count)])
    pairs = [
        (s * count + t, ((s - hop) % sections) * count + (t ^ flip))
        for s in range(sections)
        for t in range(count)
    ]
    return lax.ppermute(array, ("section", "tp"), pairs)


def fetched(refs, held_refs, sems):
    copies = [pltpu.make_async_copy(ref, held, sems.at[i]) for i, (ref, held) in enumerate(zip(refs, held_refs))]
    for copy in copies:
        copy.start()
    return copies


def pack_kernel(held_ref, packed_ref, rows_ref, sems):
    for copy in fetched([held_ref], [rows_ref], sems):
        copy.wait()
    count, width = rows_ref.shape
    free = TILE - count
    keep = width * count // TILE
    rows = rows_ref[...]
    parts = [rows[at : at + free, keep:] for at in range(0, count, free)]
    packed_ref[...] = jnp.concatenate([rows[:, :keep], jnp.concatenate(parts, axis=1)], axis=0)


def pack(rows):
    count, width = rows.shape
    return pl.pallas_call(
        pack_kernel,
        out_shape=pltpu.VMEM((TILE, width * count // TILE), jnp.bfloat16),
        in_specs=[LEFT],
        out_specs=WHOLE,
        scratch_shapes=[pltpu.VMEM(rows.shape, rows.dtype), pltpu.SemaphoreType.DMA((1,))],
        compiler_params=PARAMS,
    )(pltpu.with_memory_space_constraint(rows, pltpu.HBM))


def spread(tokens, slots, count):
    shape = (tokens, len(slots) * TILE)
    lane = lax.broadcasted_iota(jnp.int32, shape, 1)
    row = lane & (TILE - 1)
    slot = (lane >> (TILE.bit_length() - 1)) + slots[0]
    token = (slot ^ lax.axis_index("tp")) * count + row
    hit = (lax.broadcasted_iota(jnp.int32, shape, 0) == token) & (row < count)
    return jnp.where(hit, 1.0, 0.0).astype(jnp.bfloat16)


def decoded(codes_ref, exponents_ref):
    blocks = exponents_ref.shape[0]
    per = codes_ref.shape[0] // blocks
    parts = []
    for b in range(blocks):
        scale = jnp.exp2(exponents_ref[b].astype(jnp.float32))
        codes = codes_ref[pl.ds(b * per, per), :].astype(jnp.float32)
        parts.append((codes * scale).astype(jnp.bfloat16))
    return jnp.concatenate(parts, axis=0)


def prepare_kernel(groups, count, *refs):
    gate_ref, gate_exp_ref, up_ref, up_exp_ref, down_ref, down_exp_ref = held = refs[-7:-1]
    copies = fetched(refs[:6], held, refs[-1])
    weight_ref, hidden_ref = refs[6:8]
    factor_refs = refs[8:-7]
    for copy in copies[:4]:
        copy.wait()
    where = spread(gate_ref.shape[1], range(sum(map(len, groups))), count)
    gate = jnp.dot(decoded(gate_ref, gate_exp_ref), where, preferred_element_type=jnp.float32)
    up = jnp.dot(decoded(up_ref, up_exp_ref), where, preferred_element_type=jnp.float32)
    sigmoid = jax.nn.sigmoid(gate)
    silu = gate * sigmoid
    hidden_ref[...] = (silu * up).astype(jnp.bfloat16)
    gate_factor = up * sigmoid * (1.0 + gate * (1.0 - sigmoid))
    for i, group in enumerate(groups):
        lanes = slice(group[0] * TILE, (group[-1] + 1) * TILE)
        factor_refs[2 * i][...] = gate_factor[:, lanes]
        factor_refs[2 * i + 1][...] = silu[:, lanes]
    for copy in copies[4:]:
        copy.wait()
    blocks = down_exp_ref.shape[0]
    per = down_ref.shape[0] // blocks
    for b in range(blocks):
        scale = jnp.exp2(down_exp_ref[b].astype(jnp.float32))
        codes = down_ref[pl.ds(b * per, per), :].astype(jnp.float32)
        weight_ref[pl.ds(b * per, per), :] = (codes * scale).astype(jnp.bfloat16)


def prepare(groups, count, *operands):
    units, width = operands[4].shape
    lanes = sum(map(len, groups)) * TILE
    factors = [pltpu.VMEM((units, len(group) * TILE), jnp.float32) for group in groups for _ in range(2)]
    weight, hidden, *factors = pl.pallas_call(
        functools.partial(prepare_kernel, groups, count),
        out_shape=(
            pltpu.VMEM((units, width), jnp.bfloat16),
            pltpu.VMEM((units, lanes), jnp.bfloat16),
            *factors,
        ),
        in_specs=[LEFT] * 6,
        out_specs=[WHOLE] * (2 + len(factors)),
        scratch_shapes=[pltpu.VMEM(operand.shape, operand.dtype) for operand in operands]
        + [pltpu.SemaphoreType.DMA((len(operands),))],
        compiler_params=PARAMS,
        cost_estimate=COST,
    )(*[pltpu.with_memory_space_constraint(operand, pltpu.HBM) for operand in operands])
    return weight, hidden, [factors[2 * i : 2 * i + 2] for i in range(len(groups))]


def restored(slot_ref, count, width):
    keep = slot_ref.shape[1]
    free = TILE - count
    slot = slot_ref[...]
    low = slot[count:, :]
    parts = [low[:, at : at + width - keep] for at in range(0, keep, width - keep)]
    parts.append(jnp.zeros((free, width - keep), slot.dtype))
    return slot, jnp.concatenate(parts, axis=0)


def grads(group, count, slope, factor_refs, before_refs, grad_refs):
    where = spread(grad_refs[0].shape[1], group, count)
    for factor_ref, before_ref, grad_ref in zip(factor_refs, before_refs, grad_refs):
        grad = (slope * factor_ref[...]).astype(jnp.bfloat16)
        placed = lax.dot_general(grad, where, (((1,), (1,)), ((), ())), preferred_element_type=jnp.float32)
        if before_ref is not None:
            placed += before_ref[...].astype(jnp.float32)
        grad_ref[...] = placed.astype(jnp.bfloat16)


def stage_kernel(group, count, first, *refs):
    slot_refs, refs = refs[: len(group)], refs[len(group) :]
    weight_ref, factor_refs, refs = refs[0], refs[1:3], refs[3:]
    before_refs, refs = ((None, None), refs) if first else (refs[:2], refs[2:])
    incoming_ref, *grad_refs = refs
    width = weight_ref.shape[1]
    keep = slot_refs[0].shape[1]
    for i, ref in enumerate(slot_refs):
        slot, rest = restored(ref, count, width)
        incoming_ref[i * TILE : (i + 1) * TILE, :keep] = slot
        incoming_ref[i * TILE : (i + 1) * TILE, keep:] = rest
    slope = lax.dot_general(
        weight_ref[...], incoming_ref[...], (((1,), (1,)), ((), ())), preferred_element_type=jnp.float32
    )
    grads(group, count, slope, factor_refs, before_refs, grad_refs)


def stage(group, count, tokens, slots, weight, factors, before):
    units, width = weight.shape
    operands = (*slots, weight, *factors, *before)
    return pl.pallas_call(
        functools.partial(stage_kernel, group, count, len(before) == 0),
        out_shape=(
            pltpu.VMEM((len(group) * TILE, width), jnp.bfloat16),
            pltpu.VMEM((units, tokens), jnp.bfloat16),
            pltpu.VMEM((units, tokens), jnp.bfloat16),
        ),
        in_specs=[WHOLE] * len(operands),
        out_specs=[WHOLE] * 3,
        compiler_params=PARAMS,
        cost_estimate=COST,
    )(*operands)


def last_kernel(group, count, chunk, *refs):
    slot_ref, *earlier_refs = refs[: -11]
    weight_ref, hidden_ref = refs[-11:-9]
    factor_refs, before_refs = refs[-9:-7], refs[-7:-5]
    down_ref, *grad_refs, tile_ref, sems = refs[-5:]
    width = weight_ref.shape[1]
    keep = slot_ref.shape[1]
    slot, rest = restored(slot_ref, count, width)
    newest = jnp.concatenate([slot, rest], axis=1)
    hidden = hidden_ref[...]
    copies = []
    for at in range(0, width, chunk):
        parts = [ref[:, at : at + chunk] for ref in earlier_refs] + [newest[:, at : at + chunk]]
        incoming = jnp.concatenate(parts, axis=0)
        down = jnp.dot(hidden, incoming, preferred_element_type=jnp.float32)
        tile_ref[:, at : at + chunk] = down.astype(jnp.bfloat16)
        copy = pltpu.make_async_copy(
            tile_ref.at[:, pl.ds(at, chunk)], down_ref.at[:, pl.ds(at, chunk)], sems.at[at // chunk]
        )
        copy.start()
        copies.append(copy)
    slope = lax.dot_general(
        weight_ref[...], newest, (((1,), (1,)), ((), ())), preferred_element_type=jnp.float32
    )
    grads(group, count, slope, factor_refs, before_refs, grad_refs)
    for copy in copies:
        copy.wait()


def last(group, count, slot, earlier, weight, hidden, factors, before):
    units, width = weight.shape
    tokens = before[0].shape[1]
    chunk = width // 8
    operands = (slot, *earlier, weight, hidden, *factors, *before)
    return pl.pallas_call(
        functools.partial(last_kernel, group, count, chunk),
        out_shape=(
            jax.ShapeDtypeStruct((units, width), jnp.bfloat16),
            jax.ShapeDtypeStruct((units, tokens), jnp.bfloat16),
            jax.ShapeDtypeStruct((units, tokens), jnp.bfloat16),
        ),
        in_specs=[WHOLE] * len(operands),
        out_specs=[LEFT, WHOLE, WHOLE],
        scratch_shapes=[
            pltpu.VMEM((units, width), jnp.bfloat16),
            pltpu.SemaphoreType.DMA((width // chunk,)),
        ],
        compiler_params=PARAMS,
        cost_estimate=COST,
    )(*operands)


def fanned(gate_codes, gate_exponents, up_codes, up_exponents, down_codes, down_exponents, grad_held):
    n = lax.axis_size("tp")
    count = grad_held.shape[1]
    p = pack(grad_held[0])
    got = {}
    for flip in [f for f in (2, 4, 8) if f < n] + [1, 0]:
        got[flip] = send(p, flip, 1)
    groups = [list(range(n // 2)), list(range(n // 2, n - 1)), [n - 1]]
    got[2], got[1], gate_codes = lax.optimization_barrier((got[2], got[1], gate_codes))
    weight, hidden, factors = prepare(
        groups,
        count,
        gate_codes[0].T,
        gate_exponents.transpose(2, 0, 1),
        up_codes[0].T,
        up_exponents.transpose(2, 0, 1),
        down_codes[0],
        down_exponents.transpose(1, 0, 2),
    )
    got[3] = send(got[2], 1, 0)
    got[n // 2], *_ = lax.optimization_barrier((got[n // 2], hidden, got[3]))
    for flip in range(5, n):
        low = flip & -flip
        if flip != low:
            got[flip] = send(got[flip - low], low, 0)
    earlier, before = [], []
    for group, pair in zip(groups[:2], factors):
        incoming, *before = stage(group, count, n * count, [got[j] for j in group], weight, pair, before)
        earlier.append(incoming)
    down_grad, gate_grad, up_grad = last(groups[2], count, got[n - 1], earlier, weight, hidden, factors[2], before)
    return down_grad[None], gate_grad.T[None], up_grad.T[None]


def dequantize(codes, exponents, target_axis):
    per = codes.shape[target_axis] // exponents.shape[target_axis]
    scales = jnp.exp2(jnp.repeat(exponents, per, axis=target_axis).astype(jnp.float32))
    return (codes.astype(jnp.float32) * scales).astype(jnp.bfloat16)


def ringed(gate_codes, gate_exponents, up_codes, up_exponents, down_codes, down_exponents, grad_held):
    gate = dequantize(gate_codes[0], gate_exponents[0], 1).astype(jnp.float32)
    up = dequantize(up_codes[0], up_exponents[0], 1).astype(jnp.float32)
    weight = dequantize(down_codes[0], down_exponents[0], 0)
    count = lax.axis_size("section")
    received = lax.ppermute(grad_held[0], "section", [(i, (i - 1) % count) for i in range(count)])
    incoming = lax.all_gather(received, "tp", axis=0, tiled=True)
    sigmoid = jax.nn.sigmoid(gate)
    silu = gate * sigmoid
    hidden = (silu * up).astype(jnp.bfloat16)
    down_grad = lax.dot_general(hidden, incoming, (((0,), (0,)), ((), ())), preferred_element_type=jnp.float32)
    slope = lax.dot_general(incoming, weight, (((1,), (1,)), ((), ())), preferred_element_type=jnp.float32)
    gate_grad = (slope * up * sigmoid * (1.0 + gate * (1.0 - sigmoid))).astype(jnp.bfloat16)
    up_grad = (slope * silu).astype(jnp.bfloat16)
    return down_grad.astype(jnp.bfloat16)[None], gate_grad[None], up_grad[None]


def body(*operands):
    n = lax.axis_size("tp")
    count, width = operands[-1].shape[1:]
    free = TILE - count
    small = n & (n - 1) == 0 and 4 <= n <= TILE
    fits = 0 < free < TILE and count % free == 0 and width * free % (TILE * 8 * 128) == 0
    return fanned(*operands) if small and fits else ringed(*operands)


def solution(mesh):
    wide, tall = P("section", None, "tp"), P("section", "tp", None)
    return jax.shard_map(
        body,
        mesh=mesh,
        in_specs=(wide, wide, wide, wide, tall, tall, tall),
        out_specs=(tall, wide, wide),
        check_vma=False,
    )
```

```python
import functools

import jax
import jax.numpy as jnp
from jax import lax
from jax.experimental import pallas as pl
from jax.experimental.pallas import tpu as pltpu
from jax.sharding import PartitionSpec as P

TILE = 16
WHOLE = pl.BlockSpec(memory_space=pltpu.VMEM)
LEFT = pl.BlockSpec(memory_space=pltpu.HBM)
COST = pl.CostEstimate(flops=0, bytes_accessed=16 * 1024 * 1024, transcendentals=0)
PARAMS = pltpu.CompilerParams(vmem_limit_bytes=24 * 1024 * 1024)


def send(array, flip, hop):
    sections, count = lax.axis_size("section"), lax.axis_size("tp")
    if hop == 0:
        return lax.ppermute(array, "tp", [(t, t ^ flip) for t in range(count)])
    pairs = [
        (s * count + t, ((s - hop) % sections) * count + (t ^ flip))
        for s in range(sections)
        for t in range(count)
    ]
    return lax.ppermute(array, ("section", "tp"), pairs)


def fetched(refs, held_refs, sems):
    copies = [pltpu.make_async_copy(ref, held, sems.at[i]) for i, (ref, held) in enumerate(zip(refs, held_refs))]
    for copy in copies:
        copy.start()
    return copies


def pack_kernel(held_ref, packed_ref, rows_ref, sems):
    for copy in fetched([held_ref], [rows_ref], sems):
        copy.wait()
    count, width = rows_ref.shape
    free = TILE - count
    keep = width * count // TILE
    rows = rows_ref[...]
    parts = [rows[at : at + free, keep:] for at in range(0, count, free)]
    packed_ref[...] = jnp.concatenate([rows[:, :keep], jnp.concatenate(parts, axis=1)], axis=0)


def pack(rows):
    count, width = rows.shape
    return pl.pallas_call(
        pack_kernel,
        out_shape=pltpu.VMEM((TILE, width * count // TILE), jnp.bfloat16),
        in_specs=[LEFT],
        out_specs=WHOLE,
        scratch_shapes=[pltpu.VMEM(rows.shape, rows.dtype), pltpu.SemaphoreType.DMA((1,))],
        compiler_params=PARAMS,
    )(pltpu.with_memory_space_constraint(rows, pltpu.HBM))


def spread(tokens, slots, count):
    shape = (tokens, len(slots) * TILE)
    lane = lax.broadcasted_iota(jnp.int32, shape, 1)
    row = lane & (TILE - 1)
    slot = (lane >> (TILE.bit_length() - 1)) + slots[0]
    token = (slot ^ lax.axis_index("tp")) * count + row
    hit = (lax.broadcasted_iota(jnp.int32, shape, 0) == token) & (row < count)
    return jnp.where(hit, 1.0, 0.0).astype(jnp.bfloat16)


def decoded(codes_ref, exponents_ref):
    blocks = exponents_ref.shape[0]
    per = codes_ref.shape[0] // blocks
    parts = []
    for b in range(blocks):
        scale = jnp.exp2(exponents_ref[b].astype(jnp.float32))
        codes = codes_ref[pl.ds(b * per, per), :].astype(jnp.float32)
        parts.append((codes * scale).astype(jnp.bfloat16))
    return jnp.concatenate(parts, axis=0)


def prepare_kernel(groups, count, *refs):
    gate_ref, gate_exp_ref, up_ref, up_exp_ref, down_ref, down_exp_ref = held = refs[-7:-1]
    copies = fetched(refs[:6], held, refs[-1])
    weight_ref, hidden_ref = refs[6:8]
    factor_refs = refs[8:-7]
    for copy in copies[:4]:
        copy.wait()
    where = spread(gate_ref.shape[1], range(sum(map(len, groups))), count)
    gate = jnp.dot(decoded(gate_ref, gate_exp_ref), where, preferred_element_type=jnp.float32)
    up = jnp.dot(decoded(up_ref, up_exp_ref), where, preferred_element_type=jnp.float32)
    sigmoid = jax.nn.sigmoid(gate)
    silu = gate * sigmoid
    hidden_ref[...] = (silu * up).astype(jnp.bfloat16)
    gate_factor = up * sigmoid * (1.0 + gate * (1.0 - sigmoid))
    for i, group in enumerate(groups):
        lanes = slice(group[0] * TILE, (group[-1] + 1) * TILE)
        factor_refs[2 * i][...] = gate_factor[:, lanes]
        factor_refs[2 * i + 1][...] = silu[:, lanes]
    for copy in copies[4:]:
        copy.wait()
    blocks = down_exp_ref.shape[0]
    per = down_ref.shape[0] // blocks
    for b in range(blocks):
        scale = jnp.exp2(down_exp_ref[b].astype(jnp.float32))
        codes = down_ref[pl.ds(b * per, per), :].astype(jnp.float32)
        weight_ref[pl.ds(b * per, per), :] = (codes * scale).astype(jnp.bfloat16)


def prepare(groups, count, *operands):
    units, width = operands[4].shape
    lanes = sum(map(len, groups)) * TILE
    factors = [pltpu.VMEM((units, len(group) * TILE), jnp.float32) for group in groups for _ in range(2)]
    weight, hidden, *factors = pl.pallas_call(
        functools.partial(prepare_kernel, groups, count),
        out_shape=(
            pltpu.VMEM((units, width), jnp.bfloat16),
            pltpu.VMEM((units, lanes), jnp.bfloat16),
            *factors,
        ),
        in_specs=[LEFT] * 6,
        out_specs=[WHOLE] * (2 + len(factors)),
        scratch_shapes=[pltpu.VMEM(operand.shape, operand.dtype) for operand in operands]
        + [pltpu.SemaphoreType.DMA((len(operands),))],
        compiler_params=PARAMS,
        cost_estimate=COST,
    )(*[pltpu.with_memory_space_constraint(operand, pltpu.HBM) for operand in operands])
    return weight, hidden, [factors[2 * i : 2 * i + 2] for i in range(len(groups))]


def restored(slot_ref, count, width):
    keep = slot_ref.shape[1]
    free = TILE - count
    slot = slot_ref[...]
    low = slot[count:, :]
    parts = [low[:, at : at + width - keep] for at in range(0, keep, width - keep)]
    parts.append(jnp.zeros((free, width - keep), slot.dtype))
    return slot, jnp.concatenate(parts, axis=0)


def grads(group, count, slope, factor_refs, before_refs, grad_refs):
    where = spread(grad_refs[0].shape[1], group, count)
    for factor_ref, before_ref, grad_ref in zip(factor_refs, before_refs, grad_refs):
        grad = (slope * factor_ref[...]).astype(jnp.bfloat16)
        placed = lax.dot_general(grad, where, (((1,), (1,)), ((), ())), preferred_element_type=jnp.float32)
        if before_ref is not None:
            placed += before_ref[...].astype(jnp.float32)
        grad_ref[...] = placed.astype(jnp.bfloat16)


def stage_kernel(group, count, first, *refs):
    slot_refs, refs = refs[: len(group)], refs[len(group) :]
    weight_ref, factor_refs, refs = refs[0], refs[1:3], refs[3:]
    before_refs, refs = ((None, None), refs) if first else (refs[:2], refs[2:])
    incoming_ref, *grad_refs = refs
    width = weight_ref.shape[1]
    keep = slot_refs[0].shape[1]
    for i, ref in enumerate(slot_refs):
        slot, rest = restored(ref, count, width)
        incoming_ref[i * TILE : (i + 1) * TILE, :keep] = slot
        incoming_ref[i * TILE : (i + 1) * TILE, keep:] = rest
    slope = lax.dot_general(
        weight_ref[...], incoming_ref[...], (((1,), (1,)), ((), ())), preferred_element_type=jnp.float32
    )
    grads(group, count, slope, factor_refs, before_refs, grad_refs)


def stage(group, count, tokens, slots, weight, factors, before):
    units, width = weight.shape
    operands = (*slots, weight, *factors, *before)
    return pl.pallas_call(
        functools.partial(stage_kernel, group, count, len(before) == 0),
        out_shape=(
            pltpu.VMEM((len(group) * TILE, width), jnp.bfloat16),
            pltpu.VMEM((units, tokens), jnp.bfloat16),
            pltpu.VMEM((units, tokens), jnp.bfloat16),
        ),
        in_specs=[WHOLE] * len(operands),
        out_specs=[WHOLE] * 3,
        compiler_params=PARAMS,
        cost_estimate=COST,
    )(*operands)


def last_kernel(group, count, chunk, *refs):
    slot_ref, *earlier_refs = refs[: -11]
    weight_ref, hidden_ref = refs[-11:-9]
    factor_refs, before_refs = refs[-9:-7], refs[-7:-5]
    down_ref, *grad_refs, tile_ref, sems = refs[-5:]
    width = weight_ref.shape[1]
    keep = slot_ref.shape[1]
    slot, rest = restored(slot_ref, count, width)
    newest = jnp.concatenate([slot, rest], axis=1)
    hidden = hidden_ref[...]
    copies = []
    for at in range(0, width, chunk):
        parts = [ref[:, at : at + chunk] for ref in earlier_refs] + [newest[:, at : at + chunk]]
        incoming = jnp.concatenate(parts, axis=0)
        down = jnp.dot(hidden, incoming, preferred_element_type=jnp.float32)
        tile_ref[:, at : at + chunk] = down.astype(jnp.bfloat16)
        copy = pltpu.make_async_copy(
            tile_ref.at[:, pl.ds(at, chunk)], down_ref.at[:, pl.ds(at, chunk)], sems.at[at // chunk]
        )
        copy.start()
        copies.append(copy)
    slope = lax.dot_general(
        weight_ref[...], newest, (((1,), (1,)), ((), ())), preferred_element_type=jnp.float32
    )
    grads(group, count, slope, factor_refs, before_refs, grad_refs)
    for copy in copies:
        copy.wait()


def last(group, count, slot, earlier, weight, hidden, factors, before):
    units, width = weight.shape
    tokens = before[0].shape[1]
    chunk = width // 8
    operands = (slot, *earlier, weight, hidden, *factors, *before)
    return pl.pallas_call(
        functools.partial(last_kernel, group, count, chunk),
        out_shape=(
            jax.ShapeDtypeStruct((units, width), jnp.bfloat16),
            jax.ShapeDtypeStruct((units, tokens), jnp.bfloat16),
            jax.ShapeDtypeStruct((units, tokens), jnp.bfloat16),
        ),
        in_specs=[WHOLE] * len(operands),
        out_specs=[LEFT, WHOLE, WHOLE],
        scratch_shapes=[
            pltpu.VMEM((units, width), jnp.bfloat16),
            pltpu.SemaphoreType.DMA((width // chunk,)),
        ],
        compiler_params=PARAMS,
        cost_estimate=COST,
    )(*operands)


def fanned(gate_codes, gate_exponents, up_codes, up_exponents, down_codes, down_exponents, grad_held):
    n = lax.axis_size("tp")
    count = grad_held.shape[1]
    p = pack(grad_held[0])
    got = {}
    for flip in [n // 2, *range(2, n // 2, 2), *range(n // 2 + 2, n, 2), 1, 0]:
        got[flip] = send(p, flip, 1)
    groups = [list(range(n // 2)), list(range(n // 2, n - 1)), [n - 1]]
    weight, hidden, factors = prepare(
        groups,
        count,
        gate_codes[0].T,
        gate_exponents.transpose(2, 0, 1),
        up_codes[0].T,
        up_exponents.transpose(2, 0, 1),
        down_codes[0],
        down_exponents.transpose(1, 0, 2),
    )
    for flip in range(2, n, 2):
        got[flip], *_ = lax.optimization_barrier((got[flip], hidden) if flip == 2 else (got[flip], got[3]))
        got[flip + 1] = send(got[flip], 1, 0)
    earlier, before = [], []
    for group, pair in zip(groups[:2], factors):
        incoming, *before = stage(group, count, n * count, [got[j] for j in group], weight, pair, before)
        earlier.append(incoming)
    down_grad, gate_grad, up_grad = last(groups[2], count, got[n - 1], earlier, weight, hidden, factors[2], before)
    return down_grad[None], gate_grad.T[None], up_grad.T[None]


def dequantize(codes, exponents, target_axis):
    per = codes.shape[target_axis] // exponents.shape[target_axis]
    scales = jnp.exp2(jnp.repeat(exponents, per, axis=target_axis).astype(jnp.float32))
    return (codes.astype(jnp.float32) * scales).astype(jnp.bfloat16)


def ringed(gate_codes, gate_exponents, up_codes, up_exponents, down_codes, down_exponents, grad_held):
    gate = dequantize(gate_codes[0], gate_exponents[0], 1).astype(jnp.float32)
    up = dequantize(up_codes[0], up_exponents[0], 1).astype(jnp.float32)
    weight = dequantize(down_codes[0], down_exponents[0], 0)
    count = lax.axis_size("section")
    received = lax.ppermute(grad_held[0], "section", [(i, (i - 1) % count) for i in range(count)])
    incoming = lax.all_gather(received, "tp", axis=0, tiled=True)
    sigmoid = jax.nn.sigmoid(gate)
    silu = gate * sigmoid
    hidden = (silu * up).astype(jnp.bfloat16)
    down_grad = lax.dot_general(hidden, incoming, (((0,), (0,)), ((), ())), preferred_element_type=jnp.float32)
    slope = lax.dot_general(incoming, weight, (((1,), (1,)), ((), ())), preferred_element_type=jnp.float32)
    gate_grad = (slope * up * sigmoid * (1.0 + gate * (1.0 - sigmoid))).astype(jnp.bfloat16)
    up_grad = (slope * silu).astype(jnp.bfloat16)
    return down_grad.astype(jnp.bfloat16)[None], gate_grad[None], up_grad[None]


def body(*operands):
    n = lax.axis_size("tp")
    count, width = operands[-1].shape[1:]
    free = TILE - count
    small = n & (n - 1) == 0 and 4 <= n <= TILE
    fits = 0 < free < TILE and count % free == 0 and width * free % (TILE * 8 * 128) == 0
    return fanned(*operands) if small and fits else ringed(*operands)


def solution(mesh):
    wide, tall = P("section", None, "tp"), P("section", "tp", None)
    return jax.shard_map(
        body,
        mesh=mesh,
        in_specs=(wide, wide, wide, wide, tall, tall, tall),
        out_specs=(tall, wide, wide),
        check_vma=False,
    )
```

```python
import functools

import jax
import jax.numpy as jnp
from jax import lax
from jax.experimental import pallas as pl
from jax.experimental.pallas import tpu as pltpu
from jax.sharding import PartitionSpec as P

TILE = 16
WHOLE = pl.BlockSpec(memory_space=pltpu.VMEM)
LEFT = pl.BlockSpec(memory_space=pltpu.HBM)
COST = pl.CostEstimate(flops=0, bytes_accessed=16 * 1024 * 1024, transcendentals=0)
PARAMS = pltpu.CompilerParams(vmem_limit_bytes=24 * 1024 * 1024)


def send(array, flip, hop):
    sections, count = lax.axis_size("section"), lax.axis_size("tp")
    if hop == 0:
        return lax.ppermute(array, "tp", [(t, t ^ flip) for t in range(count)])
    pairs = [
        (s * count + t, ((s - hop) % sections) * count + (t ^ flip))
        for s in range(sections)
        for t in range(count)
    ]
    return lax.ppermute(array, ("section", "tp"), pairs)


def fetched(refs, held_refs, sems):
    copies = [pltpu.make_async_copy(ref, held, sems.at[i]) for i, (ref, held) in enumerate(zip(refs, held_refs))]
    for copy in copies:
        copy.start()
    return copies


def pack_kernel(held_ref, packed_ref, rows_ref, sems):
    for copy in fetched([held_ref], [rows_ref], sems):
        copy.wait()
    count, width = rows_ref.shape
    free = TILE - count
    keep = width * count // TILE
    rows = rows_ref[...]
    parts = [rows[at : at + free, keep:] for at in range(0, count, free)]
    packed_ref[...] = jnp.concatenate([rows[:, :keep], jnp.concatenate(parts, axis=1)], axis=0)


def pack(rows):
    count, width = rows.shape
    return pl.pallas_call(
        pack_kernel,
        out_shape=pltpu.VMEM((TILE, width * count // TILE), jnp.bfloat16),
        in_specs=[LEFT],
        out_specs=WHOLE,
        scratch_shapes=[pltpu.VMEM(rows.shape, rows.dtype), pltpu.SemaphoreType.DMA((1,))],
        compiler_params=PARAMS,
    )(pltpu.with_memory_space_constraint(rows, pltpu.HBM))


def spread(tokens, slots, count):
    shape = (tokens, len(slots) * TILE)
    lane = lax.broadcasted_iota(jnp.int32, shape, 1)
    row = lane & (TILE - 1)
    place = lane >> (TILE.bit_length() - 1)
    slot = jnp.full(shape, slots[0], jnp.int32)
    for i in range(1, len(slots)):
        slot = jnp.where(place == i, slots[i], slot)
    token = (slot ^ lax.axis_index("tp")) * count + row
    hit = (lax.broadcasted_iota(jnp.int32, shape, 0) == token) & (row < count)
    return jnp.where(hit, 1.0, 0.0).astype(jnp.bfloat16)


def decoded(codes_ref, exponents_ref):
    blocks = exponents_ref.shape[0]
    per = codes_ref.shape[0] // blocks
    parts = []
    for b in range(blocks):
        scale = jnp.exp2(exponents_ref[b].astype(jnp.float32))
        codes = codes_ref[pl.ds(b * per, per), :].astype(jnp.float32)
        parts.append((codes * scale).astype(jnp.bfloat16))
    return jnp.concatenate(parts, axis=0)


def prepare_kernel(groups, count, *refs):
    gate_ref, gate_exp_ref, up_ref, up_exp_ref, down_ref, down_exp_ref = held = refs[-7:-1]
    copies = fetched(refs[:6], held, refs[-1])
    weight_ref, hidden_ref = refs[6:8]
    factor_refs = refs[8:-7]
    for copy in copies[:4]:
        copy.wait()
    where = spread(gate_ref.shape[1], sum(groups, []), count)
    gate = jnp.dot(decoded(gate_ref, gate_exp_ref), where, preferred_element_type=jnp.float32)
    up = jnp.dot(decoded(up_ref, up_exp_ref), where, preferred_element_type=jnp.float32)
    sigmoid = jax.nn.sigmoid(gate)
    silu = gate * sigmoid
    hidden_ref[...] = (silu * up).astype(jnp.bfloat16)
    gate_factor = up * sigmoid * (1.0 + gate * (1.0 - sigmoid))
    at = 0
    for i, group in enumerate(groups):
        lanes = slice(at, at + len(group) * TILE)
        at = lanes.stop
        factor_refs[2 * i][...] = gate_factor[:, lanes]
        factor_refs[2 * i + 1][...] = silu[:, lanes]
    for copy in copies[4:]:
        copy.wait()
    blocks = down_exp_ref.shape[0]
    per = down_ref.shape[0] // blocks
    for b in range(blocks):
        scale = jnp.exp2(down_exp_ref[b].astype(jnp.float32))
        codes = down_ref[pl.ds(b * per, per), :].astype(jnp.float32)
        weight_ref[pl.ds(b * per, per), :] = (codes * scale).astype(jnp.bfloat16)


def prepare(groups, count, *operands):
    units, width = operands[4].shape
    lanes = sum(map(len, groups)) * TILE
    factors = [pltpu.VMEM((units, len(group) * TILE), jnp.float32) for group in groups for _ in range(2)]
    weight, hidden, *factors = pl.pallas_call(
        functools.partial(prepare_kernel, groups, count),
        out_shape=(
            pltpu.VMEM((units, width), jnp.bfloat16),
            pltpu.VMEM((units, lanes), jnp.bfloat16),
            *factors,
        ),
        in_specs=[LEFT] * 6,
        out_specs=[WHOLE] * (2 + len(factors)),
        scratch_shapes=[pltpu.VMEM(operand.shape, operand.dtype) for operand in operands]
        + [pltpu.SemaphoreType.DMA((len(operands),))],
        compiler_params=PARAMS,
        cost_estimate=COST,
    )(*[pltpu.with_memory_space_constraint(operand, pltpu.HBM) for operand in operands])
    return weight, hidden, [factors[2 * i : 2 * i + 2] for i in range(len(groups))]


def restore(slot_refs, incoming_ref, count):
    free = TILE - count
    width = incoming_ref.shape[1]
    for i, slot_ref in enumerate(slot_refs):
        keep = slot_ref.shape[1]
        slot = slot_ref[...]
        low = slot[count:, :]
        parts = [low[:, at : at + width - keep] for at in range(0, keep, width - keep)]
        parts.append(jnp.zeros((free, width - keep), slot.dtype))
        incoming_ref[i * TILE : (i + 1) * TILE, :keep] = slot
        incoming_ref[i * TILE : (i + 1) * TILE, keep:] = jnp.concatenate(parts, axis=0)


def grads(group, count, slope, factor_refs, before_refs, grad_refs):
    where = spread(grad_refs[0].shape[1], group, count)
    for factor_ref, before_ref, grad_ref in zip(factor_refs, before_refs, grad_refs):
        grad = (slope * factor_ref[...]).astype(jnp.bfloat16)
        placed = lax.dot_general(grad, where, (((1,), (1,)), ((), ())), preferred_element_type=jnp.float32)
        if before_ref is not None:
            placed += before_ref[...].astype(jnp.float32)
        grad_ref[...] = placed.astype(jnp.bfloat16)


def stage_kernel(group, count, first, *refs):
    slot_refs, refs = refs[: len(group)], refs[len(group) :]
    weight_ref, factor_refs, refs = refs[0], refs[1:3], refs[3:]
    before_refs, refs = ((None, None), refs) if first else (refs[:2], refs[2:])
    incoming_ref, *grad_refs = refs
    restore(slot_refs, incoming_ref, count)
    slope = lax.dot_general(
        weight_ref[...], incoming_ref[...], (((1,), (1,)), ((), ())), preferred_element_type=jnp.float32
    )
    grads(group, count, slope, factor_refs, before_refs, grad_refs)


def stage(group, count, tokens, slots, weight, factors, before):
    units, width = weight.shape
    operands = (*slots, weight, *factors, *before)
    return pl.pallas_call(
        functools.partial(stage_kernel, group, count, len(before) == 0),
        out_shape=(
            pltpu.VMEM((len(group) * TILE, width), jnp.bfloat16),
            pltpu.VMEM((units, tokens), jnp.bfloat16),
            pltpu.VMEM((units, tokens), jnp.bfloat16),
        ),
        in_specs=[WHOLE] * len(operands),
        out_specs=[WHOLE] * 3,
        compiler_params=PARAMS,
        cost_estimate=COST,
    )(*operands)


def last_kernel(group, count, chunk, *refs):
    slot_refs, earlier_ref = refs[: len(group)], refs[len(group)]
    weight_ref, hidden_ref = refs[-12:-10]
    factor_refs, before_refs = refs[-10:-8], refs[-8:-6]
    down_ref, *grad_refs, newest_ref, tile_ref, sems = refs[-6:]
    width = weight_ref.shape[1]
    restore(slot_refs, newest_ref, count)
    hidden = hidden_ref[...]
    copies = []
    for at in range(0, width, chunk):
        incoming = jnp.concatenate([earlier_ref[:, at : at + chunk], newest_ref[:, at : at + chunk]], axis=0)
        down = jnp.dot(hidden, incoming, preferred_element_type=jnp.float32)
        tile_ref[:, at : at + chunk] = down.astype(jnp.bfloat16)
        copy = pltpu.make_async_copy(
            tile_ref.at[:, pl.ds(at, chunk)], down_ref.at[:, pl.ds(at, chunk)], sems.at[at // chunk]
        )
        copy.start()
        copies.append(copy)
    slope = lax.dot_general(
        weight_ref[...], newest_ref[...], (((1,), (1,)), ((), ())), preferred_element_type=jnp.float32
    )
    grads(group, count, slope, factor_refs, before_refs, grad_refs)
    for copy in copies:
        copy.wait()


def last(group, count, slots, earlier, weight, hidden, factors, before):
    units, width = weight.shape
    tokens = before[0].shape[1]
    chunk = width // 8
    operands = (*slots, earlier, weight, hidden, *factors, *before)
    return pl.pallas_call(
        functools.partial(last_kernel, group, count, chunk),
        out_shape=(
            jax.ShapeDtypeStruct((units, width), jnp.bfloat16),
            jax.ShapeDtypeStruct((units, tokens), jnp.bfloat16),
            jax.ShapeDtypeStruct((units, tokens), jnp.bfloat16),
        ),
        in_specs=[WHOLE] * len(operands),
        out_specs=[LEFT, WHOLE, WHOLE],
        scratch_shapes=[
            pltpu.VMEM((len(group) * TILE, width), jnp.bfloat16),
            pltpu.VMEM((units, width), jnp.bfloat16),
            pltpu.SemaphoreType.DMA((width // chunk,)),
        ],
        compiler_params=PARAMS,
        cost_estimate=COST,
    )(*operands)


def fanned(gate_codes, gate_exponents, up_codes, up_exponents, down_codes, down_exponents, grad_held):
    n = lax.axis_size("tp")
    count = grad_held.shape[1]
    p = pack(grad_held[0])
    groups = [[f for f in range(n) if f & (f - 1) == 0], [f for f in reversed(range(n)) if f & (f - 1)]]
    got = {}
    for flip in reversed(groups[0]):
        got[flip] = send(p, flip, 1)
    weight, hidden, factors = prepare(
        groups,
        count,
        gate_codes[0].T,
        gate_exponents.transpose(2, 0, 1),
        up_codes[0].T,
        up_exponents.transpose(2, 0, 1),
        down_codes[0],
        down_exponents.transpose(1, 0, 2),
    )
    for flip, tied in zip(groups[0][1:], lax.optimization_barrier((*[got[f] for f in groups[0][1:]], hidden))):
        got[flip] = tied
    for flip in sorted(groups[1], key=lambda f: -(f & 1) * f):
        step = flip & -flip
        if flip & 1 and flip - 1 not in groups[0]:
            step = flip - 1
        got[flip] = send(got[flip - step], step, 0)
    early = [got[j] for j in groups[0]]
    earlier, *before = stage(groups[0], count, n * count, early, weight, factors[0], [])
    late = [got[j] for j in groups[1]]
    down_grad, gate_grad, up_grad = last(groups[1], count, late, earlier, weight, hidden, factors[1], before)
    return down_grad[None], gate_grad.T[None], up_grad.T[None]


def dequantize(codes, exponents, target_axis):
    per = codes.shape[target_axis] // exponents.shape[target_axis]
    scales = jnp.exp2(jnp.repeat(exponents, per, axis=target_axis).astype(jnp.float32))
    return (codes.astype(jnp.float32) * scales).astype(jnp.bfloat16)


def ringed(gate_codes, gate_exponents, up_codes, up_exponents, down_codes, down_exponents, grad_held):
    gate = dequantize(gate_codes[0], gate_exponents[0], 1).astype(jnp.float32)
    up = dequantize(up_codes[0], up_exponents[0], 1).astype(jnp.float32)
    weight = dequantize(down_codes[0], down_exponents[0], 0)
    count = lax.axis_size("section")
    received = lax.ppermute(grad_held[0], "section", [(i, (i - 1) % count) for i in range(count)])
    incoming = lax.all_gather(received, "tp", axis=0, tiled=True)
    sigmoid = jax.nn.sigmoid(gate)
    silu = gate * sigmoid
    hidden = (silu * up).astype(jnp.bfloat16)
    down_grad = lax.dot_general(hidden, incoming, (((0,), (0,)), ((), ())), preferred_element_type=jnp.float32)
    slope = lax.dot_general(incoming, weight, (((1,), (1,)), ((), ())), preferred_element_type=jnp.float32)
    gate_grad = (slope * up * sigmoid * (1.0 + gate * (1.0 - sigmoid))).astype(jnp.bfloat16)
    up_grad = (slope * silu).astype(jnp.bfloat16)
    return down_grad.astype(jnp.bfloat16)[None], gate_grad[None], up_grad[None]


def body(*operands):
    n = lax.axis_size("tp")
    count, width = operands[-1].shape[1:]
    free = TILE - count
    small = n & (n - 1) == 0 and 4 <= n <= TILE
    fits = 0 < free < TILE and count % free == 0 and width * free % (TILE * 8 * 128) == 0
    return fanned(*operands) if small and fits else ringed(*operands)


def solution(mesh):
    wide, tall = P("section", None, "tp"), P("section", "tp", None)
    return jax.shard_map(
        body,
        mesh=mesh,
        in_specs=(wide, wide, wide, wide, tall, tall, tall),
        out_specs=(tall, wide, wide),
        check_vma=False,
    )
```

```python
import functools

import jax
import jax.numpy as jnp
from jax import lax
from jax.experimental import pallas as pl
from jax.experimental.pallas import tpu as pltpu
from jax.sharding import PartitionSpec as P

TILE = 16
WHOLE = pl.BlockSpec(memory_space=pltpu.VMEM)
LEFT = pl.BlockSpec(memory_space=pltpu.HBM)
COST = pl.CostEstimate(flops=0, bytes_accessed=16 * 1024 * 1024, transcendentals=0)
PARAMS = pltpu.CompilerParams(vmem_limit_bytes=24 * 1024 * 1024)


def send(array, flip, hop):
    sections, count = lax.axis_size("section"), lax.axis_size("tp")
    if hop == 0:
        return lax.ppermute(array, "tp", [(t, t ^ flip) for t in range(count)])
    pairs = [
        (s * count + t, ((s - hop) % sections) * count + (t ^ flip))
        for s in range(sections)
        for t in range(count)
    ]
    return lax.ppermute(array, ("section", "tp"), pairs)


def started(source_ref, target_ref, sem):
    copy = pltpu.make_async_copy(source_ref, target_ref, sem)
    copy.start()
    return [copy]


def fetched(refs, held_refs, sems):
    return sum([started(ref, held, sems.at[i]) for i, (ref, held) in enumerate(zip(refs, held_refs))], [])


def pack_kernel(held_ref, packed_ref, rows_ref, sems):
    for copy in fetched([held_ref], [rows_ref], sems):
        copy.wait()
    count, width = rows_ref.shape
    free = TILE - count
    keep = width * count // TILE
    rows = rows_ref[...]
    parts = [rows[at : at + free, keep:] for at in range(0, count, free)]
    packed_ref[...] = jnp.concatenate([rows[:, :keep], jnp.concatenate(parts, axis=1)], axis=0)


def pack(rows):
    count, width = rows.shape
    return pl.pallas_call(
        pack_kernel,
        out_shape=pltpu.VMEM((TILE, width * count // TILE), jnp.bfloat16),
        in_specs=[LEFT],
        out_specs=WHOLE,
        scratch_shapes=[pltpu.VMEM(rows.shape, rows.dtype), pltpu.SemaphoreType.DMA((1,))],
        compiler_params=PARAMS,
    )(pltpu.with_memory_space_constraint(rows, pltpu.HBM))


def spread(tokens, slots, count):
    shape = (tokens, len(slots) * TILE)
    lane = lax.broadcasted_iota(jnp.int32, shape, 1)
    row = lane & (TILE - 1)
    place = lane >> (TILE.bit_length() - 1)
    slot = jnp.full(shape, slots[0], jnp.int32)
    for i in range(1, len(slots)):
        slot = jnp.where(place == i, slots[i], slot)
    token = (slot ^ lax.axis_index("tp")) * count + row
    hit = (lax.broadcasted_iota(jnp.int32, shape, 0) == token) & (row < count)
    return jnp.where(hit, 1.0, 0.0).astype(jnp.bfloat16)


def decoded(codes_ref, exponents_ref):
    blocks = exponents_ref.shape[0]
    per = codes_ref.shape[0] // blocks
    parts = []
    for b in range(blocks):
        scale = jnp.exp2(exponents_ref[b].astype(jnp.float32))
        codes = codes_ref[pl.ds(b * per, per), :].astype(jnp.float32)
        parts.append((codes * scale).astype(jnp.bfloat16))
    return jnp.concatenate(parts, axis=0)


def prepare_kernel(groups, count, *refs):
    gate_ref, gate_exp_ref, up_ref, up_exp_ref, down_ref, down_exp_ref = held = refs[-7:-1]
    copies = fetched(refs[:6], held, refs[-1])
    weight_ref, hidden_ref = refs[6:8]
    factor_refs = refs[8:-7]
    for copy in copies[:4]:
        copy.wait()
    where = spread(gate_ref.shape[1], sum(groups, []), count)
    gate = jnp.dot(decoded(gate_ref, gate_exp_ref), where, preferred_element_type=jnp.float32)
    up = jnp.dot(decoded(up_ref, up_exp_ref), where, preferred_element_type=jnp.float32)
    sigmoid = jax.nn.sigmoid(gate)
    silu = gate * sigmoid
    hidden_ref[...] = (silu * up).astype(jnp.bfloat16)
    gate_factor = up * sigmoid * (1.0 + gate * (1.0 - sigmoid))
    at = 0
    for i, group in enumerate(groups):
        lanes = slice(at, at + len(group) * TILE)
        at = lanes.stop
        factor_refs[2 * i][...] = gate_factor[:, lanes]
        factor_refs[2 * i + 1][...] = silu[:, lanes]
    for copy in copies[4:]:
        copy.wait()
    blocks = down_exp_ref.shape[0]
    per = down_ref.shape[0] // blocks
    for b in range(blocks):
        scale = jnp.exp2(down_exp_ref[b].astype(jnp.float32))
        codes = down_ref[pl.ds(b * per, per), :].astype(jnp.float32)
        weight_ref[pl.ds(b * per, per), :] = (codes * scale).astype(jnp.bfloat16)


def prepare(groups, count, *operands):
    units, width = operands[4].shape
    lanes = sum(map(len, groups)) * TILE
    factors = [pltpu.VMEM((units, len(group) * TILE), jnp.float32) for group in groups for _ in range(2)]
    weight, hidden, *factors = pl.pallas_call(
        functools.partial(prepare_kernel, groups, count),
        out_shape=(
            pltpu.VMEM((units, width), jnp.bfloat16),
            pltpu.VMEM((units, lanes), jnp.bfloat16),
            *factors,
        ),
        in_specs=[LEFT] * 6,
        out_specs=[WHOLE] * (2 + len(factors)),
        scratch_shapes=[pltpu.VMEM(operand.shape, operand.dtype) for operand in operands]
        + [pltpu.SemaphoreType.DMA((len(operands),))],
        compiler_params=PARAMS,
        cost_estimate=COST,
    )(*[pltpu.with_memory_space_constraint(operand, pltpu.HBM) for operand in operands])
    return weight, hidden, [factors[2 * i : 2 * i + 2] for i in range(len(groups))]


def restore(slot_refs, incoming_ref, count):
    free = TILE - count
    width = incoming_ref.shape[1]
    for i, slot_ref in enumerate(slot_refs):
        keep = slot_ref.shape[1]
        slot = slot_ref[...]
        low = slot[count:, :]
        parts = [low[:, at : at + width - keep] for at in range(0, keep, width - keep)]
        parts.append(jnp.zeros((free, width - keep), slot.dtype))
        incoming_ref[i * TILE : (i + 1) * TILE, :keep] = slot
        incoming_ref[i * TILE : (i + 1) * TILE, keep:] = jnp.concatenate(parts, axis=0)


def grads(group, count, slope, factor_refs, before_refs, grad_refs):
    where = spread(grad_refs[0].shape[1], group, count)
    for factor_ref, before_ref, grad_ref in zip(factor_refs, before_refs, grad_refs):
        grad = (slope * factor_ref[...]).astype(jnp.bfloat16)
        placed = lax.dot_general(grad, where, (((1,), (1,)), ((), ())), preferred_element_type=jnp.float32)
        if before_ref is not None:
            placed += before_ref[...].astype(jnp.float32)
        grad_ref[...] = placed.astype(jnp.bfloat16)


def stage_kernel(group, count, first, *refs):
    slot_refs, refs = refs[: len(group)], refs[len(group) :]
    weight_ref, factor_refs, refs = refs[0], refs[1:3], refs[3:]
    before_refs, refs = ((None, None), refs) if first else (refs[:2], refs[2:])
    incoming_ref, *grad_refs = refs
    restore(slot_refs, incoming_ref, count)
    slope = lax.dot_general(
        weight_ref[...], incoming_ref[...], (((1,), (1,)), ((), ())), preferred_element_type=jnp.float32
    )
    grads(group, count, slope, factor_refs, before_refs, grad_refs)


def stage(group, count, tokens, slots, weight, factors, before):
    units, width = weight.shape
    operands = (*slots, weight, *factors, *before)
    return pl.pallas_call(
        functools.partial(stage_kernel, group, count, len(before) == 0),
        out_shape=(
            pltpu.VMEM((len(group) * TILE, width), jnp.bfloat16),
            pltpu.VMEM((units, tokens), jnp.bfloat16),
            pltpu.VMEM((units, tokens), jnp.bfloat16),
        ),
        in_specs=[WHOLE] * len(operands),
        out_specs=[WHOLE] * 3,
        compiler_params=PARAMS,
        cost_estimate=COST,
    )(*operands)


def last_kernel(group, count, parts, *refs):
    slot_refs, earlier_ref = refs[: len(group)], refs[len(group)]
    weight_ref, hidden_ref, *factor_refs = refs[len(group) + 1 : len(group) + 5]
    before_refs, out_refs = refs[len(group) + 5 : len(group) + 7], refs[len(group) + 7 : len(group) + 10]
    newest_ref, *held_refs, sems = refs[len(group) + 10 :]
    restore(slot_refs, newest_ref, count)
    incoming = jnp.concatenate([earlier_ref[...], newest_ref[...]], axis=0)
    rows = hidden_ref.shape[0] // parts
    copies = []
    for i in range(parts):
        here = pl.ds(i * rows, rows)
        down = jnp.dot(hidden_ref[here, :], incoming, preferred_element_type=jnp.float32)
        held_refs[0][here, :] = down.astype(jnp.bfloat16)
        copies += started(held_refs[0].at[here, :], out_refs[0].at[here, :], sems.at[2 + i])
    slope = lax.dot_general(
        weight_ref[...], newest_ref[...], (((1,), (1,)), ((), ())), preferred_element_type=jnp.float32
    )
    grads(group, count, slope, factor_refs, before_refs, held_refs[1:])
    for i in range(2):
        copies += started(held_refs[1 + i], out_refs[1 + i], sems.at[i])
    for copy in copies:
        copy.wait()


def last(group, count, slots, earlier, weight, hidden, factors, before):
    units, width = weight.shape
    tokens = before[0].shape[1]
    parts = 2 if units % (2 * TILE) == 0 else 1
    operands = (*slots, earlier, weight, hidden, *factors, *before)
    shapes = [(units, width), (units, tokens), (units, tokens)]
    return pl.pallas_call(
        functools.partial(last_kernel, group, count, parts),
        out_shape=[jax.ShapeDtypeStruct(shape, jnp.bfloat16) for shape in shapes],
        in_specs=[WHOLE] * len(operands),
        out_specs=[LEFT] * 3,
        scratch_shapes=[
            pltpu.VMEM((len(group) * TILE, width), jnp.bfloat16),
            *[pltpu.VMEM(shape, jnp.bfloat16) for shape in shapes],
            pltpu.SemaphoreType.DMA((2 + parts,)),
        ],
        compiler_params=PARAMS,
        cost_estimate=COST,
    )(*operands)


def fanned(gate_codes, gate_exponents, up_codes, up_exponents, down_codes, down_exponents, grad_held):
    n = lax.axis_size("tp")
    count = grad_held.shape[1]
    p = pack(grad_held[0])
    first = [f for f in range(n) if f & (f - 1) == 0]
    groups = [[*first, 3], [f for f in range(5, n) if f not in first]]
    got = {}
    for flip in reversed(first):
        got[flip] = send(p, flip, 1)
    weight, hidden, factors = prepare(
        groups,
        count,
        gate_codes[0].T,
        gate_exponents.transpose(2, 0, 1),
        up_codes[0].T,
        up_exponents.transpose(2, 0, 1),
        down_codes[0],
        down_exponents.transpose(1, 0, 2),
    )
    got[3] = send(got[2], 1, 0)
    got[n // 2], *_ = lax.optimization_barrier((got[n // 2], hidden))
    early = [got[j] for j in groups[0]]
    earlier, *before = stage(groups[0], count, n * count, early, weight, factors[0], [])
    for flip in groups[1]:
        step = 1 if flip - 1 in first else 2
        if flip & 1 and step == 2:
            got[flip - step], *_ = lax.optimization_barrier((got[flip - step], earlier))
        got[flip] = send(got[flip - step], step, 0)
    late = [got[j] for j in groups[1]]
    down_grad, gate_grad, up_grad = last(groups[1], count, late, earlier, weight, hidden, factors[1], before)
    return down_grad[None], gate_grad.T[None], up_grad.T[None]


def dequantize(codes, exponents, target_axis):
    per = codes.shape[target_axis] // exponents.shape[target_axis]
    scales = jnp.exp2(jnp.repeat(exponents, per, axis=target_axis).astype(jnp.float32))
    return (codes.astype(jnp.float32) * scales).astype(jnp.bfloat16)


def ringed(gate_codes, gate_exponents, up_codes, up_exponents, down_codes, down_exponents, grad_held):
    gate = dequantize(gate_codes[0], gate_exponents[0], 1).astype(jnp.float32)
    up = dequantize(up_codes[0], up_exponents[0], 1).astype(jnp.float32)
    weight = dequantize(down_codes[0], down_exponents[0], 0)
    count = lax.axis_size("section")
    received = lax.ppermute(grad_held[0], "section", [(i, (i - 1) % count) for i in range(count)])
    incoming = lax.all_gather(received, "tp", axis=0, tiled=True)
    sigmoid = jax.nn.sigmoid(gate)
    silu = gate * sigmoid
    hidden = (silu * up).astype(jnp.bfloat16)
    down_grad = lax.dot_general(hidden, incoming, (((0,), (0,)), ((), ())), preferred_element_type=jnp.float32)
    slope = lax.dot_general(incoming, weight, (((1,), (1,)), ((), ())), preferred_element_type=jnp.float32)
    gate_grad = (slope * up * sigmoid * (1.0 + gate * (1.0 - sigmoid))).astype(jnp.bfloat16)
    up_grad = (slope * silu).astype(jnp.bfloat16)
    return down_grad.astype(jnp.bfloat16)[None], gate_grad[None], up_grad[None]


def body(*operands):
    n = lax.axis_size("tp")
    count, width = operands[-1].shape[1:]
    free = TILE - count
    small = n & (n - 1) == 0 and 4 <= n <= TILE
    fits = 0 < free < TILE and count % free == 0 and width * free % (TILE * 8 * 128) == 0
    return fanned(*operands) if small and fits else ringed(*operands)


def solution(mesh):
    wide, tall = P("section", None, "tp"), P("section", "tp", None)
    return jax.shard_map(
        body,
        mesh=mesh,
        in_specs=(wide, wide, wide, wide, tall, tall, tall),
        out_specs=(tall, wide, wide),
        check_vma=False,
    )
```

```python
import functools

import jax
import jax.numpy as jnp
from jax import lax
from jax.experimental import pallas as pl
from jax.experimental.pallas import tpu as pltpu
from jax.sharding import PartitionSpec as P

TILE = 16
WHOLE = pl.BlockSpec(memory_space=pltpu.VMEM)
LEFT = pl.BlockSpec(memory_space=pltpu.HBM)
COST = pl.CostEstimate(flops=0, bytes_accessed=16 * 1024 * 1024, transcendentals=0)
PARAMS = pltpu.CompilerParams(vmem_limit_bytes=24 * 1024 * 1024)


def send(array, flip, hop):
    sections, count = lax.axis_size("section"), lax.axis_size("tp")
    if hop == 0:
        return lax.ppermute(array, "tp", [(t, t ^ flip) for t in range(count)])
    pairs = [
        (s * count + t, ((s - hop) % sections) * count + (t ^ flip))
        for s in range(sections)
        for t in range(count)
    ]
    return lax.ppermute(array, ("section", "tp"), pairs)


def started(source_ref, target_ref, sem):
    copy = pltpu.make_async_copy(source_ref, target_ref, sem)
    copy.start()
    return [copy]


def fetched(refs, held_refs, sems):
    return sum([started(ref, held, sems.at[i]) for i, (ref, held) in enumerate(zip(refs, held_refs))], [])


def pack_kernel(held_ref, packed_ref, rows_ref, sems):
    for copy in fetched([held_ref], [rows_ref], sems):
        copy.wait()
    count, width = rows_ref.shape
    free = TILE - count
    keep = width * count // TILE
    rows = rows_ref[...]
    parts = [rows[at : at + free, keep:] for at in range(0, count, free)]
    packed_ref[...] = jnp.concatenate([rows[:, :keep], jnp.concatenate(parts, axis=1)], axis=0)


def pack(rows):
    count, width = rows.shape
    return pl.pallas_call(
        pack_kernel,
        out_shape=pltpu.VMEM((TILE, width * count // TILE), jnp.bfloat16),
        in_specs=[LEFT],
        out_specs=WHOLE,
        scratch_shapes=[pltpu.VMEM(rows.shape, rows.dtype), pltpu.SemaphoreType.DMA((1,))],
        compiler_params=PARAMS,
    )(pltpu.with_memory_space_constraint(rows, pltpu.HBM))


def spread(tokens, slots, count):
    shape = (tokens, len(slots) * TILE)
    lane = lax.broadcasted_iota(jnp.int32, shape, 1)
    row = lane & (TILE - 1)
    place = lane >> (TILE.bit_length() - 1)
    slot = jnp.full(shape, slots[0], jnp.int32)
    for i in range(1, len(slots)):
        slot = jnp.where(place == i, slots[i], slot)
    token = (slot ^ lax.axis_index("tp")) * count + row
    hit = (lax.broadcasted_iota(jnp.int32, shape, 0) == token) & (row < count)
    return jnp.where(hit, 1.0, 0.0).astype(jnp.bfloat16)


def decoded(codes_ref, exponents_ref):
    blocks = exponents_ref.shape[0]
    per = codes_ref.shape[0] // blocks
    parts = []
    for b in range(blocks):
        scale = jnp.exp2(exponents_ref[b].astype(jnp.float32))
        codes = codes_ref[pl.ds(b * per, per), :].astype(jnp.float32)
        parts.append((codes * scale).astype(jnp.bfloat16))
    return jnp.concatenate(parts, axis=0)


def prepare_kernel(groups, count, *refs):
    gate_ref, gate_exp_ref, up_ref, up_exp_ref, down_ref, down_exp_ref = held = refs[-7:-1]
    copies = fetched(refs[:6], held, refs[-1])
    weight_ref, hidden_ref = refs[6:8]
    factor_refs = refs[8:-7]
    for copy in copies[:4]:
        copy.wait()
    where = spread(gate_ref.shape[1], sum(groups, []), count)
    gate = jnp.dot(decoded(gate_ref, gate_exp_ref), where, preferred_element_type=jnp.float32)
    up = jnp.dot(decoded(up_ref, up_exp_ref), where, preferred_element_type=jnp.float32)
    sigmoid = jax.nn.sigmoid(gate)
    silu = gate * sigmoid
    hidden_ref[...] = (silu * up).astype(jnp.bfloat16)
    gate_factor = up * sigmoid * (1.0 + gate * (1.0 - sigmoid))
    at = 0
    for i, group in enumerate(groups):
        lanes = slice(at, at + len(group) * TILE)
        at = lanes.stop
        factor_refs[2 * i][...] = gate_factor[:, lanes]
        factor_refs[2 * i + 1][...] = silu[:, lanes]
    for copy in copies[4:]:
        copy.wait()
    blocks = down_exp_ref.shape[0]
    per = down_ref.shape[0] // blocks
    for b in range(blocks):
        scale = jnp.exp2(down_exp_ref[b].astype(jnp.float32))
        codes = down_ref[pl.ds(b * per, per), :].astype(jnp.float32)
        weight_ref[pl.ds(b * per, per), :] = (codes * scale).astype(jnp.bfloat16)


def prepare(groups, count, *operands):
    units, width = operands[4].shape
    lanes = sum(map(len, groups)) * TILE
    factors = [pltpu.VMEM((units, len(group) * TILE), jnp.float32) for group in groups for _ in range(2)]
    weight, hidden, *factors = pl.pallas_call(
        functools.partial(prepare_kernel, groups, count),
        out_shape=(
            pltpu.VMEM((units, width), jnp.bfloat16),
            pltpu.VMEM((units, lanes), jnp.bfloat16),
            *factors,
        ),
        in_specs=[LEFT] * 6,
        out_specs=[WHOLE] * (2 + len(factors)),
        scratch_shapes=[pltpu.VMEM(operand.shape, operand.dtype) for operand in operands]
        + [pltpu.SemaphoreType.DMA((len(operands),))],
        compiler_params=PARAMS,
        cost_estimate=COST,
    )(*[pltpu.with_memory_space_constraint(operand, pltpu.HBM) for operand in operands])
    return weight, hidden, [factors[2 * i : 2 * i + 2] for i in range(len(groups))]


def restore(slot_refs, incoming_ref, count):
    free = TILE - count
    width = incoming_ref.shape[1]
    for i, slot_ref in enumerate(slot_refs):
        keep = slot_ref.shape[1]
        slot = slot_ref[...]
        low = slot[count:, :]
        parts = [low[:, at : at + width - keep] for at in range(0, keep, width - keep)]
        parts.append(jnp.zeros((free, width - keep), slot.dtype))
        incoming_ref[i * TILE : (i + 1) * TILE, :keep] = slot
        incoming_ref[i * TILE : (i + 1) * TILE, keep:] = jnp.concatenate(parts, axis=0)


def grads(group, count, slope, factor_refs, before_refs, grad_refs):
    where = spread(grad_refs[0].shape[1], group, count)
    for factor_ref, before_ref, grad_ref in zip(factor_refs, before_refs, grad_refs):
        grad = (slope * factor_ref[...]).astype(jnp.bfloat16)
        placed = lax.dot_general(grad, where, (((1,), (1,)), ((), ())), preferred_element_type=jnp.float32)
        if before_ref is not None:
            placed += before_ref[...].astype(jnp.float32)
        grad_ref[...] = placed.astype(jnp.bfloat16)


def stage_kernel(group, count, first, *refs):
    slot_refs, refs = refs[: len(group)], refs[len(group) :]
    weight_ref, factor_refs, refs = refs[0], refs[1:3], refs[3:]
    before_refs, refs = ((None, None), refs) if first else (refs[:2], refs[2:])
    incoming_ref, *grad_refs = refs
    restore(slot_refs, incoming_ref, count)
    slope = lax.dot_general(
        weight_ref[...], incoming_ref[...], (((1,), (1,)), ((), ())), preferred_element_type=jnp.float32
    )
    grads(group, count, slope, factor_refs, before_refs, grad_refs)


def stage(group, count, tokens, slots, weight, factors, before):
    units, width = weight.shape
    operands = (*slots, weight, *factors, *before)
    return pl.pallas_call(
        functools.partial(stage_kernel, group, count, len(before) == 0),
        out_shape=(
            pltpu.VMEM((len(group) * TILE, width), jnp.bfloat16),
            pltpu.VMEM((units, tokens), jnp.bfloat16),
            pltpu.VMEM((units, tokens), jnp.bfloat16),
        ),
        in_specs=[WHOLE] * len(operands),
        out_specs=[WHOLE] * 3,
        compiler_params=PARAMS,
        cost_estimate=COST,
    )(*operands)


def last_kernel(group, count, parts, *refs):
    slot_refs, earlier_ref = refs[: len(group)], refs[len(group)]
    weight_ref, hidden_ref, *factor_refs = refs[len(group) + 1 : len(group) + 5]
    before_refs, out_refs = refs[len(group) + 5 : len(group) + 7], refs[len(group) + 7 : len(group) + 10]
    newest_ref, *held_refs, sems = refs[len(group) + 10 :]
    restore(slot_refs, newest_ref, count)
    incoming = jnp.concatenate([earlier_ref[...], newest_ref[...]], axis=0)
    rows = hidden_ref.shape[0] // parts
    copies = []
    for i in range(parts):
        here = pl.ds(i * rows, rows)
        down = jnp.dot(hidden_ref[here, :], incoming, preferred_element_type=jnp.float32)
        held_refs[0][here, :] = down.astype(jnp.bfloat16)
        copies += started(held_refs[0].at[here, :], out_refs[0].at[here, :], sems.at[2 + i])
    slope = lax.dot_general(
        weight_ref[...], newest_ref[...], (((1,), (1,)), ((), ())), preferred_element_type=jnp.float32
    )
    grads(group, count, slope, factor_refs, before_refs, held_refs[1:])
    for i in range(2):
        copies += started(held_refs[1 + i], out_refs[1 + i], sems.at[i])
    for copy in copies:
        copy.wait()


def last(group, count, slots, earlier, weight, hidden, factors, before):
    units, width = weight.shape
    tokens = before[0].shape[1]
    parts = 2 if units % (2 * TILE) == 0 else 1
    operands = (*slots, earlier, weight, hidden, *factors, *before)
    shapes = [(units, width), (units, tokens), (units, tokens)]
    return pl.pallas_call(
        functools.partial(last_kernel, group, count, parts),
        out_shape=[jax.ShapeDtypeStruct(shape, jnp.bfloat16) for shape in shapes],
        in_specs=[WHOLE] * len(operands),
        out_specs=[LEFT] * 3,
        scratch_shapes=[
            pltpu.VMEM((len(group) * TILE, width), jnp.bfloat16),
            *[pltpu.VMEM(shape, jnp.bfloat16) for shape in shapes],
            pltpu.SemaphoreType.DMA((2 + parts,)),
        ],
        compiler_params=PARAMS,
        cost_estimate=COST,
    )(*operands)


def fanned(gate_codes, gate_exponents, up_codes, up_exponents, down_codes, down_exponents, grad_held):
    n = lax.axis_size("tp")
    count = grad_held.shape[1]
    p = pack(grad_held[0])
    first = [f for f in range(n) if f & (f - 1) == 0]
    groups = [first, [f for f in range(n) if f not in first]]
    got = {}
    for flip in reversed(first):
        got[flip] = send(p, flip, 1)
    for flip in reversed(groups[1]):
        step = flip & -flip
        if flip & 1 and flip - 1 not in first:
            step = flip - 1
        got[flip] = send(got[flip - step], step, 0)
    weight, hidden, factors = prepare(
        groups,
        count,
        gate_codes[0].T,
        gate_exponents.transpose(2, 0, 1),
        up_codes[0].T,
        up_exponents.transpose(2, 0, 1),
        down_codes[0],
        down_exponents.transpose(1, 0, 2),
    )
    early = [got[j] for j in groups[0]]
    earlier, *before = stage(groups[0], count, n * count, early, weight, factors[0], [])
    late = [got[j] for j in groups[1]]
    down_grad, gate_grad, up_grad = last(groups[1], count, late, earlier, weight, hidden, factors[1], before)
    return down_grad[None], gate_grad.T[None], up_grad.T[None]


def dequantize(codes, exponents, target_axis):
    per = codes.shape[target_axis] // exponents.shape[target_axis]
    scales = jnp.exp2(jnp.repeat(exponents, per, axis=target_axis).astype(jnp.float32))
    return (codes.astype(jnp.float32) * scales).astype(jnp.bfloat16)


def ringed(gate_codes, gate_exponents, up_codes, up_exponents, down_codes, down_exponents, grad_held):
    gate = dequantize(gate_codes[0], gate_exponents[0], 1).astype(jnp.float32)
    up = dequantize(up_codes[0], up_exponents[0], 1).astype(jnp.float32)
    weight = dequantize(down_codes[0], down_exponents[0], 0)
    count = lax.axis_size("section")
    received = lax.ppermute(grad_held[0], "section", [(i, (i - 1) % count) for i in range(count)])
    incoming = lax.all_gather(received, "tp", axis=0, tiled=True)
    sigmoid = jax.nn.sigmoid(gate)
    silu = gate * sigmoid
    hidden = (silu * up).astype(jnp.bfloat16)
    down_grad = lax.dot_general(hidden, incoming, (((0,), (0,)), ((), ())), preferred_element_type=jnp.float32)
    slope = lax.dot_general(incoming, weight, (((1,), (1,)), ((), ())), preferred_element_type=jnp.float32)
    gate_grad = (slope * up * sigmoid * (1.0 + gate * (1.0 - sigmoid))).astype(jnp.bfloat16)
    up_grad = (slope * silu).astype(jnp.bfloat16)
    return down_grad.astype(jnp.bfloat16)[None], gate_grad[None], up_grad[None]


def body(*operands):
    n = lax.axis_size("tp")
    count, width = operands[-1].shape[1:]
    free = TILE - count
    small = n & (n - 1) == 0 and 4 <= n <= TILE
    fits = 0 < free < TILE and count % free == 0 and width * free % (TILE * 8 * 128) == 0
    return fanned(*operands) if small and fits else ringed(*operands)


def solution(mesh):
    wide, tall = P("section", None, "tp"), P("section", "tp", None)
    return jax.shard_map(
        body,
        mesh=mesh,
        in_specs=(wide, wide, wide, wide, tall, tall, tall),
        out_specs=(tall, wide, wide),
        check_vma=False,
    )
```

```python
import functools

import jax
import jax.numpy as jnp
from jax import lax
from jax.experimental import pallas as pl
from jax.experimental.pallas import tpu as pltpu
from jax.sharding import PartitionSpec as P

TILE = 16
WHOLE = pl.BlockSpec(memory_space=pltpu.VMEM)
LEFT = pl.BlockSpec(memory_space=pltpu.HBM)
COST = pl.CostEstimate(flops=0, bytes_accessed=16 * 1024 * 1024, transcendentals=0)
PARAMS = pltpu.CompilerParams(vmem_limit_bytes=24 * 1024 * 1024)


def send(array, flip, hop):
    sections, count = lax.axis_size("section"), lax.axis_size("tp")
    if hop == 0:
        return lax.ppermute(array, "tp", [(t, t ^ flip) for t in range(count)])
    pairs = [
        (s * count + t, ((s - hop) % sections) * count + (t ^ flip))
        for s in range(sections)
        for t in range(count)
    ]
    return lax.ppermute(array, ("section", "tp"), pairs)


def started(source_ref, target_ref, sem):
    copy = pltpu.make_async_copy(source_ref, target_ref, sem)
    copy.start()
    return [copy]


def fetched(refs, held_refs, sems):
    return sum([started(ref, held, sems.at[i]) for i, (ref, held) in enumerate(zip(refs, held_refs))], [])


def pack_kernel(held_ref, packed_ref, rows_ref, sems):
    for copy in fetched([held_ref], [rows_ref], sems):
        copy.wait()
    count, width = rows_ref.shape
    free = TILE - count
    keep = width * count // TILE
    rows = rows_ref[...]
    parts = [rows[at : at + free, keep:] for at in range(0, count, free)]
    packed_ref[...] = jnp.concatenate([rows[:, :keep], jnp.concatenate(parts, axis=1)], axis=0)


def pack(rows):
    count, width = rows.shape
    return pl.pallas_call(
        pack_kernel,
        out_shape=pltpu.VMEM((TILE, width * count // TILE), jnp.bfloat16),
        in_specs=[LEFT],
        out_specs=WHOLE,
        scratch_shapes=[pltpu.VMEM(rows.shape, rows.dtype), pltpu.SemaphoreType.DMA((1,))],
        compiler_params=PARAMS,
    )(pltpu.with_memory_space_constraint(rows, pltpu.HBM))


def spread(tokens, slots, count):
    shape = (tokens, len(slots) * TILE)
    lane = lax.broadcasted_iota(jnp.int32, shape, 1)
    row = lane & (TILE - 1)
    place = lane >> (TILE.bit_length() - 1)
    slot = jnp.full(shape, slots[0], jnp.int32)
    for i in range(1, len(slots)):
        slot = jnp.where(place == i, slots[i], slot)
    token = (slot ^ lax.axis_index("tp")) * count + row
    hit = (lax.broadcasted_iota(jnp.int32, shape, 0) == token) & (row < count)
    return jnp.where(hit, 1.0, 0.0).astype(jnp.bfloat16)


def decoded(codes_ref, exponents_ref):
    blocks = exponents_ref.shape[0]
    per = codes_ref.shape[0] // blocks
    parts = []
    for b in range(blocks):
        scale = jnp.exp2(exponents_ref[b].astype(jnp.float32))
        codes = codes_ref[pl.ds(b * per, per), :].astype(jnp.float32)
        parts.append((codes * scale).astype(jnp.bfloat16))
    return jnp.concatenate(parts, axis=0)


def prepare_kernel(groups, count, *refs):
    gate_ref, gate_exp_ref, up_ref, up_exp_ref, down_ref, down_exp_ref = held = refs[-7:-1]
    copies = fetched(refs[:6], held, refs[-1])
    weight_ref, hidden_ref = refs[6:8]
    factor_refs = refs[8:-7]
    for copy in copies[:4]:
        copy.wait()
    where = spread(gate_ref.shape[1], sum(groups, []), count)
    gate = jnp.dot(decoded(gate_ref, gate_exp_ref), where, preferred_element_type=jnp.float32)
    up = jnp.dot(decoded(up_ref, up_exp_ref), where, preferred_element_type=jnp.float32)
    sigmoid = jax.nn.sigmoid(gate)
    silu = gate * sigmoid
    hidden_ref[...] = (silu * up).astype(jnp.bfloat16)
    gate_factor = up * sigmoid * (1.0 + gate * (1.0 - sigmoid))
    at = 0
    for i, group in enumerate(groups):
        lanes = slice(at, at + len(group) * TILE)
        at = lanes.stop
        factor_refs[2 * i][...] = gate_factor[:, lanes]
        factor_refs[2 * i + 1][...] = silu[:, lanes]
    for copy in copies[4:]:
        copy.wait()
    blocks = down_exp_ref.shape[0]
    per = down_ref.shape[0] // blocks
    for b in range(blocks):
        scale = jnp.exp2(down_exp_ref[b].astype(jnp.float32))
        codes = down_ref[pl.ds(b * per, per), :].astype(jnp.float32)
        weight_ref[pl.ds(b * per, per), :] = (codes * scale).astype(jnp.bfloat16)


def prepare(groups, count, *operands):
    units, width = operands[4].shape
    lanes = sum(map(len, groups)) * TILE
    factors = [pltpu.VMEM((units, len(group) * TILE), jnp.float32) for group in groups for _ in range(2)]
    weight, hidden, *factors = pl.pallas_call(
        functools.partial(prepare_kernel, groups, count),
        out_shape=(
            pltpu.VMEM((units, width), jnp.bfloat16),
            pltpu.VMEM((units, lanes), jnp.bfloat16),
            *factors,
        ),
        in_specs=[LEFT] * 6,
        out_specs=[WHOLE] * (2 + len(factors)),
        scratch_shapes=[pltpu.VMEM(operand.shape, operand.dtype) for operand in operands]
        + [pltpu.SemaphoreType.DMA((len(operands),))],
        compiler_params=PARAMS,
        cost_estimate=COST,
    )(*[pltpu.with_memory_space_constraint(operand, pltpu.HBM) for operand in operands])
    return weight, hidden, [factors[2 * i : 2 * i + 2] for i in range(len(groups))]


def restore(slot_refs, incoming_ref, count):
    free = TILE - count
    width = incoming_ref.shape[1]
    for i, slot_ref in enumerate(slot_refs):
        keep = slot_ref.shape[1]
        slot = slot_ref[...]
        low = slot[count:, :]
        parts = [low[:, at : at + width - keep] for at in range(0, keep, width - keep)]
        parts.append(jnp.zeros((free, width - keep), slot.dtype))
        incoming_ref[i * TILE : (i + 1) * TILE, :keep] = slot
        incoming_ref[i * TILE : (i + 1) * TILE, keep:] = jnp.concatenate(parts, axis=0)


def grads(group, count, slope, factor_refs, before_refs, grad_refs):
    where = spread(grad_refs[0].shape[1], group, count)
    for factor_ref, before_ref, grad_ref in zip(factor_refs, before_refs, grad_refs):
        grad = (slope * factor_ref[...]).astype(jnp.bfloat16)
        placed = lax.dot_general(grad, where, (((1,), (1,)), ((), ())), preferred_element_type=jnp.float32)
        if before_ref is not None:
            placed += before_ref[...].astype(jnp.float32)
        grad_ref[...] = placed.astype(jnp.bfloat16)


def stage_kernel(group, count, first, *refs):
    slot_refs, refs = refs[: len(group)], refs[len(group) :]
    weight_ref, factor_refs, refs = refs[0], refs[1:3], refs[3:]
    before_refs, refs = ((None, None), refs) if first else (refs[:2], refs[2:])
    incoming_ref, *grad_refs = refs
    restore(slot_refs, incoming_ref, count)
    slope = lax.dot_general(
        weight_ref[...], incoming_ref[...], (((1,), (1,)), ((), ())), preferred_element_type=jnp.float32
    )
    grads(group, count, slope, factor_refs, before_refs, grad_refs)


def stage(group, count, tokens, slots, weight, factors, before):
    units, width = weight.shape
    operands = (*slots, weight, *factors, *before)
    return pl.pallas_call(
        functools.partial(stage_kernel, group, count, len(before) == 0),
        out_shape=(
            pltpu.VMEM((len(group) * TILE, width), jnp.bfloat16),
            pltpu.VMEM((units, tokens), jnp.bfloat16),
            pltpu.VMEM((units, tokens), jnp.bfloat16),
        ),
        in_specs=[WHOLE] * len(operands),
        out_specs=[WHOLE] * 3,
        compiler_params=PARAMS,
        cost_estimate=COST,
    )(*operands)


def last_kernel(slots, group, count, parts, *refs):
    slot_refs, earlier_refs, refs = refs[: len(group)], refs[len(group) : slots], refs[slots:]
    weight_ref, hidden_ref, *factor_refs = refs[:4]
    before_refs, out_refs, (newest_ref, *held_refs, sems) = refs[4:6], refs[6:9], refs[9:]
    restore(slot_refs, newest_ref, count)
    chunk = weight_ref.shape[1] // parts
    copies = []
    for i in range(parts):
        here = pl.ds(i * chunk, chunk)
        incoming = jnp.concatenate([ref[:, here] for ref in (*earlier_refs, newest_ref)], axis=0)
        down = jnp.dot(hidden_ref[...], incoming, preferred_element_type=jnp.float32)
        held_refs[0][:, here] = down.astype(jnp.bfloat16)
        copies += started(held_refs[0].at[:, here], out_refs[0].at[:, here], sems.at[2 + i])
    slope = lax.dot_general(
        weight_ref[...], newest_ref[...], (((1,), (1,)), ((), ())), preferred_element_type=jnp.float32
    )
    grads(group, count, slope, factor_refs, before_refs, held_refs[1:])
    for i in range(2):
        copies += started(held_refs[1 + i], out_refs[1 + i], sems.at[i])
    for copy in copies:
        copy.wait()


def last(group, count, slots, earlier, weight, hidden, factors, before):
    units, width = weight.shape
    tokens = before[0].shape[1]
    parts = 4
    operands = (*slots, *earlier, weight, hidden, *factors, *before)
    shapes = [(units, width), (units, tokens), (units, tokens)]
    return pl.pallas_call(
        functools.partial(last_kernel, len(slots) + len(earlier), group, count, parts),
        out_shape=[jax.ShapeDtypeStruct(shape, jnp.bfloat16) for shape in shapes],
        in_specs=[WHOLE] * len(operands),
        out_specs=[LEFT] * 3,
        scratch_shapes=[
            pltpu.VMEM((len(group) * TILE, width), jnp.bfloat16),
            *[pltpu.VMEM(shape, jnp.bfloat16) for shape in shapes],
            pltpu.SemaphoreType.DMA((2 + parts,)),
        ],
        compiler_params=PARAMS,
        cost_estimate=COST,
    )(*operands)


def fanned(gate_codes, gate_exponents, up_codes, up_exponents, down_codes, down_exponents, grad_held):
    n = lax.axis_size("tp")
    count = grad_held.shape[1]
    p = pack(grad_held[0])
    first = [f for f in range(n) if f & (f - 1) == 0]
    rest = [f for f in range(n) if f not in first]
    late = [f for f in rest if f - n // 2 in first]
    groups = [group for group in (first[::-1], [f for f in reversed(rest) if f not in late], late[::-1]) if group]
    got = {}
    for flip in reversed(first):
        got[flip] = send(p, flip, 1)
    for flip in reversed(rest):
        step = flip & -flip
        if flip & 1 and flip - 1 not in first:
            step = flip - 1
        got[flip] = send(got[flip - step], step, 0)
    weight, hidden, factors = prepare(
        groups,
        count,
        gate_codes[0].T,
        gate_exponents.transpose(2, 0, 1),
        up_codes[0].T,
        up_exponents.transpose(2, 0, 1),
        down_codes[0],
        down_exponents.transpose(1, 0, 2),
    )
    earlier, before = [], []
    for group, pair in zip(groups[:-1], factors):
        incoming, *before = stage(group, count, n * count, [got[j] for j in group], weight, pair, before)
        earlier.append(incoming)
    arrived = [got[j] for j in groups[-1]]
    down_grad, gate_grad, up_grad = last(groups[-1], count, arrived, earlier, weight, hidden, factors[-1], before)
    return down_grad[None], gate_grad.T[None], up_grad.T[None]


def dequantize(codes, exponents, target_axis):
    per = codes.shape[target_axis] // exponents.shape[target_axis]
    scales = jnp.exp2(jnp.repeat(exponents, per, axis=target_axis).astype(jnp.float32))
    return (codes.astype(jnp.float32) * scales).astype(jnp.bfloat16)


def ringed(gate_codes, gate_exponents, up_codes, up_exponents, down_codes, down_exponents, grad_held):
    gate = dequantize(gate_codes[0], gate_exponents[0], 1).astype(jnp.float32)
    up = dequantize(up_codes[0], up_exponents[0], 1).astype(jnp.float32)
    weight = dequantize(down_codes[0], down_exponents[0], 0)
    count = lax.axis_size("section")
    received = lax.ppermute(grad_held[0], "section", [(i, (i - 1) % count) for i in range(count)])
    incoming = lax.all_gather(received, "tp", axis=0, tiled=True)
    sigmoid = jax.nn.sigmoid(gate)
    silu = gate * sigmoid
    hidden = (silu * up).astype(jnp.bfloat16)
    down_grad = lax.dot_general(hidden, incoming, (((0,), (0,)), ((), ())), preferred_element_type=jnp.float32)
    slope = lax.dot_general(incoming, weight, (((1,), (1,)), ((), ())), preferred_element_type=jnp.float32)
    gate_grad = (slope * up * sigmoid * (1.0 + gate * (1.0 - sigmoid))).astype(jnp.bfloat16)
    up_grad = (slope * silu).astype(jnp.bfloat16)
    return down_grad.astype(jnp.bfloat16)[None], gate_grad[None], up_grad[None]


def body(*operands):
    n = lax.axis_size("tp")
    count, width = operands[-1].shape[1:]
    free = TILE - count
    small = n & (n - 1) == 0 and 4 <= n <= TILE
    fits = 0 < free < TILE and count % free == 0 and width * free % (TILE * 128) == 0 and width % (4 * 128) == 0
    return fanned(*operands) if small and fits else ringed(*operands)


def solution(mesh):
    wide, tall = P("section", None, "tp"), P("section", "tp", None)
    return jax.shard_map(
        body,
        mesh=mesh,
        in_specs=(wide, wide, wide, wide, tall, tall, tall),
        out_specs=(tall, wide, wide),
        check_vma=False,
    )
```

```python
import functools

import jax
import jax.numpy as jnp
from jax import lax
from jax.experimental import pallas as pl
from jax.experimental.pallas import tpu as pltpu
from jax.sharding import PartitionSpec as P

TILE = 16
WHOLE = pl.BlockSpec(memory_space=pltpu.VMEM)
LEFT = pl.BlockSpec(memory_space=pltpu.HBM)
COST = pl.CostEstimate(flops=0, bytes_accessed=16 * 1024 * 1024, transcendentals=0)
PARAMS = pltpu.CompilerParams(vmem_limit_bytes=24 * 1024 * 1024)


def send(array, flip, hop):
    sections, count = lax.axis_size("section"), lax.axis_size("tp")
    if hop == 0:
        return lax.ppermute(array, "tp", [(t, t ^ flip) for t in range(count)])
    pairs = [
        (s * count + t, ((s - hop) % sections) * count + (t ^ flip))
        for s in range(sections)
        for t in range(count)
    ]
    return lax.ppermute(array, ("section", "tp"), pairs)


def started(source_ref, target_ref, sem, priority=0):
    copy = pltpu.make_async_copy(source_ref, target_ref, sem)
    copy.start(priority=priority)
    return [copy]


def fetched(refs, held_refs, sems):
    return sum([started(ref, held, sems.at[i]) for i, (ref, held) in enumerate(zip(refs, held_refs))], [])


def pack_kernel(held_ref, packed_ref, rows_ref, sems):
    for copy in fetched([held_ref], [rows_ref], sems):
        copy.wait()
    count, width = rows_ref.shape
    free = TILE - count
    keep = width * count // TILE
    rows = rows_ref[...]
    parts = [rows[at : at + free, keep:] for at in range(0, count, free)]
    packed_ref[...] = jnp.concatenate([rows[:, :keep], jnp.concatenate(parts, axis=1)], axis=0)


def pack(rows):
    count, width = rows.shape
    return pl.pallas_call(
        pack_kernel,
        out_shape=pltpu.VMEM((TILE, width * count // TILE), jnp.bfloat16),
        in_specs=[LEFT],
        out_specs=WHOLE,
        scratch_shapes=[pltpu.VMEM(rows.shape, rows.dtype), pltpu.SemaphoreType.DMA((1,))],
        compiler_params=PARAMS,
    )(pltpu.with_memory_space_constraint(rows, pltpu.HBM))


def spread(tokens, slots, count):
    shape = (tokens, len(slots) * TILE)
    lane = lax.broadcasted_iota(jnp.int32, shape, 1)
    row = lane & (TILE - 1)
    place = lane >> (TILE.bit_length() - 1)
    slot = jnp.full(shape, slots[0], jnp.int32)
    for i in range(1, len(slots)):
        slot = jnp.where(place == i, slots[i], slot)
    token = (slot ^ lax.axis_index("tp")) * count + row
    hit = (lax.broadcasted_iota(jnp.int32, shape, 0) == token) & (row < count)
    return jnp.where(hit, 1.0, 0.0).astype(jnp.bfloat16)


def decoded(codes_ref, exponents_ref):
    blocks = exponents_ref.shape[0]
    per = codes_ref.shape[0] // blocks
    parts = []
    for b in range(blocks):
        scale = jnp.exp2(exponents_ref[b].astype(jnp.float32))
        codes = codes_ref[pl.ds(b * per, per), :].astype(jnp.float32)
        parts.append((codes * scale).astype(jnp.bfloat16))
    return jnp.concatenate(parts, axis=0)


def prepare_kernel(groups, count, *refs):
    gate_ref, gate_exp_ref, up_ref, up_exp_ref, down_ref, down_exp_ref = held = refs[-7:-1]
    copies = fetched(refs[:6], held, refs[-1])
    weight_ref, hidden_ref = refs[6:8]
    factor_refs = refs[8:-7]
    for copy in copies[:4]:
        copy.wait()
    where = spread(gate_ref.shape[1], sum(groups, []), count)
    gate = jnp.dot(decoded(gate_ref, gate_exp_ref), where, preferred_element_type=jnp.float32)
    up = jnp.dot(decoded(up_ref, up_exp_ref), where, preferred_element_type=jnp.float32)
    sigmoid = jax.nn.sigmoid(gate)
    silu = gate * sigmoid
    hidden_ref[...] = (silu * up).astype(jnp.bfloat16)
    gate_factor = up * sigmoid * (1.0 + gate * (1.0 - sigmoid))
    at = 0
    for i, group in enumerate(groups):
        lanes = slice(at, at + len(group) * TILE)
        at = lanes.stop
        factor_refs[2 * i][...] = gate_factor[:, lanes]
        factor_refs[2 * i + 1][...] = silu[:, lanes]
    for copy in copies[4:]:
        copy.wait()
    blocks = down_exp_ref.shape[0]
    per = down_ref.shape[0] // blocks
    for b in range(blocks):
        scale = jnp.exp2(down_exp_ref[b].astype(jnp.float32))
        codes = down_ref[pl.ds(b * per, per), :].astype(jnp.float32)
        weight_ref[pl.ds(b * per, per), :] = (codes * scale).astype(jnp.bfloat16)


def prepare(groups, count, *operands):
    units, width = operands[4].shape
    lanes = sum(map(len, groups)) * TILE
    factors = [pltpu.VMEM((units, len(group) * TILE), jnp.float32) for group in groups for _ in range(2)]
    weight, hidden, *factors = pl.pallas_call(
        functools.partial(prepare_kernel, groups, count),
        out_shape=(
            pltpu.VMEM((units, width), jnp.bfloat16),
            pltpu.VMEM((units, lanes), jnp.bfloat16),
            *factors,
        ),
        in_specs=[LEFT] * 6,
        out_specs=[WHOLE] * (2 + len(factors)),
        scratch_shapes=[pltpu.VMEM(operand.shape, operand.dtype) for operand in operands]
        + [pltpu.SemaphoreType.DMA((len(operands),))],
        compiler_params=PARAMS,
        cost_estimate=COST,
    )(*[pltpu.with_memory_space_constraint(operand, pltpu.HBM) for operand in operands])
    return weight, hidden, [factors[2 * i : 2 * i + 2] for i in range(len(groups))]


def restore(slot_refs, incoming_ref, count):
    free = TILE - count
    width = incoming_ref.shape[1]
    for i, slot_ref in enumerate(slot_refs):
        keep = slot_ref.shape[1]
        slot = slot_ref[...]
        low = slot[count:, :]
        parts = [low[:, at : at + width - keep] for at in range(0, keep, width - keep)]
        parts.append(jnp.zeros((free, width - keep), slot.dtype))
        incoming_ref[i * TILE : (i + 1) * TILE, :keep] = slot
        incoming_ref[i * TILE : (i + 1) * TILE, keep:] = jnp.concatenate(parts, axis=0)


def grads(group, count, slope, factor_refs, before_refs, grad_refs):
    where = spread(grad_refs[0].shape[1], group, count)
    for factor_ref, before_ref, grad_ref in zip(factor_refs, before_refs, grad_refs):
        grad = (slope * factor_ref[...]).astype(jnp.bfloat16)
        placed = lax.dot_general(grad, where, (((1,), (1,)), ((), ())), preferred_element_type=jnp.float32)
        if before_ref is not None:
            placed += before_ref[...].astype(jnp.float32)
        grad_ref[...] = placed.astype(jnp.bfloat16)


def stage_kernel(group, count, first, *refs):
    slot_refs, refs = refs[: len(group)], refs[len(group) :]
    weight_ref, factor_refs, refs = refs[0], refs[1:3], refs[3:]
    before_refs, refs = ((None, None), refs) if first else (refs[:2], refs[2:])
    incoming_ref, *grad_refs = refs
    restore(slot_refs, incoming_ref, count)
    slope = lax.dot_general(
        weight_ref[...], incoming_ref[...], (((1,), (1,)), ((), ())), preferred_element_type=jnp.float32
    )
    grads(group, count, slope, factor_refs, before_refs, grad_refs)


def stage(group, count, tokens, slots, weight, factors, before):
    units, width = weight.shape
    operands = (*slots, weight, *factors, *before)
    return pl.pallas_call(
        functools.partial(stage_kernel, group, count, len(before) == 0),
        out_shape=(
            pltpu.VMEM((len(group) * TILE, width), jnp.bfloat16),
            pltpu.VMEM((units, tokens), jnp.bfloat16),
            pltpu.VMEM((units, tokens), jnp.bfloat16),
        ),
        in_specs=[WHOLE] * len(operands),
        out_specs=[WHOLE] * 3,
        compiler_params=PARAMS,
        cost_estimate=COST,
    )(*operands)


def last_kernel(slots, group, count, parts, *refs):
    slot_refs, earlier_refs, refs = refs[: len(group)], refs[len(group) : slots], refs[slots:]
    weight_ref, hidden_ref, *factor_refs = refs[:4]
    before_refs, out_refs, (newest_ref, *held_refs, sems) = refs[4:6], refs[6:9], refs[9:]
    restore(slot_refs, newest_ref, count)
    chunk = weight_ref.shape[1] // parts
    copies = []
    for i in range(parts):
        here = pl.ds(i * chunk, chunk)
        incoming = jnp.concatenate([ref[:, here] for ref in (*earlier_refs, newest_ref)], axis=0)
        down = jnp.dot(hidden_ref[...], incoming, preferred_element_type=jnp.float32)
        held_refs[0][:, here] = down.astype(jnp.bfloat16)
        copies += started(held_refs[0].at[:, here], out_refs[0].at[:, here], sems.at[2 + i], i % 2)
    slope = lax.dot_general(
        weight_ref[...], newest_ref[...], (((1,), (1,)), ((), ())), preferred_element_type=jnp.float32
    )
    grads(group, count, slope, factor_refs, before_refs, held_refs[1:])
    for i in range(2):
        copies += started(held_refs[1 + i], out_refs[1 + i], sems.at[i])
    for copy in copies:
        copy.wait()


def last(group, count, slots, earlier, weight, hidden, factors, before):
    units, width = weight.shape
    tokens = before[0].shape[1]
    parts = 4
    operands = (*slots, *earlier, weight, hidden, *factors, *before)
    shapes = [(units, width), (units, tokens), (units, tokens)]
    return pl.pallas_call(
        functools.partial(last_kernel, len(slots) + len(earlier), group, count, parts),
        out_shape=[jax.ShapeDtypeStruct(shape, jnp.bfloat16) for shape in shapes],
        in_specs=[WHOLE] * len(operands),
        out_specs=[LEFT] * 3,
        scratch_shapes=[
            pltpu.VMEM((len(group) * TILE, width), jnp.bfloat16),
            *[pltpu.VMEM(shape, jnp.bfloat16) for shape in shapes],
            pltpu.SemaphoreType.DMA((2 + parts,)),
        ],
        compiler_params=PARAMS,
        cost_estimate=COST,
    )(*operands)


def fanned(gate_codes, gate_exponents, up_codes, up_exponents, down_codes, down_exponents, grad_held):
    n = lax.axis_size("tp")
    count = grad_held.shape[1]
    p = pack(grad_held[0])
    first = [f for f in range(n) if f & (f - 1) == 0]
    rest = [f for f in range(n) if f not in first]
    groups = [first, [n - 1], rest[-2::-1]] if len(rest) > 1 else [first, rest]
    got = {}
    for flip in reversed(first):
        got[flip] = send(p, flip, 1)
    for flip, tied in zip(first[2:], lax.optimization_barrier([got[f] for f in first[2:]])):
        got[flip] = tied
    for flip in reversed(rest):
        step = flip & -flip
        if flip & 1 and flip - 1 not in first:
            step = flip - 1
        got[flip] = send(got[flip - step], step, 0)
    weight, hidden, factors = prepare(
        groups,
        count,
        gate_codes[0].T,
        gate_exponents.transpose(2, 0, 1),
        up_codes[0].T,
        up_exponents.transpose(2, 0, 1),
        down_codes[0],
        down_exponents.transpose(1, 0, 2),
    )
    earlier, before = [], []
    for group, pair in zip(groups[:-1], factors):
        incoming, *before = stage(group, count, n * count, [got[j] for j in group], weight, pair, before)
        earlier.append(incoming)
    arrived = [got[j] for j in groups[-1]]
    down_grad, gate_grad, up_grad = last(groups[-1], count, arrived, earlier, weight, hidden, factors[-1], before)
    return down_grad[None], gate_grad.T[None], up_grad.T[None]


def dequantize(codes, exponents, target_axis):
    per = codes.shape[target_axis] // exponents.shape[target_axis]
    scales = jnp.exp2(jnp.repeat(exponents, per, axis=target_axis).astype(jnp.float32))
    return (codes.astype(jnp.float32) * scales).astype(jnp.bfloat16)


def ringed(gate_codes, gate_exponents, up_codes, up_exponents, down_codes, down_exponents, grad_held):
    gate = dequantize(gate_codes[0], gate_exponents[0], 1).astype(jnp.float32)
    up = dequantize(up_codes[0], up_exponents[0], 1).astype(jnp.float32)
    weight = dequantize(down_codes[0], down_exponents[0], 0)
    count = lax.axis_size("section")
    received = lax.ppermute(grad_held[0], "section", [(i, (i - 1) % count) for i in range(count)])
    incoming = lax.all_gather(received, "tp", axis=0, tiled=True)
    sigmoid = jax.nn.sigmoid(gate)
    silu = gate * sigmoid
    hidden = (silu * up).astype(jnp.bfloat16)
    down_grad = lax.dot_general(hidden, incoming, (((0,), (0,)), ((), ())), preferred_element_type=jnp.float32)
    slope = lax.dot_general(incoming, weight, (((1,), (1,)), ((), ())), preferred_element_type=jnp.float32)
    gate_grad = (slope * up * sigmoid * (1.0 + gate * (1.0 - sigmoid))).astype(jnp.bfloat16)
    up_grad = (slope * silu).astype(jnp.bfloat16)
    return down_grad.astype(jnp.bfloat16)[None], gate_grad[None], up_grad[None]


def body(*operands):
    n = lax.axis_size("tp")
    count, width = operands[-1].shape[1:]
    free = TILE - count
    small = n & (n - 1) == 0 and 4 <= n <= TILE
    fits = 0 < free < TILE and count % free == 0 and width * free % (TILE * 128) == 0 and width % (4 * 128) == 0
    return fanned(*operands) if small and fits else ringed(*operands)


def solution(mesh):
    wide, tall = P("section", None, "tp"), P("section", "tp", None)
    return jax.shard_map(
        body,
        mesh=mesh,
        in_specs=(wide, wide, wide, wide, tall, tall, tall),
        out_specs=(tall, wide, wide),
        check_vma=False,
    )
```

```python
import functools

import jax
import jax.numpy as jnp
from jax import lax
from jax.experimental import pallas as pl
from jax.experimental.pallas import tpu as pltpu
from jax.sharding import PartitionSpec as P

TILE = 16
WHOLE = pl.BlockSpec(memory_space=pltpu.VMEM)
LEFT = pl.BlockSpec(memory_space=pltpu.HBM)
COST = pl.CostEstimate(flops=0, bytes_accessed=16 * 1024 * 1024, transcendentals=0)
PARAMS = pltpu.CompilerParams(vmem_limit_bytes=24 * 1024 * 1024)


def send(array, flip, hop):
    sections, count = lax.axis_size("section"), lax.axis_size("tp")
    if hop == 0:
        return lax.ppermute(array, "tp", [(t, t ^ flip) for t in range(count)])
    pairs = [
        (s * count + t, ((s - hop) % sections) * count + (t ^ flip))
        for s in range(sections)
        for t in range(count)
    ]
    return lax.ppermute(array, ("section", "tp"), pairs)


def started(source_ref, target_ref, sem, priority=0):
    copy = pltpu.make_async_copy(source_ref, target_ref, sem)
    copy.start(priority=priority)
    return [copy]


def fetched(refs, held_refs, sems):
    return sum([started(ref, held, sems.at[i]) for i, (ref, held) in enumerate(zip(refs, held_refs))], [])


def pack_kernel(held_ref, packed_ref, rows_ref, sems):
    for copy in fetched([held_ref], [rows_ref], sems):
        copy.wait()
    count, width = rows_ref.shape
    free = TILE - count
    keep = width * count // TILE
    rows = rows_ref[...]
    parts = [rows[at : at + free, keep:] for at in range(0, count, free)]
    packed_ref[...] = jnp.concatenate([rows[:, :keep], jnp.concatenate(parts, axis=1)], axis=0)


def pack(rows):
    count, width = rows.shape
    return pl.pallas_call(
        pack_kernel,
        out_shape=pltpu.VMEM((TILE, width * count // TILE), jnp.bfloat16),
        in_specs=[LEFT],
        out_specs=WHOLE,
        scratch_shapes=[pltpu.VMEM(rows.shape, rows.dtype), pltpu.SemaphoreType.DMA((1,))],
        compiler_params=PARAMS,
    )(pltpu.with_memory_space_constraint(rows, pltpu.HBM))


def spread(tokens, slots, count):
    shape = (tokens, len(slots) * TILE)
    lane = lax.broadcasted_iota(jnp.int32, shape, 1)
    row = lane & (TILE - 1)
    place = lane >> (TILE.bit_length() - 1)
    slot = jnp.full(shape, slots[0], jnp.int32)
    for i in range(1, len(slots)):
        slot = jnp.where(place == i, slots[i], slot)
    token = (slot ^ lax.axis_index("tp")) * count + row
    hit = (lax.broadcasted_iota(jnp.int32, shape, 0) == token) & (row < count)
    return jnp.where(hit, 1.0, 0.0).astype(jnp.bfloat16)


def decoded(codes_ref, exponents_ref):
    blocks = exponents_ref.shape[0]
    per = codes_ref.shape[0] // blocks
    parts = []
    for b in range(blocks):
        scale = jnp.exp2(exponents_ref[b].astype(jnp.float32))
        codes = codes_ref[pl.ds(b * per, per), :].astype(jnp.float32)
        parts.append((codes * scale).astype(jnp.bfloat16))
    return jnp.concatenate(parts, axis=0)


def prepare_kernel(groups, count, *refs):
    gate_ref, gate_exp_ref, up_ref, up_exp_ref, down_ref, down_exp_ref = held = refs[-7:-1]
    copies = fetched(refs[:6], held, refs[-1])
    weight_ref, hidden_ref = refs[6:8]
    factor_refs = refs[8:-7]
    for copy in copies[:4]:
        copy.wait()
    where = spread(gate_ref.shape[1], sum(groups, []), count)
    gate = jnp.dot(decoded(gate_ref, gate_exp_ref), where, preferred_element_type=jnp.float32)
    up = jnp.dot(decoded(up_ref, up_exp_ref), where, preferred_element_type=jnp.float32)
    sigmoid = jax.nn.sigmoid(gate)
    silu = gate * sigmoid
    hidden_ref[...] = (silu * up).astype(jnp.bfloat16)
    gate_factor = up * sigmoid * (1.0 + gate * (1.0 - sigmoid))
    at = 0
    for i, group in enumerate(groups):
        lanes = slice(at, at + len(group) * TILE)
        at = lanes.stop
        factor_refs[2 * i][...] = gate_factor[:, lanes]
        factor_refs[2 * i + 1][...] = silu[:, lanes]
    for copy in copies[4:]:
        copy.wait()
    blocks = down_exp_ref.shape[0]
    per = down_ref.shape[0] // blocks
    for b in range(blocks):
        scale = jnp.exp2(down_exp_ref[b].astype(jnp.float32))
        codes = down_ref[pl.ds(b * per, per), :].astype(jnp.float32)
        weight_ref[pl.ds(b * per, per), :] = (codes * scale).astype(jnp.bfloat16)


def prepare(groups, count, *operands):
    units, width = operands[4].shape
    lanes = sum(map(len, groups)) * TILE
    factors = [pltpu.VMEM((units, len(group) * TILE), jnp.float32) for group in groups for _ in range(2)]
    weight, hidden, *factors = pl.pallas_call(
        functools.partial(prepare_kernel, groups, count),
        out_shape=(
            pltpu.VMEM((units, width), jnp.bfloat16),
            pltpu.VMEM((units, lanes), jnp.bfloat16),
            *factors,
        ),
        in_specs=[LEFT] * 6,
        out_specs=[WHOLE] * (2 + len(factors)),
        scratch_shapes=[pltpu.VMEM(operand.shape, operand.dtype) for operand in operands]
        + [pltpu.SemaphoreType.DMA((len(operands),))],
        compiler_params=PARAMS,
        cost_estimate=COST,
    )(*[pltpu.with_memory_space_constraint(operand, pltpu.HBM) for operand in operands])
    return weight, hidden, [factors[2 * i : 2 * i + 2] for i in range(len(groups))]


def restore(slot_refs, incoming_ref, count):
    free = TILE - count
    width = incoming_ref.shape[1]
    for i, slot_ref in enumerate(slot_refs):
        keep = slot_ref.shape[1]
        slot = slot_ref[...]
        low = slot[count:, :]
        parts = [low[:, at : at + width - keep] for at in range(0, keep, width - keep)]
        parts.append(jnp.zeros((free, width - keep), slot.dtype))
        incoming_ref[i * TILE : (i + 1) * TILE, :keep] = slot
        incoming_ref[i * TILE : (i + 1) * TILE, keep:] = jnp.concatenate(parts, axis=0)


def grads(group, count, slope, factor_refs, before_refs, grad_refs):
    where = spread(grad_refs[0].shape[1], group, count)
    for factor_ref, before_ref, grad_ref in zip(factor_refs, before_refs, grad_refs):
        grad = (slope * factor_ref[...]).astype(jnp.bfloat16)
        placed = lax.dot_general(grad, where, (((1,), (1,)), ((), ())), preferred_element_type=jnp.float32)
        if before_ref is not None:
            placed += before_ref[...].astype(jnp.float32)
        grad_ref[...] = placed.astype(jnp.bfloat16)


def stage_kernel(group, count, first, *refs):
    slot_refs, refs = refs[: len(group)], refs[len(group) :]
    weight_ref, factor_refs, refs = refs[0], refs[1:3], refs[3:]
    before_refs, refs = ((None, None), refs) if first else (refs[:2], refs[2:])
    incoming_ref, *grad_refs = refs
    restore(slot_refs, incoming_ref, count)
    slope = lax.dot_general(
        weight_ref[...], incoming_ref[...], (((1,), (1,)), ((), ())), preferred_element_type=jnp.float32
    )
    grads(group, count, slope, factor_refs, before_refs, grad_refs)


def stage(group, count, tokens, slots, weight, factors, before):
    units, width = weight.shape
    operands = (*slots, weight, *factors, *before)
    return pl.pallas_call(
        functools.partial(stage_kernel, group, count, len(before) == 0),
        out_shape=(
            pltpu.VMEM((len(group) * TILE, width), jnp.bfloat16),
            pltpu.VMEM((units, tokens), jnp.bfloat16),
            pltpu.VMEM((units, tokens), jnp.bfloat16),
        ),
        in_specs=[WHOLE] * len(operands),
        out_specs=[WHOLE] * 3,
        compiler_params=PARAMS,
        cost_estimate=COST,
    )(*operands)


def last_kernel(slots, group, count, parts, *refs):
    slot_refs, earlier_refs, refs = refs[: len(group)], refs[len(group) : slots], refs[slots:]
    weight_ref, hidden_ref, *factor_refs = refs[:4]
    before_refs, out_refs, (newest_ref, *held_refs, sems) = refs[4:6], refs[6:9], refs[9:]
    restore(slot_refs, newest_ref, count)
    chunk = weight_ref.shape[1] // parts
    copies = []
    for i in range(parts):
        here = pl.ds(i * chunk, chunk)
        incoming = jnp.concatenate([ref[:, here] for ref in (*earlier_refs, newest_ref)], axis=0)
        down = jnp.dot(hidden_ref[...], incoming, preferred_element_type=jnp.float32)
        held_refs[0][:, here] = down.astype(jnp.bfloat16)
        copies += started(held_refs[0].at[:, here], out_refs[0].at[:, here], sems.at[2 + i], i % 2)
    slope = lax.dot_general(
        weight_ref[...], newest_ref[...], (((1,), (1,)), ((), ())), preferred_element_type=jnp.float32
    )
    grads(group, count, slope, factor_refs, before_refs, held_refs[1:])
    for i in range(2):
        copies += started(held_refs[1 + i], out_refs[1 + i], sems.at[i])
    for copy in copies:
        copy.wait()


def last(group, count, slots, earlier, weight, hidden, factors, before):
    units, width = weight.shape
    tokens = before[0].shape[1]
    parts = 4
    operands = (*slots, *earlier, weight, hidden, *factors, *before)
    shapes = [(units, width), (units, tokens), (units, tokens)]
    return pl.pallas_call(
        functools.partial(last_kernel, len(slots) + len(earlier), group, count, parts),
        out_shape=[jax.ShapeDtypeStruct(shape, jnp.bfloat16) for shape in shapes],
        in_specs=[WHOLE] * len(operands),
        out_specs=[LEFT] * 3,
        scratch_shapes=[
            pltpu.VMEM((len(group) * TILE, width), jnp.bfloat16),
            *[pltpu.VMEM(shape, jnp.bfloat16) for shape in shapes],
            pltpu.SemaphoreType.DMA((2 + parts,)),
        ],
        compiler_params=PARAMS,
        cost_estimate=COST,
    )(*operands)


def fanned(gate_codes, gate_exponents, up_codes, up_exponents, down_codes, down_exponents, grad_held):
    n = lax.axis_size("tp")
    count = grad_held.shape[1]
    p = pack(grad_held[0])
    first = [f for f in range(n) if f & (f - 1) == 0]
    straight = [*first, n - 1]
    rest = [f for f in range(n) if f not in straight]
    groups = [first, [*rest[::-1], n - 1]]
    got = {}
    for flip in reversed(straight):
        got[flip] = send(p, flip, 1)
    for flip, tied in zip(first[2:], lax.optimization_barrier([got[f] for f in first[2:]])):
        got[flip] = tied
    for flip in reversed(rest):
        got[flip] = send(got[flip - (flip & -flip if flip % 2 == 0 else 1)], flip & -flip, 0)
    weight, hidden, factors = prepare(
        groups,
        count,
        gate_codes[0].T,
        gate_exponents.transpose(2, 0, 1),
        up_codes[0].T,
        up_exponents.transpose(2, 0, 1),
        down_codes[0],
        down_exponents.transpose(1, 0, 2),
    )
    earlier, before = [], []
    for group, pair in zip(groups[:-1], factors):
        incoming, *before = stage(group, count, n * count, [got[j] for j in group], weight, pair, before)
        earlier.append(incoming)
    arrived = [got[j] for j in groups[-1]]
    down_grad, gate_grad, up_grad = last(groups[-1], count, arrived, earlier, weight, hidden, factors[-1], before)
    return down_grad[None], gate_grad.T[None], up_grad.T[None]


def dequantize(codes, exponents, target_axis):
    per = codes.shape[target_axis] // exponents.shape[target_axis]
    scales = jnp.exp2(jnp.repeat(exponents, per, axis=target_axis).astype(jnp.float32))
    return (codes.astype(jnp.float32) * scales).astype(jnp.bfloat16)


def ringed(gate_codes, gate_exponents, up_codes, up_exponents, down_codes, down_exponents, grad_held):
    gate = dequantize(gate_codes[0], gate_exponents[0], 1).astype(jnp.float32)
    up = dequantize(up_codes[0], up_exponents[0], 1).astype(jnp.float32)
    weight = dequantize(down_codes[0], down_exponents[0], 0)
    count = lax.axis_size("section")
    received = lax.ppermute(grad_held[0], "section", [(i, (i - 1) % count) for i in range(count)])
    incoming = lax.all_gather(received, "tp", axis=0, tiled=True)
    sigmoid = jax.nn.sigmoid(gate)
    silu = gate * sigmoid
    hidden = (silu * up).astype(jnp.bfloat16)
    down_grad = lax.dot_general(hidden, incoming, (((0,), (0,)), ((), ())), preferred_element_type=jnp.float32)
    slope = lax.dot_general(incoming, weight, (((1,), (1,)), ((), ())), preferred_element_type=jnp.float32)
    gate_grad = (slope * up * sigmoid * (1.0 + gate * (1.0 - sigmoid))).astype(jnp.bfloat16)
    up_grad = (slope * silu).astype(jnp.bfloat16)
    return down_grad.astype(jnp.bfloat16)[None], gate_grad[None], up_grad[None]


def body(*operands):
    n = lax.axis_size("tp")
    count, width = operands[-1].shape[1:]
    free = TILE - count
    small = n & (n - 1) == 0 and 4 <= n <= TILE
    fits = 0 < free < TILE and count % free == 0 and width * free % (TILE * 128) == 0 and width % (4 * 128) == 0
    return fanned(*operands) if small and fits else ringed(*operands)


def solution(mesh):
    wide, tall = P("section", None, "tp"), P("section", "tp", None)
    return jax.shard_map(
        body,
        mesh=mesh,
        in_specs=(wide, wide, wide, wide, tall, tall, tall),
        out_specs=(tall, wide, wide),
        check_vma=False,
    )
```

```python
import functools

import jax
import jax.numpy as jnp
from jax import lax
from jax.experimental import pallas as pl
from jax.experimental.pallas import tpu as pltpu
from jax.sharding import PartitionSpec as P

TILE = 16
WHOLE = pl.BlockSpec(memory_space=pltpu.VMEM)
LEFT = pl.BlockSpec(memory_space=pltpu.HBM)
COST = pl.CostEstimate(flops=0, bytes_accessed=16 * 1024 * 1024, transcendentals=0)
PARAMS = pltpu.CompilerParams(vmem_limit_bytes=24 * 1024 * 1024)


def send(array, flip, hop):
    sections, count = lax.axis_size("section"), lax.axis_size("tp")
    if hop == 0:
        return lax.ppermute(array, "tp", [(t, t ^ flip) for t in range(count)])
    pairs = [
        (s * count + t, ((s - hop) % sections) * count + (t ^ flip))
        for s in range(sections)
        for t in range(count)
    ]
    return lax.ppermute(array, ("section", "tp"), pairs)


def started(source_ref, target_ref, sem, priority=0):
    copy = pltpu.make_async_copy(source_ref, target_ref, sem)
    copy.start(priority=priority)
    return [copy]


def fetched(refs, held_refs, sems):
    return sum([started(ref, held, sems.at[i]) for i, (ref, held) in enumerate(zip(refs, held_refs))], [])


def pack_kernel(held_ref, packed_ref, rows_ref, sems):
    for copy in fetched([held_ref], [rows_ref], sems):
        copy.wait()
    count, width = rows_ref.shape
    free = TILE - count
    keep = width * count // TILE
    rows = rows_ref[...]
    parts = [rows[at : at + free, keep:] for at in range(0, count, free)]
    packed_ref[...] = jnp.concatenate([rows[:, :keep], jnp.concatenate(parts, axis=1)], axis=0)


def pack(rows):
    count, width = rows.shape
    return pl.pallas_call(
        pack_kernel,
        out_shape=pltpu.VMEM((TILE, width * count // TILE), jnp.bfloat16),
        in_specs=[LEFT],
        out_specs=WHOLE,
        scratch_shapes=[pltpu.VMEM(rows.shape, rows.dtype), pltpu.SemaphoreType.DMA((1,))],
        compiler_params=PARAMS,
    )(pltpu.with_memory_space_constraint(rows, pltpu.HBM))


def spread(tokens, slots, count):
    shape = (tokens, len(slots) * TILE)
    lane = lax.broadcasted_iota(jnp.int32, shape, 1)
    row = lane & (TILE - 1)
    place = lane >> (TILE.bit_length() - 1)
    slot = jnp.full(shape, slots[0], jnp.int32)
    for i in range(1, len(slots)):
        slot = jnp.where(place == i, slots[i], slot)
    token = (slot ^ lax.axis_index("tp")) * count + row
    hit = (lax.broadcasted_iota(jnp.int32, shape, 0) == token) & (row < count)
    return jnp.where(hit, 1.0, 0.0).astype(jnp.bfloat16)


def decoded(codes_ref, exponents_ref):
    blocks = exponents_ref.shape[0]
    per = codes_ref.shape[0] // blocks
    parts = []
    for b in range(blocks):
        scale = jnp.exp2(exponents_ref[b].astype(jnp.float32))
        codes = codes_ref[pl.ds(b * per, per), :].astype(jnp.float32)
        parts.append((codes * scale).astype(jnp.bfloat16))
    return jnp.concatenate(parts, axis=0)


def prepare_kernel(groups, count, *refs):
    gate_ref, gate_exp_ref, up_ref, up_exp_ref, down_ref, down_exp_ref = held = refs[-7:-1]
    copies = fetched(refs[:6], held, refs[-1])
    weight_ref, hidden_ref = refs[6:8]
    factor_refs = refs[8:-7]
    for copy in copies[:4]:
        copy.wait()
    where = spread(gate_ref.shape[1], sum(groups, []), count)
    gate = jnp.dot(decoded(gate_ref, gate_exp_ref), where, preferred_element_type=jnp.float32)
    up = jnp.dot(decoded(up_ref, up_exp_ref), where, preferred_element_type=jnp.float32)
    sigmoid = jax.nn.sigmoid(gate)
    silu = gate * sigmoid
    hidden_ref[...] = (silu * up).astype(jnp.bfloat16)
    gate_factor = up * sigmoid * (1.0 + gate * (1.0 - sigmoid))
    at = 0
    for i, group in enumerate(groups):
        lanes = slice(at, at + len(group) * TILE)
        at = lanes.stop
        factor_refs[2 * i][...] = gate_factor[:, lanes]
        factor_refs[2 * i + 1][...] = silu[:, lanes]
    for copy in copies[4:]:
        copy.wait()
    blocks = down_exp_ref.shape[0]
    per = down_ref.shape[0] // blocks
    for b in range(blocks):
        scale = jnp.exp2(down_exp_ref[b].astype(jnp.float32))
        codes = down_ref[pl.ds(b * per, per), :].astype(jnp.float32)
        weight_ref[pl.ds(b * per, per), :] = (codes * scale).astype(jnp.bfloat16)


def prepare(groups, count, *operands):
    units, width = operands[4].shape
    lanes = sum(map(len, groups)) * TILE
    factors = [pltpu.VMEM((units, len(group) * TILE), jnp.float32) for group in groups for _ in range(2)]
    weight, hidden, *factors = pl.pallas_call(
        functools.partial(prepare_kernel, groups, count),
        out_shape=(
            pltpu.VMEM((units, width), jnp.bfloat16),
            pltpu.VMEM((units, lanes), jnp.bfloat16),
            *factors,
        ),
        in_specs=[LEFT] * 6,
        out_specs=[WHOLE] * (2 + len(factors)),
        scratch_shapes=[pltpu.VMEM(operand.shape, operand.dtype) for operand in operands]
        + [pltpu.SemaphoreType.DMA((len(operands),))],
        compiler_params=PARAMS,
        cost_estimate=COST,
    )(*[pltpu.with_memory_space_constraint(operand, pltpu.HBM) for operand in operands])
    return weight, hidden, [factors[2 * i : 2 * i + 2] for i in range(len(groups))]


def restore(slot_refs, incoming_ref, count):
    free = TILE - count
    width = incoming_ref.shape[1]
    for i, slot_ref in enumerate(slot_refs):
        keep = slot_ref.shape[1]
        slot = slot_ref[...]
        low = slot[count:, :]
        parts = [low[:, at : at + width - keep] for at in range(0, keep, width - keep)]
        parts.append(jnp.zeros((free, width - keep), slot.dtype))
        incoming_ref[i * TILE : (i + 1) * TILE, :keep] = slot
        incoming_ref[i * TILE : (i + 1) * TILE, keep:] = jnp.concatenate(parts, axis=0)


def grads(group, count, slope, factor_refs, before_refs, grad_refs):
    where = spread(grad_refs[0].shape[1], group, count)
    for factor_ref, before_ref, grad_ref in zip(factor_refs, before_refs, grad_refs):
        grad = (slope * factor_ref[...]).astype(jnp.bfloat16)
        placed = lax.dot_general(grad, where, (((1,), (1,)), ((), ())), preferred_element_type=jnp.float32)
        if before_ref is not None:
            placed += before_ref[...].astype(jnp.float32)
        grad_ref[...] = placed.astype(jnp.bfloat16)


def stage_kernel(group, count, first, *refs):
    slot_refs, refs = refs[: len(group)], refs[len(group) :]
    weight_ref, factor_refs, refs = refs[0], refs[1:3], refs[3:]
    before_refs, refs = ((None, None), refs) if first else (refs[:2], refs[2:])
    incoming_ref, *grad_refs = refs
    restore(slot_refs, incoming_ref, count)
    slope = lax.dot_general(
        weight_ref[...], incoming_ref[...], (((1,), (1,)), ((), ())), preferred_element_type=jnp.float32
    )
    grads(group, count, slope, factor_refs, before_refs, grad_refs)


def stage(group, count, tokens, slots, weight, factors, before):
    units, width = weight.shape
    operands = (*slots, weight, *factors, *before)
    return pl.pallas_call(
        functools.partial(stage_kernel, group, count, len(before) == 0),
        out_shape=(
            pltpu.VMEM((len(group) * TILE, width), jnp.bfloat16),
            pltpu.VMEM((units, tokens), jnp.bfloat16),
            pltpu.VMEM((units, tokens), jnp.bfloat16),
        ),
        in_specs=[WHOLE] * len(operands),
        out_specs=[WHOLE] * 3,
        compiler_params=PARAMS,
        cost_estimate=COST,
    )(*operands)


def last_kernel(slots, group, count, parts, *refs):
    slot_refs, earlier_refs, refs = refs[: len(group)], refs[len(group) : slots], refs[slots:]
    weight_ref, hidden_ref, *factor_refs = refs[:4]
    before_refs, out_refs, (newest_ref, *held_refs, sems) = refs[4:6], refs[6:9], refs[9:]
    restore(slot_refs, newest_ref, count)
    chunk = weight_ref.shape[1] // parts
    copies = []
    for i in range(parts):
        here = pl.ds(i * chunk, chunk)
        incoming = jnp.concatenate([ref[:, here] for ref in (*earlier_refs, newest_ref)], axis=0)
        down = jnp.dot(hidden_ref[...], incoming, preferred_element_type=jnp.float32)
        held_refs[0][:, here] = down.astype(jnp.bfloat16)
        copies += started(held_refs[0].at[:, here], out_refs[0].at[:, here], sems.at[2 + i], i % 2)
    slope = lax.dot_general(
        weight_ref[...], newest_ref[...], (((1,), (1,)), ((), ())), preferred_element_type=jnp.float32
    )
    grads(group, count, slope, factor_refs, before_refs, held_refs[1:])
    for i in range(2):
        copies += started(held_refs[1 + i], out_refs[1 + i], sems.at[i])
    for copy in copies:
        copy.wait()


def last(group, count, slots, earlier, weight, hidden, factors, before):
    units, width = weight.shape
    tokens = before[0].shape[1]
    parts = 4
    operands = (*slots, *earlier, weight, hidden, *factors, *before)
    shapes = [(units, width), (units, tokens), (units, tokens)]
    return pl.pallas_call(
        functools.partial(last_kernel, len(slots) + len(earlier), group, count, parts),
        out_shape=[jax.ShapeDtypeStruct(shape, jnp.bfloat16) for shape in shapes],
        in_specs=[WHOLE] * len(operands),
        out_specs=[LEFT] * 3,
        scratch_shapes=[
            pltpu.VMEM((len(group) * TILE, width), jnp.bfloat16),
            *[pltpu.VMEM(shape, jnp.bfloat16) for shape in shapes],
            pltpu.SemaphoreType.DMA((2 + parts,)),
        ],
        compiler_params=PARAMS,
        cost_estimate=COST,
    )(*operands)


def fanned(gate_codes, gate_exponents, up_codes, up_exponents, down_codes, down_exponents, grad_held):
    n = lax.axis_size("tp")
    count = grad_held.shape[1]
    p = pack(grad_held[0])
    groups = [[f for f in range(n) if f & (f - 1) == 0 or f == 3], [f for f in range(n - 2, 4, -1) if f & (f - 1)] + [n - 1]]
    got = {}
    for flip in reversed(groups[0]):
        got[flip] = send(p, flip, 1)
    for flip in reversed(groups[1]):
        step = flip & -flip
        if flip & 1 and flip - 1 & flip - 2:
            step = flip - 1
        got[flip] = send(got[flip - step], step, 0)
    weight, hidden, factors = prepare(
        groups,
        count,
        gate_codes[0].T,
        gate_exponents.transpose(2, 0, 1),
        up_codes[0].T,
        up_exponents.transpose(2, 0, 1),
        down_codes[0],
        down_exponents.transpose(1, 0, 2),
    )
    earlier, before = [], []
    for group, pair in zip(groups[:-1], factors):
        incoming, *before = stage(group, count, n * count, [got[j] for j in group], weight, pair, before)
        earlier.append(incoming)
    arrived = [got[j] for j in groups[-1]]
    down_grad, gate_grad, up_grad = last(groups[-1], count, arrived, earlier, weight, hidden, factors[-1], before)
    return down_grad[None], gate_grad.T[None], up_grad.T[None]


def dequantize(codes, exponents, target_axis):
    per = codes.shape[target_axis] // exponents.shape[target_axis]
    scales = jnp.exp2(jnp.repeat(exponents, per, axis=target_axis).astype(jnp.float32))
    return (codes.astype(jnp.float32) * scales).astype(jnp.bfloat16)


def ringed(gate_codes, gate_exponents, up_codes, up_exponents, down_codes, down_exponents, grad_held):
    gate = dequantize(gate_codes[0], gate_exponents[0], 1).astype(jnp.float32)
    up = dequantize(up_codes[0], up_exponents[0], 1).astype(jnp.float32)
    weight = dequantize(down_codes[0], down_exponents[0], 0)
    count = lax.axis_size("section")
    received = lax.ppermute(grad_held[0], "section", [(i, (i - 1) % count) for i in range(count)])
    incoming = lax.all_gather(received, "tp", axis=0, tiled=True)
    sigmoid = jax.nn.sigmoid(gate)
    silu = gate * sigmoid
    hidden = (silu * up).astype(jnp.bfloat16)
    down_grad = lax.dot_general(hidden, incoming, (((0,), (0,)), ((), ())), preferred_element_type=jnp.float32)
    slope = lax.dot_general(incoming, weight, (((1,), (1,)), ((), ())), preferred_element_type=jnp.float32)
    gate_grad = (slope * up * sigmoid * (1.0 + gate * (1.0 - sigmoid))).astype(jnp.bfloat16)
    up_grad = (slope * silu).astype(jnp.bfloat16)
    return down_grad.astype(jnp.bfloat16)[None], gate_grad[None], up_grad[None]


def body(*operands):
    n = lax.axis_size("tp")
    count, width = operands[-1].shape[1:]
    free = TILE - count
    small = n & (n - 1) == 0 and 8 <= n <= TILE
    fits = 0 < free < TILE and count % free == 0 and width * free % (TILE * 128) == 0 and width % (4 * 128) == 0
    return fanned(*operands) if small and fits else ringed(*operands)


def solution(mesh):
    wide, tall = P("section", None, "tp"), P("section", "tp", None)
    return jax.shard_map(
        body,
        mesh=mesh,
        in_specs=(wide, wide, wide, wide, tall, tall, tall),
        out_specs=(tall, wide, wide),
        check_vma=False,
    )
```

```python
import functools

import jax
import jax.numpy as jnp
from jax import lax
from jax.experimental import pallas as pl
from jax.experimental.pallas import tpu as pltpu
from jax.sharding import PartitionSpec as P

TILE = 16
WHOLE = pl.BlockSpec(memory_space=pltpu.VMEM)
LEFT = pl.BlockSpec(memory_space=pltpu.HBM)
COST = pl.CostEstimate(flops=0, bytes_accessed=16 * 1024 * 1024, transcendentals=0)
PARAMS = pltpu.CompilerParams(vmem_limit_bytes=24 * 1024 * 1024)


def send(array, flip, hop):
    sections, count = lax.axis_size("section"), lax.axis_size("tp")
    if hop == 0:
        return lax.ppermute(array, "tp", [(t, t ^ flip) for t in range(count)])
    pairs = [
        (s * count + t, ((s - hop) % sections) * count + (t ^ flip))
        for s in range(sections)
        for t in range(count)
    ]
    return lax.ppermute(array, ("section", "tp"), pairs)


def started(source_ref, target_ref, sem, priority=0):
    copy = pltpu.make_async_copy(source_ref, target_ref, sem)
    copy.start(priority=priority)
    return [copy]


def fetched(refs, held_refs, sems):
    return sum([started(ref, held, sems.at[i]) for i, (ref, held) in enumerate(zip(refs, held_refs))], [])


def pack_kernel(held_ref, packed_ref, rows_ref, sems):
    for copy in fetched([held_ref], [rows_ref], sems):
        copy.wait()
    count, width = rows_ref.shape
    free = TILE - count
    keep = width * count // TILE
    rows = rows_ref[...]
    parts = [rows[at : at + free, keep:] for at in range(0, count, free)]
    packed_ref[...] = jnp.concatenate([rows[:, :keep], jnp.concatenate(parts, axis=1)], axis=0)


def pack(rows):
    count, width = rows.shape
    return pl.pallas_call(
        pack_kernel,
        out_shape=pltpu.VMEM((TILE, width * count // TILE), jnp.bfloat16),
        in_specs=[LEFT],
        out_specs=WHOLE,
        scratch_shapes=[pltpu.VMEM(rows.shape, rows.dtype), pltpu.SemaphoreType.DMA((1,))],
        compiler_params=PARAMS,
    )(pltpu.with_memory_space_constraint(rows, pltpu.HBM))


def spread(tokens, slots, count):
    shape = (tokens, len(slots) * TILE)
    lane = lax.broadcasted_iota(jnp.int32, shape, 1)
    row = lane & (TILE - 1)
    place = lane >> (TILE.bit_length() - 1)
    slot = jnp.full(shape, slots[0], jnp.int32)
    for i in range(1, len(slots)):
        slot = jnp.where(place == i, slots[i], slot)
    token = (slot ^ lax.axis_index("tp")) * count + row
    hit = (lax.broadcasted_iota(jnp.int32, shape, 0) == token) & (row < count)
    return jnp.where(hit, 1.0, 0.0).astype(jnp.bfloat16)


def decoded(codes_ref, exponents_ref):
    blocks = exponents_ref.shape[0]
    per = codes_ref.shape[0] // blocks
    parts = []
    for b in range(blocks):
        scale = jnp.exp2(exponents_ref[b].astype(jnp.float32))
        codes = codes_ref[pl.ds(b * per, per), :].astype(jnp.float32)
        parts.append((codes * scale).astype(jnp.bfloat16))
    return jnp.concatenate(parts, axis=0)


def prepare_kernel(groups, count, *refs):
    gate_ref, gate_exp_ref, up_ref, up_exp_ref, down_ref, down_exp_ref = held = refs[-7:-1]
    copies = fetched(refs[:6], held, refs[-1])
    weight_ref, hidden_ref = refs[6:8]
    factor_refs = refs[8:-7]
    for copy in copies[:4]:
        copy.wait()
    where = spread(gate_ref.shape[1], sum(groups, []), count)
    gate = jnp.dot(decoded(gate_ref, gate_exp_ref), where, preferred_element_type=jnp.float32)
    up = jnp.dot(decoded(up_ref, up_exp_ref), where, preferred_element_type=jnp.float32)
    sigmoid = jax.nn.sigmoid(gate)
    silu = gate * sigmoid
    hidden_ref[...] = (silu * up).astype(jnp.bfloat16)
    gate_factor = up * sigmoid * (1.0 + gate * (1.0 - sigmoid))
    at = 0
    for i, group in enumerate(groups):
        lanes = slice(at, at + len(group) * TILE)
        at = lanes.stop
        factor_refs[2 * i][...] = gate_factor[:, lanes]
        factor_refs[2 * i + 1][...] = silu[:, lanes]
    for copy in copies[4:]:
        copy.wait()
    blocks = down_exp_ref.shape[0]
    per = down_ref.shape[0] // blocks
    for b in range(blocks):
        scale = jnp.exp2(down_exp_ref[b].astype(jnp.float32))
        codes = down_ref[pl.ds(b * per, per), :].astype(jnp.float32)
        weight_ref[pl.ds(b * per, per), :] = (codes * scale).astype(jnp.bfloat16)


def prepare(groups, count, *operands):
    units, width = operands[4].shape
    lanes = sum(map(len, groups)) * TILE
    factors = [pltpu.VMEM((units, len(group) * TILE), jnp.float32) for group in groups for _ in range(2)]
    weight, hidden, *factors = pl.pallas_call(
        functools.partial(prepare_kernel, groups, count),
        out_shape=(
            pltpu.VMEM((units, width), jnp.bfloat16),
            pltpu.VMEM((units, lanes), jnp.bfloat16),
            *factors,
        ),
        in_specs=[LEFT] * 6,
        out_specs=[WHOLE] * (2 + len(factors)),
        scratch_shapes=[pltpu.VMEM(operand.shape, operand.dtype) for operand in operands]
        + [pltpu.SemaphoreType.DMA((len(operands),))],
        compiler_params=PARAMS,
        cost_estimate=COST,
    )(*[pltpu.with_memory_space_constraint(operand, pltpu.HBM) for operand in operands])
    return weight, hidden, [factors[2 * i : 2 * i + 2] for i in range(len(groups))]


def restore(slot_refs, incoming_ref, count):
    free = TILE - count
    width = incoming_ref.shape[1]
    for i, slot_ref in enumerate(slot_refs):
        keep = slot_ref.shape[1]
        slot = slot_ref[...]
        low = slot[count:, :]
        parts = [low[:, at : at + width - keep] for at in range(0, keep, width - keep)]
        parts.append(jnp.zeros((free, width - keep), slot.dtype))
        incoming_ref[i * TILE : (i + 1) * TILE, :keep] = slot
        incoming_ref[i * TILE : (i + 1) * TILE, keep:] = jnp.concatenate(parts, axis=0)


def grads(group, count, slope, factor_refs, before_refs, grad_refs):
    where = spread(grad_refs[0].shape[1], group, count)
    for factor_ref, before_ref, grad_ref in zip(factor_refs, before_refs, grad_refs):
        grad = (slope * factor_ref[...]).astype(jnp.bfloat16)
        placed = lax.dot_general(grad, where, (((1,), (1,)), ((), ())), preferred_element_type=jnp.float32)
        if before_ref is not None:
            placed += before_ref[...].astype(jnp.float32)
        grad_ref[...] = placed.astype(jnp.bfloat16)


def stage_kernel(group, count, first, *refs):
    slot_refs, refs = refs[: len(group)], refs[len(group) :]
    weight_ref, factor_refs, refs = refs[0], refs[1:3], refs[3:]
    before_refs, refs = ((None, None), refs) if first else (refs[:2], refs[2:])
    incoming_ref, *grad_refs = refs
    restore(slot_refs, incoming_ref, count)
    slope = lax.dot_general(
        weight_ref[...], incoming_ref[...], (((1,), (1,)), ((), ())), preferred_element_type=jnp.float32
    )
    grads(group, count, slope, factor_refs, before_refs, grad_refs)


def stage(group, count, tokens, slots, weight, factors, before):
    units, width = weight.shape
    operands = (*slots, weight, *factors, *before)
    return pl.pallas_call(
        functools.partial(stage_kernel, group, count, len(before) == 0),
        out_shape=(
            pltpu.VMEM((len(group) * TILE, width), jnp.bfloat16),
            pltpu.VMEM((units, tokens), jnp.bfloat16),
            pltpu.VMEM((units, tokens), jnp.bfloat16),
        ),
        in_specs=[WHOLE] * len(operands),
        out_specs=[WHOLE] * 3,
        compiler_params=PARAMS,
        cost_estimate=COST,
    )(*operands)


def last_kernel(slots, group, count, parts, *refs):
    slot_refs, earlier_refs, refs = refs[: len(group)], refs[len(group) : slots], refs[slots:]
    weight_ref, hidden_ref, *factor_refs = refs[:4]
    before_refs, out_refs, (newest_ref, *held_refs, sems) = refs[4:6], refs[6:9], refs[9:]
    restore(slot_refs, newest_ref, count)
    chunk = weight_ref.shape[1] // parts
    copies = []
    for i in range(parts):
        here = pl.ds(i * chunk, chunk)
        incoming = jnp.concatenate([ref[:, here] for ref in (*earlier_refs, newest_ref)], axis=0)
        down = jnp.dot(hidden_ref[...], incoming, preferred_element_type=jnp.float32)
        held_refs[0][:, here] = down.astype(jnp.bfloat16)
        copies += started(held_refs[0].at[:, here], out_refs[0].at[:, here], sems.at[2 + i], i % 2)
    slope = lax.dot_general(
        weight_ref[...], newest_ref[...], (((1,), (1,)), ((), ())), preferred_element_type=jnp.float32
    )
    grads(group, count, slope, factor_refs, before_refs, held_refs[1:])
    for i in range(2):
        copies += started(held_refs[1 + i], out_refs[1 + i], sems.at[i])
    for copy in copies:
        copy.wait()


def last(group, count, slots, earlier, weight, hidden, factors, before):
    units, width = weight.shape
    tokens = before[0].shape[1]
    parts = 4
    operands = (*slots, *earlier, weight, hidden, *factors, *before)
    shapes = [(units, width), (units, tokens), (units, tokens)]
    return pl.pallas_call(
        functools.partial(last_kernel, len(slots) + len(earlier), group, count, parts),
        out_shape=[jax.ShapeDtypeStruct(shape, jnp.bfloat16) for shape in shapes],
        in_specs=[WHOLE] * len(operands),
        out_specs=[LEFT] * 3,
        scratch_shapes=[
            pltpu.VMEM((len(group) * TILE, width), jnp.bfloat16),
            *[pltpu.VMEM(shape, jnp.bfloat16) for shape in shapes],
            pltpu.SemaphoreType.DMA((2 + parts,)),
        ],
        compiler_params=PARAMS,
        cost_estimate=COST,
    )(*operands)


def fanned(gate_codes, gate_exponents, up_codes, up_exponents, down_codes, down_exponents, grad_held):
    n = lax.axis_size("tp")
    count = grad_held.shape[1]
    p = pack(grad_held[0])
    groups = [[f for f in range(1, n // 2) if f & (f - 1) == 0 or f == 3] + [0, n // 2], [f for f in range(5, n) if f & (f - 1)]]
    got = {}
    for flip in reversed(groups[0]):
        got[flip] = send(p, flip, 1)
    for flip in reversed(groups[1]):
        step = flip & -flip
        if flip & 1 and flip - 1 & flip - 2:
            step = flip - 1
        got[flip] = send(got[flip - step], step, 0)
    weight, hidden, factors = prepare(
        groups,
        count,
        gate_codes[0].T,
        gate_exponents.transpose(2, 0, 1),
        up_codes[0].T,
        up_exponents.transpose(2, 0, 1),
        down_codes[0],
        down_exponents.transpose(1, 0, 2),
    )
    earlier, before = [], []
    for group, pair in zip(groups[:-1], factors):
        incoming, *before = stage(group, count, n * count, [got[j] for j in group], weight, pair, before)
        earlier.append(incoming)
    arrived = [got[j] for j in groups[-1]]
    down_grad, gate_grad, up_grad = last(groups[-1], count, arrived, earlier, weight, hidden, factors[-1], before)
    return down_grad[None], gate_grad.T[None], up_grad.T[None]


def dequantize(codes, exponents, target_axis):
    per = codes.shape[target_axis] // exponents.shape[target_axis]
    scales = jnp.exp2(jnp.repeat(exponents, per, axis=target_axis).astype(jnp.float32))
    return (codes.astype(jnp.float32) * scales).astype(jnp.bfloat16)


def ringed(gate_codes, gate_exponents, up_codes, up_exponents, down_codes, down_exponents, grad_held):
    gate = dequantize(gate_codes[0], gate_exponents[0], 1).astype(jnp.float32)
    up = dequantize(up_codes[0], up_exponents[0], 1).astype(jnp.float32)
    weight = dequantize(down_codes[0], down_exponents[0], 0)
    count = lax.axis_size("section")
    received = lax.ppermute(grad_held[0], "section", [(i, (i - 1) % count) for i in range(count)])
    incoming = lax.all_gather(received, "tp", axis=0, tiled=True)
    sigmoid = jax.nn.sigmoid(gate)
    silu = gate * sigmoid
    hidden = (silu * up).astype(jnp.bfloat16)
    down_grad = lax.dot_general(hidden, incoming, (((0,), (0,)), ((), ())), preferred_element_type=jnp.float32)
    slope = lax.dot_general(incoming, weight, (((1,), (1,)), ((), ())), preferred_element_type=jnp.float32)
    gate_grad = (slope * up * sigmoid * (1.0 + gate * (1.0 - sigmoid))).astype(jnp.bfloat16)
    up_grad = (slope * silu).astype(jnp.bfloat16)
    return down_grad.astype(jnp.bfloat16)[None], gate_grad[None], up_grad[None]


def body(*operands):
    n = lax.axis_size("tp")
    count, width = operands[-1].shape[1:]
    free = TILE - count
    small = n & (n - 1) == 0 and 8 <= n <= TILE
    fits = 0 < free < TILE and count % free == 0 and width * free % (TILE * 128) == 0 and width % (4 * 128) == 0
    return fanned(*operands) if small and fits else ringed(*operands)


def solution(mesh):
    wide, tall = P("section", None, "tp"), P("section", "tp", None)
    return jax.shard_map(
        body,
        mesh=mesh,
        in_specs=(wide, wide, wide, wide, tall, tall, tall),
        out_specs=(tall, wide, wide),
        check_vma=False,
    )
```

```python
import functools

import jax
import jax.numpy as jnp
from jax import lax
from jax.experimental import pallas as pl
from jax.experimental.pallas import tpu as pltpu
from jax.sharding import PartitionSpec as P

TILE = 16
WHOLE = pl.BlockSpec(memory_space=pltpu.VMEM)
LEFT = pl.BlockSpec(memory_space=pltpu.HBM)
COST = pl.CostEstimate(flops=0, bytes_accessed=16 * 1024 * 1024, transcendentals=0)
PARAMS = pltpu.CompilerParams(vmem_limit_bytes=24 * 1024 * 1024)


def send(array, flip, hop):
    sections, count = lax.axis_size("section"), lax.axis_size("tp")
    if hop == 0:
        return lax.ppermute(array, "tp", [(t, t ^ flip) for t in range(count)])
    pairs = [
        (s * count + t, ((s - hop) % sections) * count + (t ^ flip))
        for s in range(sections)
        for t in range(count)
    ]
    return lax.ppermute(array, ("section", "tp"), pairs)


def started(source_ref, target_ref, sem, priority=0):
    copy = pltpu.make_async_copy(source_ref, target_ref, sem)
    copy.start(priority=priority)
    return [copy]


def fetched(refs, held_refs, sems):
    return sum([started(ref, held, sems.at[i]) for i, (ref, held) in enumerate(zip(refs, held_refs))], [])


def pack_kernel(held_ref, packed_ref, rows_ref, sems):
    for copy in fetched([held_ref], [rows_ref], sems):
        copy.wait()
    count, width = rows_ref.shape
    free = TILE - count
    keep = width * count // TILE
    rows = rows_ref[...]
    parts = [rows[at : at + free, keep:] for at in range(0, count, free)]
    packed_ref[...] = jnp.concatenate([rows[:, :keep], jnp.concatenate(parts, axis=1)], axis=0)


def pack(rows):
    count, width = rows.shape
    return pl.pallas_call(
        pack_kernel,
        out_shape=pltpu.VMEM((TILE, width * count // TILE), jnp.bfloat16),
        in_specs=[LEFT],
        out_specs=WHOLE,
        scratch_shapes=[pltpu.VMEM(rows.shape, rows.dtype), pltpu.SemaphoreType.DMA((1,))],
        compiler_params=PARAMS,
    )(pltpu.with_memory_space_constraint(rows, pltpu.HBM))


def spread(tokens, slots, count):
    shape = (tokens, len(slots) * TILE)
    lane = lax.broadcasted_iota(jnp.int32, shape, 1)
    row = lane & (TILE - 1)
    place = lane >> (TILE.bit_length() - 1)
    slot = jnp.full(shape, slots[0], jnp.int32)
    for i in range(1, len(slots)):
        slot = jnp.where(place == i, slots[i], slot)
    token = (slot ^ lax.axis_index("tp")) * count + row
    hit = (lax.broadcasted_iota(jnp.int32, shape, 0) == token) & (row < count)
    return jnp.where(hit, 1.0, 0.0).astype(jnp.bfloat16)


def decoded(codes_ref, exponents_ref):
    blocks = exponents_ref.shape[0]
    per = codes_ref.shape[0] // blocks
    parts = []
    for b in range(blocks):
        scale = jnp.exp2(exponents_ref[b].astype(jnp.float32))
        codes = codes_ref[pl.ds(b * per, per), :].astype(jnp.float32)
        parts.append((codes * scale).astype(jnp.bfloat16))
    return jnp.concatenate(parts, axis=0)


def prepare_kernel(groups, count, *refs):
    gate_ref, gate_exp_ref, up_ref, up_exp_ref, down_ref, down_exp_ref = held = refs[-7:-1]
    copies = fetched(refs[:6], held, refs[-1])
    weight_ref, hidden_ref = refs[6:8]
    factor_refs = refs[8:-7]
    for copy in copies[:4]:
        copy.wait()
    where = spread(gate_ref.shape[1], sum(groups, []), count)
    gate = jnp.dot(decoded(gate_ref, gate_exp_ref), where, preferred_element_type=jnp.float32)
    up = jnp.dot(decoded(up_ref, up_exp_ref), where, preferred_element_type=jnp.float32)
    sigmoid = jax.nn.sigmoid(gate)
    silu = gate * sigmoid
    hidden_ref[...] = (silu * up).astype(jnp.bfloat16)
    gate_factor = up * sigmoid * (1.0 + gate * (1.0 - sigmoid))
    at = 0
    for i, group in enumerate(groups):
        lanes = slice(at, at + len(group) * TILE)
        at = lanes.stop
        factor_refs[2 * i][...] = gate_factor[:, lanes]
        factor_refs[2 * i + 1][...] = silu[:, lanes]
    for copy in copies[4:]:
        copy.wait()
    blocks = down_exp_ref.shape[0]
    per = down_ref.shape[0] // blocks
    for b in range(blocks):
        scale = jnp.exp2(down_exp_ref[b].astype(jnp.float32))
        codes = down_ref[pl.ds(b * per, per), :].astype(jnp.float32)
        weight_ref[pl.ds(b * per, per), :] = (codes * scale).astype(jnp.bfloat16)


def prepare(groups, count, *operands):
    units, width = operands[4].shape
    lanes = sum(map(len, groups)) * TILE
    factors = [pltpu.VMEM((units, len(group) * TILE), jnp.float32) for group in groups for _ in range(2)]
    weight, hidden, *factors = pl.pallas_call(
        functools.partial(prepare_kernel, groups, count),
        out_shape=(
            pltpu.VMEM((units, width), jnp.bfloat16),
            pltpu.VMEM((units, lanes), jnp.bfloat16),
            *factors,
        ),
        in_specs=[LEFT] * 6,
        out_specs=[WHOLE] * (2 + len(factors)),
        scratch_shapes=[pltpu.VMEM(operand.shape, operand.dtype) for operand in operands]
        + [pltpu.SemaphoreType.DMA((len(operands),))],
        compiler_params=PARAMS,
        cost_estimate=COST,
    )(*[pltpu.with_memory_space_constraint(operand, pltpu.HBM) for operand in operands])
    return weight, hidden, [factors[2 * i : 2 * i + 2] for i in range(len(groups))]


def restore(slot_refs, incoming_ref, count):
    free = TILE - count
    width = incoming_ref.shape[1]
    for i, slot_ref in enumerate(slot_refs):
        keep = slot_ref.shape[1]
        slot = slot_ref[...]
        low = slot[count:, :]
        parts = [low[:, at : at + width - keep] for at in range(0, keep, width - keep)]
        parts.append(jnp.zeros((free, width - keep), slot.dtype))
        incoming_ref[i * TILE : (i + 1) * TILE, :keep] = slot
        incoming_ref[i * TILE : (i + 1) * TILE, keep:] = jnp.concatenate(parts, axis=0)


def grads(group, count, slope, factor_refs, before_refs, grad_refs):
    where = spread(grad_refs[0].shape[1], group, count)
    for factor_ref, before_ref, grad_ref in zip(factor_refs, before_refs, grad_refs):
        grad = (slope * factor_ref[...]).astype(jnp.bfloat16)
        placed = lax.dot_general(grad, where, (((1,), (1,)), ((), ())), preferred_element_type=jnp.float32)
        if before_ref is not None:
            placed += before_ref[...].astype(jnp.float32)
        grad_ref[...] = placed.astype(jnp.bfloat16)


def stage_kernel(group, count, first, *refs):
    slot_refs, refs = refs[: len(group)], refs[len(group) :]
    weight_ref, factor_refs, refs = refs[0], refs[1:3], refs[3:]
    before_refs, refs = ((None, None), refs) if first else (refs[:2], refs[2:])
    incoming_ref, *grad_refs = refs
    restore(slot_refs, incoming_ref, count)
    slope = lax.dot_general(
        weight_ref[...], incoming_ref[...], (((1,), (1,)), ((), ())), preferred_element_type=jnp.float32
    )
    grads(group, count, slope, factor_refs, before_refs, grad_refs)


def stage(group, count, tokens, slots, weight, factors, before):
    units, width = weight.shape
    operands = (*slots, weight, *factors, *before)
    return pl.pallas_call(
        functools.partial(stage_kernel, group, count, len(before) == 0),
        out_shape=(
            pltpu.VMEM((len(group) * TILE, width), jnp.bfloat16),
            pltpu.VMEM((units, tokens), jnp.bfloat16),
            pltpu.VMEM((units, tokens), jnp.bfloat16),
        ),
        in_specs=[WHOLE] * len(operands),
        out_specs=[WHOLE] * 3,
        compiler_params=PARAMS,
        cost_estimate=COST,
    )(*operands)


def last_kernel(slots, group, count, parts, *refs):
    slot_refs, earlier_refs, refs = refs[: len(group)], refs[len(group) : slots], refs[slots:]
    weight_ref, hidden_ref, *factor_refs = refs[:4]
    before_refs, out_refs, (newest_ref, *held_refs, sems) = refs[4:6], refs[6:9], refs[9:]
    restore(slot_refs, newest_ref, count)
    chunk = weight_ref.shape[1] // parts
    copies = []
    for i in range(parts):
        here = pl.ds(i * chunk, chunk)
        incoming = jnp.concatenate([ref[:, here] for ref in (*earlier_refs, newest_ref)], axis=0)
        down = jnp.dot(hidden_ref[...], incoming, preferred_element_type=jnp.float32)
        held_refs[0][:, here] = down.astype(jnp.bfloat16)
        copies += started(held_refs[0].at[:, here], out_refs[0].at[:, here], sems.at[2 + i], i % 2)
    slope = lax.dot_general(
        weight_ref[...], newest_ref[...], (((1,), (1,)), ((), ())), preferred_element_type=jnp.float32
    )
    grads(group, count, slope, factor_refs, before_refs, held_refs[1:])
    for i in range(2):
        copies += started(held_refs[1 + i], out_refs[1 + i], sems.at[i])
    for copy in copies:
        copy.wait()


def last(group, count, slots, earlier, weight, hidden, factors, before):
    units, width = weight.shape
    tokens = before[0].shape[1]
    parts = 4
    operands = (*slots, *earlier, weight, hidden, *factors, *before)
    shapes = [(units, width), (units, tokens), (units, tokens)]
    return pl.pallas_call(
        functools.partial(last_kernel, len(slots) + len(earlier), group, count, parts),
        out_shape=[jax.ShapeDtypeStruct(shape, jnp.bfloat16) for shape in shapes],
        in_specs=[WHOLE] * len(operands),
        out_specs=[LEFT] * 3,
        scratch_shapes=[
            pltpu.VMEM((len(group) * TILE, width), jnp.bfloat16),
            *[pltpu.VMEM(shape, jnp.bfloat16) for shape in shapes],
            pltpu.SemaphoreType.DMA((2 + parts,)),
        ],
        compiler_params=PARAMS,
        cost_estimate=COST,
    )(*operands)


def fanned(gate_codes, gate_exponents, up_codes, up_exponents, down_codes, down_exponents, grad_held):
    n = lax.axis_size("tp")
    count = grad_held.shape[1]
    p = pack(grad_held[0])
    first = [f for f in range(n) if f & (f - 1) == 0]
    rest = [f for f in range(n) if f not in first]
    late = [f for f in rest if f - n // 2 in first]
    groups = [first, [f for f in rest[:-1] if f not in late] + late[::-1] + rest[-1:]]
    got = {}
    for flip in reversed(first):
        got[flip] = send(p, flip, 1)
    for flip in reversed(rest):
        step = flip & -flip
        if flip & 1 and flip - 1 not in first:
            step = flip - 1
        got[flip] = send(got[flip - step], step, 0)
    weight, hidden, factors = prepare(
        groups,
        count,
        gate_codes[0].T,
        gate_exponents.transpose(2, 0, 1),
        up_codes[0].T,
        up_exponents.transpose(2, 0, 1),
        down_codes[0],
        down_exponents.transpose(1, 0, 2),
    )
    earlier, before = [], []
    for group, pair in zip(groups[:-1], factors):
        incoming, *before = stage(group, count, n * count, [got[j] for j in group], weight, pair, before)
        earlier.append(incoming)
    arrived = [got[j] for j in groups[-1]]
    down_grad, gate_grad, up_grad = last(groups[-1], count, arrived, earlier, weight, hidden, factors[-1], before)
    return down_grad[None], gate_grad.T[None], up_grad.T[None]


def dequantize(codes, exponents, target_axis):
    per = codes.shape[target_axis] // exponents.shape[target_axis]
    scales = jnp.exp2(jnp.repeat(exponents, per, axis=target_axis).astype(jnp.float32))
    return (codes.astype(jnp.float32) * scales).astype(jnp.bfloat16)


def ringed(gate_codes, gate_exponents, up_codes, up_exponents, down_codes, down_exponents, grad_held):
    gate = dequantize(gate_codes[0], gate_exponents[0], 1).astype(jnp.float32)
    up = dequantize(up_codes[0], up_exponents[0], 1).astype(jnp.float32)
    weight = dequantize(down_codes[0], down_exponents[0], 0)
    count = lax.axis_size("section")
    received = lax.ppermute(grad_held[0], "section", [(i, (i - 1) % count) for i in range(count)])
    incoming = lax.all_gather(received, "tp", axis=0, tiled=True)
    sigmoid = jax.nn.sigmoid(gate)
    silu = gate * sigmoid
    hidden = (silu * up).astype(jnp.bfloat16)
    down_grad = lax.dot_general(hidden, incoming, (((0,), (0,)), ((), ())), preferred_element_type=jnp.float32)
    slope = lax.dot_general(incoming, weight, (((1,), (1,)), ((), ())), preferred_element_type=jnp.float32)
    gate_grad = (slope * up * sigmoid * (1.0 + gate * (1.0 - sigmoid))).astype(jnp.bfloat16)
    up_grad = (slope * silu).astype(jnp.bfloat16)
    return down_grad.astype(jnp.bfloat16)[None], gate_grad[None], up_grad[None]


def body(*operands):
    n = lax.axis_size("tp")
    count, width = operands[-1].shape[1:]
    free = TILE - count
    small = n & (n - 1) == 0 and 4 <= n <= TILE
    fits = 0 < free < TILE and count % free == 0 and width * free % (TILE * 128) == 0 and width % (4 * 128) == 0
    return fanned(*operands) if small and fits else ringed(*operands)


def solution(mesh):
    wide, tall = P("section", None, "tp"), P("section", "tp", None)
    return jax.shard_map(
        body,
        mesh=mesh,
        in_specs=(wide, wide, wide, wide, tall, tall, tall),
        out_specs=(tall, wide, wide),
        check_vma=False,
    )
```

```python
import functools

import jax
import jax.numpy as jnp
from jax import lax
from jax.experimental import pallas as pl
from jax.experimental.pallas import tpu as pltpu
from jax.sharding import PartitionSpec as P

TILE = 16
WHOLE = pl.BlockSpec(memory_space=pltpu.VMEM)
LEFT = pl.BlockSpec(memory_space=pltpu.HBM)
COST = pl.CostEstimate(flops=0, bytes_accessed=16 * 1024 * 1024, transcendentals=0)
PARAMS = pltpu.CompilerParams(vmem_limit_bytes=24 * 1024 * 1024)


def send(array, flip, hop):
    sections, count = lax.axis_size("section"), lax.axis_size("tp")
    if hop == 0:
        return lax.ppermute(array, "tp", [(t, t ^ flip) for t in range(count)])
    pairs = [
        (s * count + t, ((s - hop) % sections) * count + (t ^ flip))
        for s in range(sections)
        for t in range(count)
    ]
    return lax.ppermute(array, ("section", "tp"), pairs)


def started(source_ref, target_ref, sem, priority=0):
    copy = pltpu.make_async_copy(source_ref, target_ref, sem)
    copy.start(priority=priority)
    return [copy]


def fetched(refs, held_refs, sems):
    return sum([started(ref, held, sems.at[i]) for i, (ref, held) in enumerate(zip(refs, held_refs))], [])


def pack_kernel(held_ref, packed_ref, rows_ref, sems):
    for copy in fetched([held_ref], [rows_ref], sems):
        copy.wait()
    count, width = rows_ref.shape
    free = TILE - count
    keep = width * count // TILE
    rows = rows_ref[...]
    parts = [rows[at : at + free, keep:] for at in range(0, count, free)]
    packed_ref[...] = jnp.concatenate([rows[:, :keep], jnp.concatenate(parts, axis=1)], axis=0)


def pack(rows):
    count, width = rows.shape
    return pl.pallas_call(
        pack_kernel,
        out_shape=pltpu.VMEM((TILE, width * count // TILE), jnp.bfloat16),
        in_specs=[LEFT],
        out_specs=WHOLE,
        scratch_shapes=[pltpu.VMEM(rows.shape, rows.dtype), pltpu.SemaphoreType.DMA((1,))],
        compiler_params=PARAMS,
    )(pltpu.with_memory_space_constraint(rows, pltpu.HBM))


def spread(tokens, slots, count):
    shape = (tokens, len(slots) * TILE)
    lane = lax.broadcasted_iota(jnp.int32, shape, 1)
    row = lane & (TILE - 1)
    place = lane >> (TILE.bit_length() - 1)
    slot = jnp.full(shape, slots[0], jnp.int32)
    for i in range(1, len(slots)):
        slot = jnp.where(place == i, slots[i], slot)
    token = (slot ^ lax.axis_index("tp")) * count + row
    hit = (lax.broadcasted_iota(jnp.int32, shape, 0) == token) & (row < count)
    return jnp.where(hit, 1.0, 0.0).astype(jnp.bfloat16)


def decoded(codes_ref, exponents_ref):
    blocks = exponents_ref.shape[0]
    per = codes_ref.shape[0] // blocks
    parts = []
    for b in range(blocks):
        scale = jnp.exp2(exponents_ref[b].astype(jnp.float32))
        codes = codes_ref[pl.ds(b * per, per), :].astype(jnp.float32)
        parts.append((codes * scale).astype(jnp.bfloat16))
    return jnp.concatenate(parts, axis=0)


def prepare_kernel(groups, count, *refs):
    gate_ref, gate_exp_ref, up_ref, up_exp_ref, down_ref, down_exp_ref = held = refs[-7:-1]
    copies = fetched(refs[:6], held, refs[-1])
    weight_ref, hidden_ref = refs[6:8]
    factor_refs = refs[8:-7]
    for copy in copies[:4]:
        copy.wait()
    where = spread(gate_ref.shape[1], sum(groups, []), count)
    gate = jnp.dot(decoded(gate_ref, gate_exp_ref), where, preferred_element_type=jnp.float32)
    up = jnp.dot(decoded(up_ref, up_exp_ref), where, preferred_element_type=jnp.float32)
    sigmoid = jax.nn.sigmoid(gate)
    silu = gate * sigmoid
    hidden_ref[...] = (silu * up).astype(jnp.bfloat16)
    gate_factor = up * sigmoid * (1.0 + gate * (1.0 - sigmoid))
    at = 0
    for i, group in enumerate(groups):
        lanes = slice(at, at + len(group) * TILE)
        at = lanes.stop
        factor_refs[2 * i][...] = gate_factor[:, lanes]
        factor_refs[2 * i + 1][...] = silu[:, lanes]
    for copy in copies[4:]:
        copy.wait()
    blocks = down_exp_ref.shape[0]
    per = down_ref.shape[0] // blocks
    for b in range(blocks):
        scale = jnp.exp2(down_exp_ref[b].astype(jnp.float32))
        codes = down_ref[pl.ds(b * per, per), :].astype(jnp.float32)
        weight_ref[pl.ds(b * per, per), :] = (codes * scale).astype(jnp.bfloat16)


def prepare(groups, count, *operands):
    units, width = operands[4].shape
    lanes = sum(map(len, groups)) * TILE
    factors = [pltpu.VMEM((units, len(group) * TILE), jnp.float32) for group in groups for _ in range(2)]
    weight, hidden, *factors = pl.pallas_call(
        functools.partial(prepare_kernel, groups, count),
        out_shape=(
            pltpu.VMEM((units, width), jnp.bfloat16),
            pltpu.VMEM((units, lanes), jnp.bfloat16),
            *factors,
        ),
        in_specs=[LEFT] * 6,
        out_specs=[WHOLE] * (2 + len(factors)),
        scratch_shapes=[pltpu.VMEM(operand.shape, operand.dtype) for operand in operands]
        + [pltpu.SemaphoreType.DMA((len(operands),))],
        compiler_params=PARAMS,
        cost_estimate=COST,
    )(*[pltpu.with_memory_space_constraint(operand, pltpu.HBM) for operand in operands])
    return weight, hidden, [factors[2 * i : 2 * i + 2] for i in range(len(groups))]


def restore(slot_refs, incoming_ref, count):
    free = TILE - count
    width = incoming_ref.shape[1]
    for i, slot_ref in enumerate(slot_refs):
        keep = slot_ref.shape[1]
        slot = slot_ref[...]
        low = slot[count:, :]
        parts = [low[:, at : at + width - keep] for at in range(0, keep, width - keep)]
        parts.append(jnp.zeros((free, width - keep), slot.dtype))
        incoming_ref[i * TILE : (i + 1) * TILE, :keep] = slot
        incoming_ref[i * TILE : (i + 1) * TILE, keep:] = jnp.concatenate(parts, axis=0)


def grads(group, count, slope, factor_refs, before_refs, grad_refs):
    where = spread(grad_refs[0].shape[1], group, count)
    for factor_ref, before_ref, grad_ref in zip(factor_refs, before_refs, grad_refs):
        grad = (slope * factor_ref[...]).astype(jnp.bfloat16)
        placed = lax.dot_general(grad, where, (((1,), (1,)), ((), ())), preferred_element_type=jnp.float32)
        if before_ref is not None:
            placed += before_ref[...].astype(jnp.float32)
        grad_ref[...] = placed.astype(jnp.bfloat16)


def stage_kernel(group, count, first, *refs):
    slot_refs, refs = refs[: len(group)], refs[len(group) :]
    weight_ref, factor_refs, refs = refs[0], refs[1:3], refs[3:]
    before_refs, refs = ((None, None), refs) if first else (refs[:2], refs[2:])
    incoming_ref, *grad_refs = refs
    restore(slot_refs, incoming_ref, count)
    slope = lax.dot_general(
        weight_ref[...], incoming_ref[...], (((1,), (1,)), ((), ())), preferred_element_type=jnp.float32
    )
    grads(group, count, slope, factor_refs, before_refs, grad_refs)


def stage(group, count, tokens, slots, weight, factors, before):
    units, width = weight.shape
    operands = (*slots, weight, *factors, *before)
    return pl.pallas_call(
        functools.partial(stage_kernel, group, count, len(before) == 0),
        out_shape=(
            pltpu.VMEM((len(group) * TILE, width), jnp.bfloat16),
            pltpu.VMEM((units, tokens), jnp.bfloat16),
            pltpu.VMEM((units, tokens), jnp.bfloat16),
        ),
        in_specs=[WHOLE] * len(operands),
        out_specs=[WHOLE] * 3,
        compiler_params=PARAMS,
        cost_estimate=COST,
    )(*operands)


def last_kernel(slots, group, count, parts, *refs):
    slot_refs, earlier_refs, refs = refs[: len(group)], refs[len(group) : slots], refs[slots:]
    weight_ref, hidden_ref, *factor_refs = refs[:4]
    before_refs, out_refs, (newest_ref, *held_refs, sems) = refs[4:6], refs[6:9], refs[9:]
    restore(slot_refs, newest_ref, count)
    chunk = weight_ref.shape[1] // parts
    copies = []
    for i in range(parts):
        here = pl.ds(i * chunk, chunk)
        incoming = jnp.concatenate([ref[:, here] for ref in (*earlier_refs, newest_ref)], axis=0)
        down = jnp.dot(hidden_ref[...], incoming, preferred_element_type=jnp.float32)
        held_refs[0][:, here] = down.astype(jnp.bfloat16)
        copies += started(held_refs[0].at[:, here], out_refs[0].at[:, here], sems.at[2 + i], i % 2)
    slope = lax.dot_general(
        weight_ref[...], newest_ref[...], (((1,), (1,)), ((), ())), preferred_element_type=jnp.float32
    )
    grads(group, count, slope, factor_refs, before_refs, held_refs[1:])
    for i in range(2):
        copies += started(held_refs[1 + i], out_refs[1 + i], sems.at[i])
    for copy in copies:
        copy.wait()


def last(group, count, slots, earlier, weight, hidden, factors, before):
    units, width = weight.shape
    tokens = before[0].shape[1]
    parts = 4
    operands = (*slots, *earlier, weight, hidden, *factors, *before)
    shapes = [(units, width), (units, tokens), (units, tokens)]
    return pl.pallas_call(
        functools.partial(last_kernel, len(slots) + len(earlier), group, count, parts),
        out_shape=[jax.ShapeDtypeStruct(shape, jnp.bfloat16) for shape in shapes],
        in_specs=[WHOLE] * len(operands),
        out_specs=[LEFT] * 3,
        scratch_shapes=[
            pltpu.VMEM((len(group) * TILE, width), jnp.bfloat16),
            *[pltpu.VMEM(shape, jnp.bfloat16) for shape in shapes],
            pltpu.SemaphoreType.DMA((2 + parts,)),
        ],
        compiler_params=PARAMS,
        cost_estimate=COST,
    )(*operands)


def fanned(gate_codes, gate_exponents, up_codes, up_exponents, down_codes, down_exponents, grad_held):
    n = lax.axis_size("tp")
    count = grad_held.shape[1]
    p = pack(grad_held[0])
    first = [f for f in range(n) if f & (f - 1) == 0]
    rest = [f for f in range(n) if f not in first]
    late = [f for f in rest[:-1] if f - n // 2 in first]
    groups = [first, [n - 1], [f for f in rest[:-1] if f not in late] + late[::-1]]
    got = {}
    for flip in reversed(first):
        got[flip] = send(p, flip, 1)
    weight, hidden, factors = prepare(
        groups,
        count,
        gate_codes[0].T,
        gate_exponents.transpose(2, 0, 1),
        up_codes[0].T,
        up_exponents.transpose(2, 0, 1),
        down_codes[0],
        down_exponents.transpose(1, 0, 2),
    )
    got[1], _ = lax.optimization_barrier((got[1], hidden))
    for flip in reversed(rest):
        step = flip & -flip
        if flip & 1 and flip - 1 not in first:
            step = flip - 1
        got[flip] = send(got[flip - step], step, 0)
    earlier, before = [], []
    for group, pair in zip(groups[:-1], factors):
        incoming, *before = stage(group, count, n * count, [got[j] for j in group], weight, pair, before)
        earlier.append(incoming)
    arrived = [got[j] for j in groups[-1]]
    down_grad, gate_grad, up_grad = last(groups[-1], count, arrived, earlier, weight, hidden, factors[-1], before)
    return down_grad[None], gate_grad.T[None], up_grad.T[None]


def dequantize(codes, exponents, target_axis):
    per = codes.shape[target_axis] // exponents.shape[target_axis]
    scales = jnp.exp2(jnp.repeat(exponents, per, axis=target_axis).astype(jnp.float32))
    return (codes.astype(jnp.float32) * scales).astype(jnp.bfloat16)


def ringed(gate_codes, gate_exponents, up_codes, up_exponents, down_codes, down_exponents, grad_held):
    gate = dequantize(gate_codes[0], gate_exponents[0], 1).astype(jnp.float32)
    up = dequantize(up_codes[0], up_exponents[0], 1).astype(jnp.float32)
    weight = dequantize(down_codes[0], down_exponents[0], 0)
    count = lax.axis_size("section")
    received = lax.ppermute(grad_held[0], "section", [(i, (i - 1) % count) for i in range(count)])
    incoming = lax.all_gather(received, "tp", axis=0, tiled=True)
    sigmoid = jax.nn.sigmoid(gate)
    silu = gate * sigmoid
    hidden = (silu * up).astype(jnp.bfloat16)
    down_grad = lax.dot_general(hidden, incoming, (((0,), (0,)), ((), ())), preferred_element_type=jnp.float32)
    slope = lax.dot_general(incoming, weight, (((1,), (1,)), ((), ())), preferred_element_type=jnp.float32)
    gate_grad = (slope * up * sigmoid * (1.0 + gate * (1.0 - sigmoid))).astype(jnp.bfloat16)
    up_grad = (slope * silu).astype(jnp.bfloat16)
    return down_grad.astype(jnp.bfloat16)[None], gate_grad[None], up_grad[None]


def body(*operands):
    n = lax.axis_size("tp")
    count, width = operands[-1].shape[1:]
    free = TILE - count
    small = n & (n - 1) == 0 and 8 <= n <= TILE
    fits = 0 < free < TILE and count % free == 0 and width * free % (TILE * 128) == 0 and width % (4 * 128) == 0
    return fanned(*operands) if small and fits else ringed(*operands)


def solution(mesh):
    wide, tall = P("section", None, "tp"), P("section", "tp", None)
    return jax.shard_map(
        body,
        mesh=mesh,
        in_specs=(wide, wide, wide, wide, tall, tall, tall),
        out_specs=(tall, wide, wide),
        check_vma=False,
    )
```

```python
import functools

import jax
import jax.numpy as jnp
from jax import lax
from jax.experimental import pallas as pl
from jax.experimental.pallas import tpu as pltpu
from jax.sharding import PartitionSpec as P

TILE = 16
WHOLE = pl.BlockSpec(memory_space=pltpu.VMEM)
LEFT = pl.BlockSpec(memory_space=pltpu.HBM)
COST = pl.CostEstimate(flops=0, bytes_accessed=16 * 1024 * 1024, transcendentals=0)
PARAMS = pltpu.CompilerParams(vmem_limit_bytes=24 * 1024 * 1024)


def send(array, flip, hop):
    sections, count = lax.axis_size("section"), lax.axis_size("tp")
    if hop == 0:
        return lax.ppermute(array, "tp", [(t, t ^ flip) for t in range(count)])
    pairs = [
        (s * count + t, ((s - hop) % sections) * count + (t ^ flip))
        for s in range(sections)
        for t in range(count)
    ]
    return lax.ppermute(array, ("section", "tp"), pairs)


def started(source_ref, target_ref, sem, priority=0):
    copy = pltpu.make_async_copy(source_ref, target_ref, sem)
    copy.start(priority=priority)
    return [copy]


def fetched(refs, held_refs, sems):
    return sum([started(ref, held, sems.at[i]) for i, (ref, held) in enumerate(zip(refs, held_refs))], [])


def pack_kernel(held_ref, packed_ref, rows_ref, sems):
    for copy in fetched([held_ref], [rows_ref], sems):
        copy.wait()
    count, width = rows_ref.shape
    free = TILE - count
    keep = width * count // TILE
    rows = rows_ref[...]
    parts = [rows[at : at + free, keep:] for at in range(0, count, free)]
    packed_ref[...] = jnp.concatenate([rows[:, :keep], jnp.concatenate(parts, axis=1)], axis=0)


def pack(rows):
    count, width = rows.shape
    return pl.pallas_call(
        pack_kernel,
        out_shape=pltpu.VMEM((TILE, width * count // TILE), jnp.bfloat16),
        in_specs=[LEFT],
        out_specs=WHOLE,
        scratch_shapes=[pltpu.VMEM(rows.shape, rows.dtype), pltpu.SemaphoreType.DMA((1,))],
        compiler_params=PARAMS,
    )(pltpu.with_memory_space_constraint(rows, pltpu.HBM))


def spread(tokens, slots, count):
    shape = (tokens, len(slots) * TILE)
    lane = lax.broadcasted_iota(jnp.int32, shape, 1)
    row = lane & (TILE - 1)
    place = lane >> (TILE.bit_length() - 1)
    slot = jnp.full(shape, slots[0], jnp.int32)
    for i in range(1, len(slots)):
        slot = jnp.where(place == i, slots[i], slot)
    token = (slot ^ lax.axis_index("tp")) * count + row
    hit = (lax.broadcasted_iota(jnp.int32, shape, 0) == token) & (row < count)
    return jnp.where(hit, 1.0, 0.0).astype(jnp.bfloat16)


def decoded(codes_ref, exponents_ref):
    blocks = exponents_ref.shape[0]
    per = codes_ref.shape[0] // blocks
    parts = []
    for b in range(blocks):
        scale = jnp.exp2(exponents_ref[b].astype(jnp.float32))
        codes = codes_ref[pl.ds(b * per, per), :].astype(jnp.float32)
        parts.append((codes * scale).astype(jnp.bfloat16))
    return jnp.concatenate(parts, axis=0)


def prepare_kernel(groups, count, *refs):
    gate_ref, gate_exp_ref, up_ref, up_exp_ref, down_ref, down_exp_ref = held = refs[-7:-1]
    copies = fetched(refs[:6], held, refs[-1])
    weight_ref, hidden_ref = refs[6:8]
    factor_refs = refs[8:-7]
    for copy in copies[:4]:
        copy.wait()
    where = spread(gate_ref.shape[1], sum(groups, []), count)
    gate = jnp.dot(decoded(gate_ref, gate_exp_ref), where, preferred_element_type=jnp.float32)
    up = jnp.dot(decoded(up_ref, up_exp_ref), where, preferred_element_type=jnp.float32)
    sigmoid = jax.nn.sigmoid(gate)
    silu = gate * sigmoid
    hidden_ref[...] = (silu * up).astype(jnp.bfloat16)
    gate_factor = up * sigmoid * (1.0 + gate * (1.0 - sigmoid))
    at = 0
    for i, group in enumerate(groups):
        lanes = slice(at, at + len(group) * TILE)
        at = lanes.stop
        factor_refs[2 * i][...] = gate_factor[:, lanes]
        factor_refs[2 * i + 1][...] = silu[:, lanes]
    for copy in copies[4:]:
        copy.wait()
    blocks = down_exp_ref.shape[0]
    per = down_ref.shape[0] // blocks
    for b in range(blocks):
        scale = jnp.exp2(down_exp_ref[b].astype(jnp.float32))
        codes = down_ref[pl.ds(b * per, per), :].astype(jnp.float32)
        weight_ref[pl.ds(b * per, per), :] = (codes * scale).astype(jnp.bfloat16)


def prepare(groups, count, *operands):
    units, width = operands[4].shape
    lanes = sum(map(len, groups)) * TILE
    factors = [pltpu.VMEM((units, len(group) * TILE), jnp.float32) for group in groups for _ in range(2)]
    weight, hidden, *factors = pl.pallas_call(
        functools.partial(prepare_kernel, groups, count),
        out_shape=(
            pltpu.VMEM((units, width), jnp.bfloat16),
            pltpu.VMEM((units, lanes), jnp.bfloat16),
            *factors,
        ),
        in_specs=[LEFT] * 6,
        out_specs=[WHOLE] * (2 + len(factors)),
        scratch_shapes=[pltpu.VMEM(operand.shape, operand.dtype) for operand in operands]
        + [pltpu.SemaphoreType.DMA((len(operands),))],
        compiler_params=PARAMS,
        cost_estimate=COST,
    )(*[pltpu.with_memory_space_constraint(operand, pltpu.HBM) for operand in operands])
    return weight, hidden, [factors[2 * i : 2 * i + 2] for i in range(len(groups))]


def restore(slot_refs, incoming_ref, count):
    free = TILE - count
    width = incoming_ref.shape[1]
    for i, slot_ref in enumerate(slot_refs):
        keep = slot_ref.shape[1]
        slot = slot_ref[...]
        low = slot[count:, :]
        parts = [low[:, at : at + width - keep] for at in range(0, keep, width - keep)]
        parts.append(jnp.zeros((free, width - keep), slot.dtype))
        incoming_ref[i * TILE : (i + 1) * TILE, :keep] = slot
        incoming_ref[i * TILE : (i + 1) * TILE, keep:] = jnp.concatenate(parts, axis=0)


def grads(group, count, slope, factor_refs, before_refs, grad_refs):
    where = spread(grad_refs[0].shape[1], group, count)
    for factor_ref, before_ref, grad_ref in zip(factor_refs, before_refs, grad_refs):
        grad = (slope * factor_ref[...]).astype(jnp.bfloat16)
        placed = lax.dot_general(grad, where, (((1,), (1,)), ((), ())), preferred_element_type=jnp.float32)
        if before_ref is not None:
            placed += before_ref[...].astype(jnp.float32)
        grad_ref[...] = placed.astype(jnp.bfloat16)


def stage_kernel(group, count, first, *refs):
    slot_refs, refs = refs[: len(group)], refs[len(group) :]
    weight_ref, factor_refs, refs = refs[0], refs[1:3], refs[3:]
    before_refs, refs = ((None, None), refs) if first else (refs[:2], refs[2:])
    incoming_ref, *grad_refs = refs
    restore(slot_refs, incoming_ref, count)
    slope = lax.dot_general(
        weight_ref[...], incoming_ref[...], (((1,), (1,)), ((), ())), preferred_element_type=jnp.float32
    )
    grads(group, count, slope, factor_refs, before_refs, grad_refs)


def stage(group, count, tokens, slots, weight, factors, before):
    units, width = weight.shape
    operands = (*slots, weight, *factors, *before)
    return pl.pallas_call(
        functools.partial(stage_kernel, group, count, len(before) == 0),
        out_shape=(
            pltpu.VMEM((len(group) * TILE, width), jnp.bfloat16),
            pltpu.VMEM((units, tokens), jnp.bfloat16),
            pltpu.VMEM((units, tokens), jnp.bfloat16),
        ),
        in_specs=[WHOLE] * len(operands),
        out_specs=[WHOLE] * 3,
        compiler_params=PARAMS,
        cost_estimate=COST,
    )(*operands)


def last_kernel(slots, group, count, parts, *refs):
    slot_refs, earlier_refs, refs = refs[: len(group)], refs[len(group) : slots], refs[slots:]
    weight_ref, hidden_ref, *factor_refs = refs[:4]
    before_refs, out_refs, (newest_ref, *held_refs, sems) = refs[4:6], refs[6:9], refs[9:]
    restore(slot_refs, newest_ref, count)
    chunk = weight_ref.shape[1] // parts
    copies = []
    for i in range(parts):
        here = pl.ds(i * chunk, chunk)
        incoming = jnp.concatenate([ref[:, here] for ref in (*earlier_refs, newest_ref)], axis=0)
        down = jnp.dot(hidden_ref[...], incoming, preferred_element_type=jnp.float32)
        held_refs[0][:, here] = down.astype(jnp.bfloat16)
        copies += started(held_refs[0].at[:, here], out_refs[0].at[:, here], sems.at[2 + i], i % 2)
        if i == parts // 2 - 1:
            slope = lax.dot_general(
                weight_ref[...], newest_ref[...], (((1,), (1,)), ((), ())), preferred_element_type=jnp.float32
            )
            grads(group, count, slope, factor_refs, before_refs, held_refs[1:])
            for j in range(2):
                copies += started(held_refs[1 + j], out_refs[1 + j], sems.at[j])
    for copy in copies:
        copy.wait()


def last(group, count, slots, earlier, weight, hidden, factors, before):
    units, width = weight.shape
    tokens = before[0].shape[1]
    parts = 8
    operands = (*slots, *earlier, weight, hidden, *factors, *before)
    shapes = [(units, width), (units, tokens), (units, tokens)]
    return pl.pallas_call(
        functools.partial(last_kernel, len(slots) + len(earlier), group, count, parts),
        out_shape=[jax.ShapeDtypeStruct(shape, jnp.bfloat16) for shape in shapes],
        in_specs=[WHOLE] * len(operands),
        out_specs=[LEFT] * 3,
        scratch_shapes=[
            pltpu.VMEM((len(group) * TILE, width), jnp.bfloat16),
            *[pltpu.VMEM(shape, jnp.bfloat16) for shape in shapes],
            pltpu.SemaphoreType.DMA((2 + parts,)),
        ],
        compiler_params=PARAMS,
        cost_estimate=COST,
    )(*operands)


def fanned(gate_codes, gate_exponents, up_codes, up_exponents, down_codes, down_exponents, grad_held):
    n = lax.axis_size("tp")
    count = grad_held.shape[1]
    p = pack(grad_held[0])
    first = [f for f in range(n) if f & (f - 1) == 0]
    rest = [f for f in range(n) if f not in first]
    late = [f for f in rest if f - n // 2 in first]
    groups = [first, [f for f in rest[:-1] if f not in late] + late[::-1] + rest[-1:]]
    got = {}
    for flip in reversed(first):
        got[flip] = send(p, flip, 1)
    for flip in reversed(rest):
        step = flip & -flip
        if flip & 1 and flip - 1 not in first:
            step = flip - 1
        got[flip] = send(got[flip - step], step, 0)
    weight, hidden, factors = prepare(
        groups,
        count,
        gate_codes[0].T,
        gate_exponents.transpose(2, 0, 1),
        up_codes[0].T,
        up_exponents.transpose(2, 0, 1),
        down_codes[0],
        down_exponents.transpose(1, 0, 2),
    )
    earlier, before = [], []
    for group, pair in zip(groups[:-1], factors):
        incoming, *before = stage(group, count, n * count, [got[j] for j in group], weight, pair, before)
        earlier.append(incoming)
    arrived = [got[j] for j in groups[-1]]
    down_grad, gate_grad, up_grad = last(groups[-1], count, arrived, earlier, weight, hidden, factors[-1], before)
    return down_grad[None], gate_grad.T[None], up_grad.T[None]


def dequantize(codes, exponents, target_axis):
    per = codes.shape[target_axis] // exponents.shape[target_axis]
    scales = jnp.exp2(jnp.repeat(exponents, per, axis=target_axis).astype(jnp.float32))
    return (codes.astype(jnp.float32) * scales).astype(jnp.bfloat16)


def ringed(gate_codes, gate_exponents, up_codes, up_exponents, down_codes, down_exponents, grad_held):
    gate = dequantize(gate_codes[0], gate_exponents[0], 1).astype(jnp.float32)
    up = dequantize(up_codes[0], up_exponents[0], 1).astype(jnp.float32)
    weight = dequantize(down_codes[0], down_exponents[0], 0)
    count = lax.axis_size("section")
    received = lax.ppermute(grad_held[0], "section", [(i, (i - 1) % count) for i in range(count)])
    incoming = lax.all_gather(received, "tp", axis=0, tiled=True)
    sigmoid = jax.nn.sigmoid(gate)
    silu = gate * sigmoid
    hidden = (silu * up).astype(jnp.bfloat16)
    down_grad = lax.dot_general(hidden, incoming, (((0,), (0,)), ((), ())), preferred_element_type=jnp.float32)
    slope = lax.dot_general(incoming, weight, (((1,), (1,)), ((), ())), preferred_element_type=jnp.float32)
    gate_grad = (slope * up * sigmoid * (1.0 + gate * (1.0 - sigmoid))).astype(jnp.bfloat16)
    up_grad = (slope * silu).astype(jnp.bfloat16)
    return down_grad.astype(jnp.bfloat16)[None], gate_grad[None], up_grad[None]


def body(*operands):
    n = lax.axis_size("tp")
    count, width = operands[-1].shape[1:]
    free = TILE - count
    small = n & (n - 1) == 0 and 4 <= n <= TILE
    fits = 0 < free < TILE and count % free == 0 and width * free % (TILE * 128) == 0 and width % (8 * 128) == 0
    return fanned(*operands) if small and fits else ringed(*operands)


def solution(mesh):
    wide, tall = P("section", None, "tp"), P("section", "tp", None)
    return jax.shard_map(
        body,
        mesh=mesh,
        in_specs=(wide, wide, wide, wide, tall, tall, tall),
        out_specs=(tall, wide, wide),
        check_vma=False,
    )
```

```python
import functools

import jax
import jax.numpy as jnp
from jax import lax
from jax.experimental import pallas as pl
from jax.experimental.pallas import tpu as pltpu
from jax.sharding import PartitionSpec as P

TILE = 16
WHOLE = pl.BlockSpec(memory_space=pltpu.VMEM)
LEFT = pl.BlockSpec(memory_space=pltpu.HBM)
COST = pl.CostEstimate(flops=0, bytes_accessed=16 * 1024 * 1024, transcendentals=0)
PARAMS = pltpu.CompilerParams(vmem_limit_bytes=24 * 1024 * 1024)


def send(array, flip, hop):
    sections, count = lax.axis_size("section"), lax.axis_size("tp")
    if hop == 0:
        return lax.ppermute(array, "tp", [(t, t ^ flip) for t in range(count)])
    pairs = [
        (s * count + t, ((s - hop) % sections) * count + (t ^ flip))
        for s in range(sections)
        for t in range(count)
    ]
    return lax.ppermute(array, ("section", "tp"), pairs)


def started(source_ref, target_ref, sem, priority=0):
    copy = pltpu.make_async_copy(source_ref, target_ref, sem)
    copy.start(priority=priority)
    return [copy]


def fetched(refs, held_refs, sems):
    return sum([started(ref, held, sems.at[i]) for i, (ref, held) in enumerate(zip(refs, held_refs))], [])


def pack_kernel(held_ref, packed_ref, rows_ref, sems):
    for copy in fetched([held_ref], [rows_ref], sems):
        copy.wait()
    count, width = rows_ref.shape
    free = TILE - count
    keep = width * count // TILE
    rows = rows_ref[...]
    parts = [rows[at : at + free, keep:] for at in range(0, count, free)]
    packed_ref[...] = jnp.concatenate([rows[:, :keep], jnp.concatenate(parts, axis=1)], axis=0)


def pack(rows):
    count, width = rows.shape
    return pl.pallas_call(
        pack_kernel,
        out_shape=pltpu.VMEM((TILE, width * count // TILE), jnp.bfloat16),
        in_specs=[LEFT],
        out_specs=WHOLE,
        scratch_shapes=[pltpu.VMEM(rows.shape, rows.dtype), pltpu.SemaphoreType.DMA((1,))],
        compiler_params=PARAMS,
    )(pltpu.with_memory_space_constraint(rows, pltpu.HBM))


def spread(tokens, slots, count):
    shape = (tokens, len(slots) * TILE)
    lane = lax.broadcasted_iota(jnp.int32, shape, 1)
    row = lane & (TILE - 1)
    place = lane >> (TILE.bit_length() - 1)
    slot = jnp.full(shape, slots[0], jnp.int32)
    for i in range(1, len(slots)):
        slot = jnp.where(place == i, slots[i], slot)
    token = (slot ^ lax.axis_index("tp")) * count + row
    hit = (lax.broadcasted_iota(jnp.int32, shape, 0) == token) & (row < count)
    return jnp.where(hit, 1.0, 0.0).astype(jnp.bfloat16)


def decoded(codes_ref, exponents_ref):
    blocks = exponents_ref.shape[0]
    per = codes_ref.shape[0] // blocks
    parts = []
    for b in range(blocks):
        scale = jnp.exp2(exponents_ref[b].astype(jnp.float32))
        codes = codes_ref[pl.ds(b * per, per), :].astype(jnp.float32)
        parts.append((codes * scale).astype(jnp.bfloat16))
    return jnp.concatenate(parts, axis=0)


def prepare_kernel(groups, count, *refs):
    gate_ref, gate_exp_ref, up_ref, up_exp_ref, down_ref, down_exp_ref = held = refs[-7:-1]
    copies = fetched(refs[:6], held, refs[-1])
    weight_ref, hidden_ref = refs[6:8]
    factor_refs = refs[8:-7]
    for copy in copies[:4]:
        copy.wait()
    where = spread(gate_ref.shape[1], sum(groups, []), count)
    gate = jnp.dot(decoded(gate_ref, gate_exp_ref), where, preferred_element_type=jnp.float32)
    up = jnp.dot(decoded(up_ref, up_exp_ref), where, preferred_element_type=jnp.float32)
    sigmoid = jax.nn.sigmoid(gate)
    silu = gate * sigmoid
    hidden_ref[...] = (silu * up).astype(jnp.bfloat16)
    gate_factor = up * sigmoid * (1.0 + gate * (1.0 - sigmoid))
    at = 0
    for i, group in enumerate(groups):
        lanes = slice(at, at + len(group) * TILE)
        at = lanes.stop
        factor_refs[2 * i][...] = gate_factor[:, lanes]
        factor_refs[2 * i + 1][...] = silu[:, lanes]
    for copy in copies[4:]:
        copy.wait()
    blocks = down_exp_ref.shape[0]
    per = down_ref.shape[0] // blocks
    for b in range(blocks):
        scale = jnp.exp2(down_exp_ref[b].astype(jnp.float32))
        codes = down_ref[pl.ds(b * per, per), :].astype(jnp.float32)
        weight_ref[pl.ds(b * per, per), :] = (codes * scale).astype(jnp.bfloat16)


def prepare(groups, count, *operands):
    units, width = operands[4].shape
    lanes = sum(map(len, groups)) * TILE
    factors = [pltpu.VMEM((units, len(group) * TILE), jnp.float32) for group in groups for _ in range(2)]
    weight, hidden, *factors = pl.pallas_call(
        functools.partial(prepare_kernel, groups, count),
        out_shape=(
            pltpu.VMEM((units, width), jnp.bfloat16),
            pltpu.VMEM((units, lanes), jnp.bfloat16),
            *factors,
        ),
        in_specs=[LEFT] * 6,
        out_specs=[WHOLE] * (2 + len(factors)),
        scratch_shapes=[pltpu.VMEM(operand.shape, operand.dtype) for operand in operands]
        + [pltpu.SemaphoreType.DMA((len(operands),))],
        compiler_params=PARAMS,
        cost_estimate=COST,
    )(*[pltpu.with_memory_space_constraint(operand, pltpu.HBM) for operand in operands])
    return weight, hidden, [factors[2 * i : 2 * i + 2] for i in range(len(groups))]


def restore(slot_refs, incoming_ref, count):
    free = TILE - count
    width = incoming_ref.shape[1]
    for i, slot_ref in enumerate(slot_refs):
        keep = slot_ref.shape[1]
        slot = slot_ref[...]
        low = slot[count:, :]
        parts = [low[:, at : at + width - keep] for at in range(0, keep, width - keep)]
        parts.append(jnp.zeros((free, width - keep), slot.dtype))
        incoming_ref[i * TILE : (i + 1) * TILE, :keep] = slot
        incoming_ref[i * TILE : (i + 1) * TILE, keep:] = jnp.concatenate(parts, axis=0)


def grads(group, count, slope, factor_refs, before_refs, grad_refs):
    where = spread(grad_refs[0].shape[1], group, count)
    for factor_ref, before_ref, grad_ref in zip(factor_refs, before_refs, grad_refs):
        grad = (slope * factor_ref[...]).astype(jnp.bfloat16)
        placed = lax.dot_general(grad, where, (((1,), (1,)), ((), ())), preferred_element_type=jnp.float32)
        if before_ref is not None:
            placed += before_ref[...].astype(jnp.float32)
        grad_ref[...] = placed.astype(jnp.bfloat16)


def stage_kernel(group, count, first, *refs):
    slot_refs, refs = refs[: len(group)], refs[len(group) :]
    weight_ref, factor_refs, refs = refs[0], refs[1:3], refs[3:]
    before_refs, refs = ((None, None), refs) if first else (refs[:2], refs[2:])
    incoming_ref, *grad_refs = refs
    restore(slot_refs, incoming_ref, count)
    slope = lax.dot_general(
        weight_ref[...], incoming_ref[...], (((1,), (1,)), ((), ())), preferred_element_type=jnp.float32
    )
    grads(group, count, slope, factor_refs, before_refs, grad_refs)


def stage(group, count, tokens, slots, weight, factors, before):
    units, width = weight.shape
    operands = (*slots, weight, *factors, *before)
    return pl.pallas_call(
        functools.partial(stage_kernel, group, count, len(before) == 0),
        out_shape=(
            pltpu.VMEM((len(group) * TILE, width), jnp.bfloat16),
            pltpu.VMEM((units, tokens), jnp.bfloat16),
            pltpu.VMEM((units, tokens), jnp.bfloat16),
        ),
        in_specs=[WHOLE] * len(operands),
        out_specs=[WHOLE] * 3,
        compiler_params=PARAMS,
        cost_estimate=COST,
    )(*operands)


def last_kernel(slots, group, count, parts, *refs):
    slot_refs, earlier_refs, refs = refs[: len(group)], refs[len(group) : slots], refs[slots:]
    weight_ref, hidden_ref, *factor_refs = refs[:4]
    before_refs, out_refs, (newest_ref, *held_refs, sems) = refs[4:6], refs[6:9], refs[9:]
    restore(slot_refs, newest_ref, count)
    chunk = weight_ref.shape[1] // parts
    copies = []
    for i in range(parts):
        here = pl.ds(i * chunk, chunk)
        incoming = jnp.concatenate([ref[:, here] for ref in (*earlier_refs, newest_ref)], axis=0)
        down = jnp.dot(hidden_ref[...], incoming, preferred_element_type=jnp.float32)
        held_refs[0][:, here] = down.astype(jnp.bfloat16)
        copies += started(held_refs[0].at[:, here], out_refs[0].at[:, here], sems.at[2 + i], i % 2)
    slope = lax.dot_general(
        weight_ref[...], newest_ref[...], (((1,), (1,)), ((), ())), preferred_element_type=jnp.float32
    )
    grads(group, count, slope, factor_refs, before_refs, held_refs[1:])
    for i in range(2):
        copies += started(held_refs[1 + i], out_refs[1 + i], sems.at[i])
    for copy in copies:
        copy.wait()


def last(group, count, slots, earlier, weight, hidden, factors, before):
    units, width = weight.shape
    tokens = before[0].shape[1]
    parts = 2
    operands = (*slots, *earlier, weight, hidden, *factors, *before)
    shapes = [(units, width), (units, tokens), (units, tokens)]
    return pl.pallas_call(
        functools.partial(last_kernel, len(slots) + len(earlier), group, count, parts),
        out_shape=[jax.ShapeDtypeStruct(shape, jnp.bfloat16) for shape in shapes],
        in_specs=[WHOLE] * len(operands),
        out_specs=[LEFT] * 3,
        scratch_shapes=[
            pltpu.VMEM((len(group) * TILE, width), jnp.bfloat16),
            *[pltpu.VMEM(shape, jnp.bfloat16) for shape in shapes],
            pltpu.SemaphoreType.DMA((2 + parts,)),
        ],
        compiler_params=PARAMS,
        cost_estimate=COST,
    )(*operands)


def fanned(gate_codes, gate_exponents, up_codes, up_exponents, down_codes, down_exponents, grad_held):
    n = lax.axis_size("tp")
    count = grad_held.shape[1]
    p = pack(grad_held[0])
    first = [f for f in range(n) if f & (f - 1) == 0]
    rest = [f for f in range(n) if f not in first]
    late = [f for f in rest if f - n // 2 in first]
    groups = [first, [f for f in rest[:-1] if f not in late] + late[::-1] + rest[-1:]]
    got = {}
    for flip in reversed(first):
        got[flip] = send(p, flip, 1)
    for flip in reversed(rest):
        step = flip & -flip
        if flip & 1 and flip - 1 not in first:
            step = flip - 1
        got[flip] = send(got[flip - step], step, 0)
    weight, hidden, factors = prepare(
        groups,
        count,
        gate_codes[0].T,
        gate_exponents.transpose(2, 0, 1),
        up_codes[0].T,
        up_exponents.transpose(2, 0, 1),
        down_codes[0],
        down_exponents.transpose(1, 0, 2),
    )
    earlier, before = [], []
    for group, pair in zip(groups[:-1], factors):
        incoming, *before = stage(group, count, n * count, [got[j] for j in group], weight, pair, before)
        earlier.append(incoming)
    arrived = [got[j] for j in groups[-1]]
    down_grad, gate_grad, up_grad = last(groups[-1], count, arrived, earlier, weight, hidden, factors[-1], before)
    return down_grad[None], gate_grad.T[None], up_grad.T[None]


def dequantize(codes, exponents, target_axis):
    per = codes.shape[target_axis] // exponents.shape[target_axis]
    scales = jnp.exp2(jnp.repeat(exponents, per, axis=target_axis).astype(jnp.float32))
    return (codes.astype(jnp.float32) * scales).astype(jnp.bfloat16)


def ringed(gate_codes, gate_exponents, up_codes, up_exponents, down_codes, down_exponents, grad_held):
    gate = dequantize(gate_codes[0], gate_exponents[0], 1).astype(jnp.float32)
    up = dequantize(up_codes[0], up_exponents[0], 1).astype(jnp.float32)
    weight = dequantize(down_codes[0], down_exponents[0], 0)
    count = lax.axis_size("section")
    received = lax.ppermute(grad_held[0], "section", [(i, (i - 1) % count) for i in range(count)])
    incoming = lax.all_gather(received, "tp", axis=0, tiled=True)
    sigmoid = jax.nn.sigmoid(gate)
    silu = gate * sigmoid
    hidden = (silu * up).astype(jnp.bfloat16)
    down_grad = lax.dot_general(hidden, incoming, (((0,), (0,)), ((), ())), preferred_element_type=jnp.float32)
    slope = lax.dot_general(incoming, weight, (((1,), (1,)), ((), ())), preferred_element_type=jnp.float32)
    gate_grad = (slope * up * sigmoid * (1.0 + gate * (1.0 - sigmoid))).astype(jnp.bfloat16)
    up_grad = (slope * silu).astype(jnp.bfloat16)
    return down_grad.astype(jnp.bfloat16)[None], gate_grad[None], up_grad[None]


def body(*operands):
    n = lax.axis_size("tp")
    count, width = operands[-1].shape[1:]
    free = TILE - count
    small = n & (n - 1) == 0 and 4 <= n <= TILE
    fits = 0 < free < TILE and count % free == 0 and width * free % (TILE * 128) == 0 and width % (4 * 128) == 0
    return fanned(*operands) if small and fits else ringed(*operands)


def solution(mesh):
    wide, tall = P("section", None, "tp"), P("section", "tp", None)
    return jax.shard_map(
        body,
        mesh=mesh,
        in_specs=(wide, wide, wide, wide, tall, tall, tall),
        out_specs=(tall, wide, wide),
        check_vma=False,
    )
```
